32 devices in a mesh: dp: 4 (over y, x), fsdp: 8 (over z, core).
Axes of the slice: x: 2, y: 2, z: 4, core: 2. Of those that a mesh axis runs over, the one named last changes fastest.
Arguments:
- tokens: bfloat16 [1152, 77, 512], P(('dp', 'fsdp')), may hold values from -6 to 6
- segment_ids: int32 [1152, 77], P(('dp', 'fsdp')), may hold values from 0 to 3, never falling along the last dimension, each value on 1 to 40 neighbouring positions
- qkv_weight: bfloat16 [786432], P(('dp', 'fsdp')), may hold values from -0.25 to 0.25
- out_weight: bfloat16 [262144], P(('dp', 'fsdp')), may hold values from -0.75 to 0.75
- up_weight: bfloat16 [1048576], P(('dp', 'fsdp')), may hold values from -0.25 to 0.25
- up_bias: bfloat16 [2048], P(('dp', 'fsdp')), may hold values from -1.75 to 1.75
- down_weight: bfloat16 [1048576], P(('dp', 'fsdp')), may hold values from -0.125 to 0.125
- small_params: bfloat16 [4096], P(('dp', 'fsdp'))
- cotangent: bfloat16 [1152, 77, 512], P(('dp', 'fsdp')), may hold values from -6 to 6
Outputs:
- block_output: bfloat16 [1152, 77, 512], P(('dp', 'fsdp'))
- grad_tokens: bfloat16 [1152, 77, 512], P(('dp', 'fsdp'))
- grad_qkv_weight: float32 [786432], P(('dp', 'fsdp'))
- grad_out_weight: float32 [262144], P(('dp', 'fsdp'))
- grad_up_weight: float32 [1048576], P(('dp', 'fsdp'))
- grad_up_bias: float32 [2048], P(('dp', 'fsdp'))
- grad_down_weight: float32 [1048576], P(('dp', 'fsdp'))
- grad_small: float32 [4096], P(('dp', 'fsdp'))
The draws below stay inside these ranges and needn't reach their ends.
Inputs may be any that keep to these rules, and one draw needn't show every extreme that they name: `segment_ids`: along each packed row the ids never fall; each id labels one run of 1 to 40 consecutive tokens.
All inputs are finite; a program needn't handle non-finite values.
Results may differ from the reference program's by a relative error of at most 0.0091.
Values may be sent and summed in bfloat16 or wider, within the bound.
A program may use at most 192 MiB of HBM per device.

```python
import math
import jax
import jax.numpy as jnp
import numpy as np
from jax import lax

D = 512
HEADS = 8
HEAD_DIM = 64
FF = 2048
SEQ = 77
SEGS = 4
MOST = 40
BLOCK_ROWS = 12
ROWS = 1152


def draw_small_params(key, part):
    indexes = jnp.arange(8 * D) // D
    gain_draw = jax.random.uniform(jax.random.fold_in(key, 11), (8 * D,), jnp.float32, 0.6, 1.4)
    bias_draw = 0.3 * jax.random.normal(jax.random.fold_in(key, 12), (8 * D,), jnp.float32)
    chosen = jnp.where((indexes == 0) | (indexes == 5), gain_draw, bias_draw)
    return chosen.astype(jnp.bfloat16)


def with_spikes(entries, stream_key, source, target, shards_of, factor):
    owner, partner = [(jnp.arange(entries.shape[position]) // (entries.shape[position] // shards_of)).reshape([-1 if axis == position else 1 for axis in range(entries.ndim)]) for position in (source, target)]
    chosen = jax.random.permutation(stream_key, shards_of)[partner]
    strong = (owner == chosen) | (owner == (partner + shards_of // 2) % shards_of)
    return jnp.where(strong, factor * entries, entries)


def level_of(key, shape, pieces, least, top_value):
    loudness, own = 1.0, jax.random.fold_in(key, 6)
    for position, shards_of in pieces:
        heights = jnp.exp(jax.random.uniform(jax.random.fold_in(own, position), (shards_of,), jnp.float32, least / len(pieces), top_value / len(pieces)))
        loudness = loudness * jnp.repeat(heights, shape[position] // shards_of).reshape([-1 if axis == position else 1 for axis in range(len(shape))])
    return loudness


def split_up(count, total, most, slope):
    weights = [(1 << 20) // math.isqrt(grade ** slope) + 1 for grade in range(2, count + 1)]
    surplus, given = total - most - (count - 1), [1] * (count - 1)
    while surplus > 0:
        candidates = [i for i in range(count - 1) if given[i] < most]
        whole, budget = sum([weights[i] for i in candidates]), surplus
        for i in candidates:
            more = min(most - given[i], max(1, budget * weights[i] // whole), surplus)
            given[i] = given[i] + more
            surplus = surplus - more
    return np.array([most] + given)


def ragged(key, count, total, limit, lean):
    if count == 2:
        one = jax.random.randint(key, (), max(1, total - limit), min(limit, total - 1) + 1)
        return jnp.stack([one, total - one])
    sizes = jnp.asarray(split_up(count, total, limit, lean), jnp.int32)
    twos = (count - 1) // 2
    source_of, taker = sizes[1:1 + 2 * twos:2], sizes[2:2 + 2 * twos:2]
    slack = jnp.minimum(source_of - 1, limit - taker)
    moved = jax.random.randint(jax.random.fold_in(key, 1), (twos,), 0, 1 << 20) % (slack + 1)
    sizes = sizes.at[1:1 + 2 * twos:2].set(source_of - moved).at[2:2 + 2 * twos:2].set(taker + moved)
    return sizes[jax.random.permutation(jax.random.fold_in(key, 2), count)]


def centred(stream_key, shape, scale, most, pieces=(), held_as=jnp.bfloat16):
    entries = scale * jax.random.normal(stream_key, shape, jnp.float32)
    if pieces:
        entries = entries * level_of(stream_key, shape, pieces, -0.22, 0.18)
    return jnp.clip(entries, -most, most).astype(held_as)


def gaussian_with(key, extent, scale, bound, pieces, heavy, kind=jnp.bfloat16):
    values = scale * jax.random.normal(key, extent, jnp.float32)
    if pieces:
        values = values * level_of(key, extent, pieces, -0.22, 0.18)
    return jnp.clip(with_spikes(values, jax.random.fold_in(key, 3), *heavy), -bound, bound).astype(kind)


def setup_inputs(seed: int = 0) -> dict:
    key_list = jax.random.split(jax.random.key(seed), 10)
    return {
        "tokens": gaussian_with(key_list[0], (ROWS, SEQ, D), 1.0, 6.0, ((0, 32),), (0, 2, 32, 2.75)),
        "segment_ids": jax.vmap(lambda own: jnp.searchsorted(jnp.cumsum(ragged(own, SEGS, SEQ, MOST, 0)), jnp.arange(SEQ), side="right"))(jax.random.split(key_list[1], ROWS)).reshape((ROWS, SEQ)).astype(jnp.int32),
        "qkv_weight": centred(key_list[2], (3 * D * D,), D ** -0.5, 0.25, ((0, 32),)),
        "out_weight": centred(key_list[3], (D * D,), (D // 8) ** -0.5, 0.75, ((0, 32),)),
        "up_weight": centred(key_list[4], (D * FF,), D ** -0.5, 0.25, ((0, 32),)),
        "up_bias": centred(key_list[5], (FF,), 0.3, 1.75, ((0, 32),)),
        "down_weight": centred(key_list[6], (FF * D,), FF ** -0.5, 0.125, ((0, 32),)),
        "small_params": draw_small_params(jax.random.fold_in(key_list[9], 71), 0),
        "cotangent": gaussian_with(key_list[8], (ROWS, SEQ, D), 1.0, 6.0, ((0, 32),), (0, 2, 32, 2.75)),
    }


NORM_EPS = 1e-05
GELU_SLOPE = 1.702
MASKED_SCORE = -1e+30

@jax.custom_vjp
def low(v):
    return lax.optimization_barrier(v.astype(jnp.bfloat16)).astype(jnp.float32)

@jax.custom_vjp
def low_back(v):
    return v

def low_keep(v):
    return (low(v), None)

def low_pass(kept, grad):
    return (grad,)

def back_keep(v):
    return (v, None)

def back_low(kept, grad):
    return (low(grad),)
low.defvjp(low_keep, low_pass)
low_back.defvjp(back_keep, back_low)

def matmul_high(left, right):
    return jnp.dot(left, right, precision=lax.Precision.HIGHEST, preferred_element_type=jnp.float32)

def layer_norm(values, norm_gain, norm_shift):
    center = lax.optimization_barrier(jnp.mean(values, axis=-1, keepdims=True))
    centered = values - center
    spread = lax.optimization_barrier(jnp.mean(centered * centered, axis=-1, keepdims=True))
    return centered * lax.rsqrt(spread + NORM_EPS) * norm_gain + norm_shift

def attend_group(operands):
    queries, key_rows, value_rows, segments = operands
    score_scale = HEAD_DIM ** (-0.5)
    scores = jnp.einsum('gqhd,gkhd->ghqk', queries, key_rows, precision=lax.Precision.HIGHEST)
    scores = low_back(scores * score_scale)
    places = jnp.arange(SEQ)
    causal = places[None, :] <= places[:, None]
    allowed = (segments[:, :, None] == segments[:, None, :]) & causal[None]
    masked = jnp.where(allowed[:, None], scores, MASKED_SCORE)
    highest = lax.optimization_barrier(jnp.max(masked, axis=-1, keepdims=True))
    weights_exp = jnp.exp(masked - highest)
    prob_mat = weights_exp / lax.optimization_barrier(jnp.sum(weights_exp, axis=-1, keepdims=True))
    return jnp.einsum('ghqk,gkhd->gqhd', low(prob_mat), value_rows, precision=lax.Precision.HIGHEST)

def forward(tokens_f, segment_ids, qkv_flat, out_flat, up_flat, up_bias, down_flat, small_flat):
    small_vec = small_flat.reshape(8, D)
    flat_rows = tokens_f.reshape(ROWS * SEQ, D)
    first_low = low(layer_norm(flat_rows, small_vec[0], small_vec[1]))
    bias_qkv = jnp.concatenate([small_vec[2], jnp.zeros_like(small_vec[2]), small_vec[3]])
    qkv_low = low(low_back(matmul_high(first_low, qkv_flat.reshape(D, 3 * D)) + bias_qkv))
    groups = ROWS // BLOCK_ROWS
    split_qkv = qkv_low.reshape(groups, BLOCK_ROWS, SEQ, 3, HEADS, HEAD_DIM)
    attended = lax.map(jax.checkpoint(attend_group), (split_qkv[:, :, :, 0], split_qkv[:, :, :, 1], split_qkv[:, :, :, 2], segment_ids.reshape(groups, BLOCK_ROWS, SEQ)))
    attended = low(low_back(attended.reshape(ROWS * SEQ, D)))
    middle = flat_rows + low_back(matmul_high(attended, out_flat.reshape(D, D)) + small_vec[4])
    second = low(layer_norm(middle, small_vec[5], small_vec[6]))
    pre_act = low_back(matmul_high(second, up_flat.reshape(D, FF)) + up_bias)
    act_low = low(pre_act * jax.nn.sigmoid(GELU_SLOPE * pre_act))
    result = middle + low_back(matmul_high(act_low, down_flat.reshape(FF, D)) + small_vec[7])
    return result.reshape(ROWS, SEQ, D)

def reference(tokens, segment_ids, qkv_weight, out_weight, up_weight, up_bias, down_weight, small_params, cotangent):
    floats = tuple((argument.astype(jnp.float32) for argument in (tokens, qkv_weight, out_weight, up_weight, up_bias, down_weight, small_params)))

    def closed(tokens_f, qkv_flat, out_flat, up_flat, bias_up, down_flat, small_flat):
        return forward(tokens_f, segment_ids, qkv_flat, out_flat, up_flat, bias_up, down_flat, small_flat)
    result, pullback = jax.vjp(closed, *floats)
    gradients = pullback(cotangent.astype(jnp.float32))
    return (result.astype(jnp.bfloat16), gradients[0].astype(jnp.bfloat16), gradients[1], gradients[2], gradients[3], gradients[4], gradients[5], gradients[6])
```

```python
import functools
import jax
import jax.numpy as jnp
from jax import lax
from jax.sharding import PartitionSpec as P
from jax.experimental import pallas as pl
from jax.experimental.pallas import tpu as pltpu
bf16=jnp.bfloat16; f32=jnp.float32
D=512; H=8; HD=64
NORM_EPS=1e-5; SLOPE=1.702
def nn(a,b): return lax.dot_general(a,b,(((1,),(0,)),((),())),preferred_element_type=f32)
def nt(a,b): return lax.dot_general(a,b,(((1,),(1,)),((),())),preferred_element_type=f32)
def tn(a,b): return lax.dot_general(a,b,(((0,),(0,)),((),())),preferred_element_type=f32)

def compute_kernel(R, S, SP, RB, FC, FF, phases,
    tok, seg, wqkv, wout, wup, bup, wdown, small, cot,
    out, gtok, gwqkv, gwout, gwup, gbup, gwdown, gsmall,
    xs, cs, FL, QKV, ATT, PT, GM, start, ost, osem, pre_s, ga_s, act_s, gp_s):
    NB=R//RB; M=RB*SP
    sm=small[...].astype(f32)
    g1,c1,bq,bv,bo,g2,c2,bd=[sm[i:i+1] for i in range(8)]
    xs[...]=jnp.zeros(xs.shape,f32)
    cs[...]=jnp.zeros(cs.shape,bf16)
    sg=seg[...]
    st=jnp.zeros(sg.shape,jnp.int32)
    for v in range(1,4):
        cnt=jnp.sum((sg<v).astype(f32),axis=1,keepdims=True).astype(jnp.int32)
        st=jnp.where(sg==v,cnt,st)
    st=jnp.concatenate([st,jnp.zeros((R,SP-S),jnp.int32)],axis=1)
    start[...]=jnp.concatenate([st]*4,axis=1).reshape(R,1,4*SP)

    def load_x(b):
        for i in range(RB):
            xs[SP*i:SP*i+S]=tok[b*RB+i].astype(f32)
    def norm(x):
        mean=jnp.sum(x,axis=-1,keepdims=True)*(1.0/D)
        xc=x-mean
        inv=lax.rsqrt(jnp.sum(xc*xc,axis=-1,keepdims=True)*(1.0/D)+NORM_EPS)
        return xc*inv, inv
    bqkv=jnp.concatenate([bq*0.125,jnp.zeros_like(bq),bv],axis=1)
    lane=lax.broadcasted_iota(jnp.int32,(1,256),1)
    hm=[(lane//HD==j).astype(f32).astype(bf16) for j in range(4)]
    low_half=lax.broadcasted_iota(jnp.int32,(1,128),1)<HD
    qi=lax.broadcasted_iota(jnp.int32,(SP,SP),1)
    def stack(v):
        return jnp.concatenate([v*hm[j] for j in range(4)],axis=0)
    def p1(b,_):
        load_x(b)
        n,_inv=norm(xs[...])
        fl=(n*g1+c1).astype(bf16)
        rows=pl.ds(pl.multiple_of(b*M,16),M)
        FL[rows]=fl
        QKV[rows,0:512]=(nn(fl,wqkv[:,0:512])*0.125+bqkv[:,0:512]).astype(bf16)
        QKV[rows,512:1536]=(nn(fl,wqkv[:,512:1536])+bqkv[:,512:1536]).astype(bf16)
        return _
    kidx=lax.broadcasted_iota(jnp.int32,(SP,4*SP),0)
    qidx=lax.broadcasted_iota(jnp.int32,(1,4*SP),1)
    qidx=qidx-SP*((qidx>=SP).astype(jnp.int32)+(qidx>=2*SP).astype(jnp.int32)+(qidx>=3*SP).astype(jnp.int32))
    def attn_row(r):
        rows=pl.ds(pl.multiple_of(r*SP,16),SP)
        allowed=(kidx>=start[r])&(kidx<=qidx)
        for g in range(2):
            q=QKV[rows,256*g:256*g+256]
            k=QKV[rows,512+256*g:512+256*g+256]
            s=nt(k,stack(q))
            s=jnp.where(allowed,s,-1e30)
            m=jnp.max(s,axis=0,keepdims=True)
            e=jnp.exp(s-m)
            p=(e*(1.0/jnp.sum(e,axis=0,keepdims=True))).astype(bf16)
            PT[2*r+g]=p
            pq=p.T
            for t in range(2):
                v=QKV[rows,1024+256*g+128*t:1024+256*g+128*t+128]
                o=nn(pq[2*SP*t:2*SP*t+2*SP],v)
                ATT[rows,256*g+128*t:256*g+128*t+128]=jnp.where(low_half,o[0:SP],o[SP:2*SP]).astype(bf16)
    UN=2
    def attn(r,_):
        for u in range(UN): attn_row(r*UN+u)
        return _
    def p2(b,_):
        load_x(b)
        for i in range(RB):
            cs[SP*i:SP*i+S]=cot[b*RB+i]
        rows=pl.ds(pl.multiple_of(b*M,16),M)
        att=ATT[rows]
        mid=xs[...]+nn(att,wout[...])+bo
        xh2,r2=norm(mid)
        second=(xh2*g2+c2).astype(bf16)
        branch=cs[...]
        acc=mid+bd
        gn2=jnp.zeros((M,D),f32)
        for c in range(FF//FC):
            cc=slice(c*FC,(c+1)*FC)
            pre=nn(second,wup[:,cc])+bup[:,cc].astype(f32)
            s=0.5*jnp.tanh((0.5*SLOPE)*pre)+0.5
            a=pre*s
            act=a.astype(bf16)
            ga=nt(branch,wdown[cc,:])
            gpf=ga*(s+SLOPE*a*(1.0-s))
            gp=gpf.astype(bf16)
            gbup[:,cc]+=jnp.sum(gp.astype(f32),axis=0,keepdims=True)
            acc=acc+nn(act,wdown[cc,:])
            gn2=gn2+nt(gp,wup[:,cc])
            gwdown[cc,:]+=tn(act,branch)
            gwup[:,cc]+=tn(second,gp)
        res=acc.astype(bf16)
        for i in range(RB):
            ost[i]=res[SP*i:SP*i+S]
        cp=pltpu.make_async_copy(ost,out.at[pl.ds(b*RB,RB)],osem)
        cp.start()
        h=gn2*g2
        m1=jnp.sum(h,axis=-1,keepdims=True)*(1.0/D)
        m2=jnp.sum(h*xh2,axis=-1,keepdims=True)*(1.0/D)
        bl=branch.astype(f32)
        gm=bl+r2*(h-m1-xh2*m2)
        GM[rows]=gm
        gl=gm.astype(bf16)
        gwout[...]+=tn(att,gl)
        ATT[rows]=nt(gl,wout[...]).astype(bf16)
        gsmall[4:5]+=jnp.sum(gl.astype(f32),axis=0,keepdims=True)
        gsmall[5:6]+=jnp.sum(gn2*xh2,axis=0,keepdims=True)
        gsmall[6:7]+=jnp.sum(gn2,axis=0,keepdims=True)
        gsmall[7:8]+=jnp.sum(bl,axis=0,keepdims=True)
        cp.wait()
        return _
    def battn_row(r):
        rows=pl.ds(pl.multiple_of(r*SP,16),SP)
        for g in range(2):
            go=ATT[rows,256*g:256*g+256]
            q=QKV[rows,256*g:256*g+256]
            v=QKV[rows,1024+256*g:1024+256*g+256]
            ps=PT[2*r+g]
            p=ps.astype(f32)
            bgo=stack(go)
            dp=nt(v,bgo)
            delta=jnp.sum(p*dp,axis=0,keepdims=True)
            ds=(p*(dp-delta)).astype(bf16)
            gv=nn(ps,bgo)
            gk=nn(ds,stack(q))
            dsq=ds.T
            gqs=[]
            for t in range(2):
                k=QKV[rows,512+256*g+128*t:512+256*g+128*t+128]
                o=nn(dsq[2*SP*t:2*SP*t+2*SP],k)
                gqs.append((jnp.where(low_half,o[0:SP],o[SP:2*SP])*0.125).astype(bf16))
            for t in range(2):
                QKV[rows,256*g+128*t:256*g+128*t+128]=gqs[t]
            QKV[rows,512+256*g:512+256*g+256]=gk.astype(bf16)
            QKV[rows,1024+256*g:1024+256*g+256]=gv.astype(bf16)
    def battn(r,_):
        for u in range(UN): battn_row(r*UN+u)
        return _
    def p3(b,_):
        load_x(b)
        rows=pl.ds(pl.multiple_of(b*M,16),M)
        gq=QKV[rows]
        gwqkv[...]+=tn(FL[rows],gq)
        gn1=nt(gq,wqkv[...])
        xh1,r1=norm(xs[...])
        h=gn1*g1
        m1=jnp.sum(h,axis=-1,keepdims=True)*(1.0/D)
        m2=jnp.sum(h*xh1,axis=-1,keepdims=True)*(1.0/D)
        res=(GM[rows]+r1*(h-m1-xh1*m2)).astype(bf16)
        for i in range(RB):
            ost[i]=res[SP*i:SP*i+S]
        cp=pltpu.make_async_copy(ost,gtok.at[pl.ds(b*RB,RB)],osem)
        cp.start()
        gsmall[0:1]+=jnp.sum(gn1*xh1,axis=0,keepdims=True)
        gsmall[1:2]+=jnp.sum(gn1,axis=0,keepdims=True)
        gsmall[2:3]+=jnp.sum(gq[:,0:512].astype(f32),axis=0,keepdims=True)
        gsmall[3:4]+=jnp.sum(gq[:,1024:1536].astype(f32),axis=0,keepdims=True)
        cp.wait()
        return _
    for ref in (gwqkv,gwout,gwup,gbup,gwdown,gsmall):
        ref[...]=jnp.zeros(ref.shape,f32)
    if '1' in phases: lax.fori_loop(0,NB,p1,0)
    if 'a' in phases: lax.fori_loop(0,R//UN,attn,0)
    if '2' in phases: lax.fori_loop(0,NB,p2,0)
    if 'b' in phases: lax.fori_loop(0,R//UN,battn,0)
    if '3' in phases: lax.fori_loop(0,NB,p3,0)

def compute(tok,seg,wqkv,wout,wup,bup,wdown,small,cot,RB=6,FC=512,phases='1a2b3'):
    R,S,_=tok.shape
    SP=(S+15)//16*16
    FF=wup.shape[1]
    M=RB*SP
    T=R*SP
    V=pltpu.VMEM
    vm=pl.BlockSpec(memory_space=pltpu.VMEM); an=pl.BlockSpec(memory_space=pl.ANY)
    outs=[jax.ShapeDtypeStruct(tok.shape,bf16),jax.ShapeDtypeStruct(tok.shape,bf16)]+[jax.ShapeDtypeStruct(s,f32) for s in ((D,3*D),(D,D),(D,FF),(1,FF),(FF,D),(8,D))]
    return pl.pallas_call(functools.partial(compute_kernel,R,S,SP,RB,FC,FF,phases),
        out_shape=outs, in_specs=[vm]*9, out_specs=[an]*2+[vm]*6,
        scratch_shapes=[V((M,D),f32),V((M,D),bf16),V((T,D),bf16),V((T,3*D),bf16),V((T,D),bf16),V((2*R,SP,4*SP),bf16),V((T,D),f32),V((R,1,4*SP),jnp.int32),V((RB,S,D),bf16),pltpu.SemaphoreType.DMA,
          V((8,128),f32),V((8,128),f32),V((8,128),bf16),V((8,128),bf16)],
        compiler_params=pltpu.CompilerParams(vmem_limit_bytes=60<<20),
    )(tok,seg,wqkv,wout,wup,bup,wdown,small,cot)


def body(tokens, segment_ids, qkv_weight, out_weight, up_weight, up_bias, down_weight, small_params, cotangent):
    axes = ("dp", "fsdp")
    gather = lambda v: lax.all_gather(v, axes, axis=0, tiled=True)
    scatter = lambda v: lax.psum_scatter(v.reshape(-1), axes, scatter_dimension=0, tiled=True)
    packed = lax.all_gather(jnp.concatenate([up_bias, small_params]), axes, axis=0, tiled=False)
    nb = up_bias.shape[0]
    bias = packed[:, :nb].reshape(1, -1)
    small = packed[:, nb:].reshape(8, D)
    FF = bias.shape[1]
    o = compute(tokens, segment_ids, gather(qkv_weight).reshape(D, 3 * D), gather(out_weight).reshape(D, D),
                gather(up_weight).reshape(D, FF), bias, gather(down_weight).reshape(FF, D), small, cotangent)
    return (o[0], o[1], scatter(o[2]), scatter(o[3]), scatter(o[4]), scatter(o[5]), scatter(o[6]), scatter(o[7]))


def solution(mesh):
    rows, flat = P(("dp", "fsdp"), None, None), P(("dp", "fsdp"))
    in_specs = (rows, P(("dp", "fsdp"), None), flat, flat, flat, flat, flat, flat, rows)
    out_specs = (rows, rows, flat, flat, flat, flat, flat, flat)
    return jax.shard_map(body, mesh=mesh, in_specs=in_specs, out_specs=out_specs, check_vma=False)
```

```python
import functools

import jax
import jax.numpy as jnp
from jax import lax
from jax.experimental import pallas as pl
from jax.experimental.pallas import tpu as pltpu
from jax.sharding import PartitionSpec as P

bf16 = jnp.bfloat16
f32 = jnp.float32
HEADS = 8
HEAD_DIM = 64
GROUP = 4
NORM_EPS = 1e-05
GELU_SLOPE = 1.702
MASKED_SCORE = -1e30
MESH = pl.DeviceIdType.MESH
ROW_BLOCK = 6
UNROLL = 2
ARRAYS = ("qkv", "out", "up", "down")


def nn(a, b):
    return lax.dot_general(a, b, (((1,), (0,)), ((), ())), preferred_element_type=f32)


def nt(a, b):
    return lax.dot_general(a, b, (((1,), (1,)), ((), ())), preferred_element_type=f32)


def tn(a, b):
    return lax.dot_general(a, b, (((0,), (0,)), ((), ())), preferred_element_type=f32)


def col_sum(v):
    return jnp.sum(v, axis=0, keepdims=True)


def lane_mean(v):
    return jnp.sum(v, axis=-1, keepdims=True) * (1.0 / v.shape[-1])


def normalize(x):
    xc = x - lane_mean(x)
    inv = lax.rsqrt(lane_mean(xc * xc) + NORM_EPS)
    return xc * inv, inv


def flip(index, bits):
    low, high = index % 2, index // 2
    if bits & 1:
        low = 1 - low
    if bits & 2:
        high = 1 - high
    return high * 2 + low


class Gather:
    def __init__(self, buf, send, recv, pos):
        self.buf, self.send, self.recv = buf, send, recv
        self.dp, self.z, self.c = pos

    def copy(self, index, slot, device):
        ref = self.buf.at[index]
        return pltpu.make_async_remote_copy(
            src_ref=ref, dst_ref=ref, send_sem=self.send.at[slot], recv_sem=self.recv.at[slot],
            device_id=device, device_id_type=MESH)

    def along_z(self, k, mine=True):
        z = self.z if mine else flip(self.z, k)
        return self.copy((self.dp, z, self.c), k - 1, (self.dp, flip(self.z, k) * 2 + self.c))

    def column(self, bit, mine=True):
        dp = self.dp if mine else flip(self.dp, bit)
        return self.copy((dp, slice(None), self.c), 2 + bit, (flip(self.dp, bit), self.z * 2 + self.c))

    def onward(self, bit, mine=True):
        other = 3 - bit
        dp = flip(self.dp, other) if mine else flip(self.dp, 3)
        half = pl.ds(0, 2) if bit == 2 else pl.ds(2, 2)
        return self.copy((dp, half, self.c), 4 + bit, (flip(self.dp, bit), self.z * 2 + self.c))

    def to_core(self, mine=True):
        c = self.c if mine else 1 - self.c
        return self.copy((slice(None), slice(None), c), 7, (self.dp, self.z * 2 + 1 - self.c))

    def start_z(self):
        for k in (1, 2, 3):
            self.along_z(k).start()

    def start_column(self):
        for k in (1, 2, 3):
            self.along_z(k, False).wait_recv()
        for bit in (1, 2):
            self.column(bit).start()

    def start_onward(self):
        for bit in (1, 2):
            self.column(3 - bit, False).wait_recv()
            self.onward(bit).start()

    def start_core(self):
        for bit in (1, 2):
            self.onward(bit, False).wait_recv()
        self.to_core().start()

    def finish(self):
        self.to_core(False).wait_recv()
        for k in (1, 2, 3):
            self.along_z(k).wait_send()
        for bit in (1, 2):
            self.column(bit).wait_send()
            self.onward(bit).wait_send()
        self.to_core().wait_send()


class Scatter:
    def __init__(self, grad, half, from_core, from_dp, from_z, send, recv, pos, dtype=bf16):
        self.grad, self.half, self.from_core, self.from_dp, self.from_z = grad, half, from_core, from_dp, from_z
        self.send, self.recv, self.dtype = send, recv, dtype
        self.dp, self.z, self.c = pos

    def copy(self, src, dst, slot, device):
        return pltpu.make_async_remote_copy(
            src_ref=src, dst_ref=dst, send_sem=self.send.at[slot], recv_sem=self.recv.at[slot],
            device_id=device, device_id_type=MESH)

    def core_copy(self):
        return self.copy(self.half, self.from_core, 0, (self.dp, self.z * 2 + 1 - self.c))

    def dp_copy(self, k):
        return self.copy(self.from_core.at[flip(self.dp, k)], self.from_dp.at[k - 1], k,
                         (flip(self.dp, k), self.z * 2 + self.c))

    def z_copy(self, k):
        return self.copy(self.from_dp.at[0, flip(self.z, k)], self.from_z.at[k - 1], 3 + k,
                         (self.dp, flip(self.z, k) * 2 + self.c))

    def start_core(self, whole=None):
        if whole is None:
            self.half[...] = self.grad[:, :, 1 - self.c].astype(self.dtype)
        else:
            zero, one = whole[:, :, 0], whole[:, :, 1]
            self.grad[...] = jnp.where(self.c == 0, zero, one)
            self.half[...] = jnp.where(self.c == 0, one, zero).astype(self.dtype)
        self.core_copy().start()

    def own(self, *index):
        return index if len(self.grad.shape) == 4 else index + (slice(None),) * (2 - len(index)) + (self.c,)

    def start_dp(self):
        self.core_copy().wait_recv()
        for k in (1, 2, 3):
            dp = flip(self.dp, k)
            self.from_core[dp] = (self.grad[self.own(dp)] + self.from_core[dp].astype(f32)).astype(self.dtype)
            self.dp_copy(k).start()

    def start_z(self):
        for k in (1, 2, 3):
            self.dp_copy(k).wait_recv()
        total = self.grad[self.own(self.dp)] + self.from_core[self.dp].astype(f32)
        for k in (1, 2, 3):
            total += self.from_dp[k - 1].astype(f32)
        self.grad[self.own(self.dp)] = total
        self.from_dp[0] = total.astype(self.dtype)
        for k in (1, 2, 3):
            self.z_copy(k).start()

    def finish(self):
        for k in (1, 2, 3):
            self.z_copy(k).wait_recv()
        total = self.grad[self.own(self.dp, self.z)]
        for k in (1, 2, 3):
            total += self.from_z[k - 1].astype(f32)
        self.core_copy().wait_send()
        for k in (1, 2, 3):
            self.dp_copy(k).wait_send()
            self.z_copy(k).wait_send()
        return total


def block_kernel(comm, R, S, SP, D, FF, *refs):
    RB, M, NB, FC = ROW_BLOCK, ROW_BLOCK * SP, R // ROW_BLOCK, FF // 4
    GW = GROUP * HEAD_DIM
    refs = list(refs)

    def take(n):
        out = refs[:n]
        del refs[:n]
        return out

    tok, seg, cot = take(3)
    shards = dict(zip(ARRAYS + ("small",), take(5)))
    out, gtok = take(2)
    if comm:
        shares = dict(zip(ARRAYS + ("small",), take(5)))
    else:
        grads = dict(zip(ARRAYS + ("small",), take(5)))
    tokv, cbuf, xs, cs, FL, QKV, ATT, PT, GM, start, bias, smallv, gbias, gsmall = take(14)
    tsem, csem, osem = take(3)
    if comm:
        weights = dict(zip(ARRAYS, take(4)))
        grads = dict(zip(ARRAYS + ("small",), take(5)))
        from_core = dict(zip(ARRAYS + ("small",), take(5)))
        from_dp = dict(zip(ARRAYS + ("small",), take(5)))
        from_z = dict(zip(ARRAYS + ("small",), take(5)))
        small_half, gsend, grecv, ssend, srecv = take(5)
    else:
        weights = {k: shards[k] for k in ARRAYS}

    tok_copy = pltpu.make_async_copy(tok, tokv, tsem)
    tok_copy.start()

    def cot_copy(b, slot):
        return pltpu.make_async_copy(cot.at[pl.ds(b * RB, RB)], cbuf.at[slot], csem.at[slot])

    def out_copy(b, slot):
        return pltpu.make_async_copy(cbuf.at[slot], out.at[pl.ds(b * RB, RB)], osem.at[slot])

    cot_copy(0, 0).start()

    if comm:
        dp = lax.axis_index("dp")
        fs = lax.axis_index("fsdp")
        pos = (dp, fs // 2, fs % 2)
        z, c = pos[1], pos[2]
        peers = [(flip(dp, k), fs) for k in (1, 2, 3)] + [(dp, flip(z, k) * 2 + c) for k in (1, 2, 3)]
        peers.append((dp, z * 2 + 1 - c))
        barrier = pltpu.get_barrier_semaphore()
        for peer in peers:
            pl.semaphore_signal(barrier, inc=1, device_id=peer, device_id_type=MESH)
        spread = grads["small"].reshape(256, 128)
        for name in ARRAYS:
            rows, cols = weights[name].shape[3:]
            if name == "qkv":
                cols -= 128
            per = cols // 128
            src = shards[name]
            spread[0 : src.shape[0]] = src[...].astype(f32)
            for j in range(per):
                weights[name][dp, z, c, :, 128 * j : 128 * j + 128] = spread[pl.ds(j, rows, stride=per), :].astype(bf16)
        weights["qkv"][dp, z, c, :, 3 * D :] = shards["small"][...]
        gathers = {n: Gather(weights[n], gsend.at[i], grecv.at[i], pos) for i, n in enumerate(ARRAYS)}
        pl.semaphore_wait(barrier, len(peers))
        gathers["qkv"].start_z()
        gathers["qkv"].start_column()
        for name in ARRAYS[1:]:
            gathers[name].start_z()
        rest = [gathers[n] for n in ARRAYS[1:]]

    xs[...] = jnp.zeros(xs.shape, f32)
    cs[...] = jnp.zeros(cs.shape, bf16)
    sg = seg[...]
    st = jnp.zeros(sg.shape, jnp.int32)
    for v in range(1, 4):
        count = jnp.sum((sg < v).astype(f32), axis=1, keepdims=True).astype(jnp.int32)
        st = jnp.where(sg == v, count, st)
    st = jnp.concatenate([st, jnp.zeros((R, SP - S), jnp.int32)], axis=1)
    start[...] = jnp.concatenate([st] * GROUP, axis=1).reshape(R, 1, GROUP * SP)
    for ref in (grads["out"], grads["up"], grads["down"], gbias, gsmall):
        ref[...] = jnp.zeros(ref.shape, f32)
    tok_copy.wait()

    def load_x(b):
        for i in range(RB):
            xs[SP * i : SP * i + S] = tokv[b * RB + i].astype(f32)

    def rows_of(b):
        return pl.ds(pl.multiple_of(b * M, 16), M)

    def norm_one(b, carry):
        load_x(b)
        GM[rows_of(b)] = normalize(xs[...])[0]
        return carry

    if comm:
        gathers["qkv"].start_onward()
        lax.fori_loop(0, NB // 2, norm_one, 0)
        gathers["qkv"].start_core()
        lax.fori_loop(NB // 2, NB, norm_one, 0)
        gathers["qkv"].finish()
        wq = weights["qkv"]
        for s in range(32):
            piece = wq[s // 8, (s % 8) // 2, s % 2, :, 3 * D :].astype(f32)
            smallv[s // 4 : s // 4 + 1, 128 * (s % 4) : 128 * (s % 4) + 128] = piece[0:1]
        for s in range(0, 32, 2):
            two = [wq[s // 8, (s % 8) // 2, i, :, 3 * D : 3 * D + 64].astype(f32)[1:2] for i in (0, 1)]
            bias[:, 64 * s : 64 * s + 128] = jnp.concatenate(two, axis=1)
        for g in rest:
            g.start_column()
    else:
        lax.fori_loop(0, NB, norm_one, 0)
        bias[...] = shards["small"][8:12].astype(f32).reshape(1, FF)
        smallv[...] = shards["small"][0:8].astype(f32)

    def w_qkv(a, b):
        return weights["qkv"][:, :, :, :, a:b].reshape(D, b - a)

    sm = smallv[...]
    g1, c1, bq, bv, bo, g2, c2, bd = [sm[i : i + 1] for i in range(8)]
    scale = HEAD_DIM ** (-0.5)
    bkv = jnp.concatenate([jnp.zeros_like(bv), bv], axis=1)
    lane = lax.broadcasted_iota(jnp.int32, (1, GW), 1)
    head_mask = [(lane // HEAD_DIM == j).astype(f32).astype(bf16) for j in range(GROUP)]
    low_half = lax.broadcasted_iota(jnp.int32, (1, 128), 1) < HEAD_DIM

    def stack(v):
        return jnp.concatenate([v * head_mask[j] for j in range(GROUP)], axis=0)

    def project(b, carry):
        rows = rows_of(b)
        fl = (GM[rows] * g1 + c1).astype(bf16)
        FL[rows] = fl
        QKV[rows, 0:D] = ((nn(fl, w_qkv(0, D)) + bq) * scale).astype(bf16)
        QKV[rows, D : 3 * D] = (nn(fl, w_qkv(D, 3 * D)) + bkv).astype(bf16)
        return carry

    kidx = lax.broadcasted_iota(jnp.int32, (SP, GROUP * SP), 0)
    qidx = lax.broadcasted_iota(jnp.int32, (1, GROUP * SP), 1)
    qidx = qidx - SP * sum((qidx >= SP * j).astype(jnp.int32) for j in range(1, GROUP))

    def attend_row(r):
        rows = pl.ds(pl.multiple_of(r * SP, 16), SP)
        allowed = (kidx >= start[r]) & (kidx <= qidx)
        for g in range(HEADS // GROUP):
            q = QKV[rows, GW * g : GW * g + GW]
            k = QKV[rows, D + GW * g : D + GW * g + GW]
            s = jnp.where(allowed, nt(k, stack(q)), MASKED_SCORE)
            e = jnp.exp(s - jnp.max(s, axis=0, keepdims=True))
            p = (e * (1.0 / col_sum(e))).astype(bf16)
            PT[2 * r + g] = p
            pq = p.T
            for t in range(GW // 128):
                at = GW * g + 128 * t
                v = QKV[rows, 2 * D + at : 2 * D + at + 128]
                o = nn(pq[2 * SP * t : 2 * SP * t + 2 * SP], v)
                ATT[rows, at : at + 128] = jnp.where(low_half, o[0:SP], o[SP : 2 * SP]).astype(bf16)

    def attend(i, carry):
        for u in range(UNROLL):
            attend_row(i * UNROLL + u)
        return carry

    def feed(b, carry):
        load_x(b)
        slot = b % 2
        cot_copy(b, slot).wait()

        for i in range(RB):
            cs[SP * i : SP * i + S] = cbuf[slot, i]

        @pl.when(b > 0)
        def _():
            out_copy(b - 1, 1 - slot).wait()

        @pl.when(b + 1 < NB)
        def _():
            cot_copy(b + 1, 1 - slot).start()

        rows = rows_of(b)
        att = ATT[rows]
        w_out = weights["out"][...].reshape(D, D)
        mid = xs[...] + nn(att, w_out) + bo
        GM[rows] = mid + bd
        xh2, r2 = normalize(mid)
        xs[...] = xh2
        second = (xh2 * g2 + c2).astype(bf16)
        branch = cs[...]
        gn2 = jnp.zeros((M, D), f32)
        for j in range(FF // FC):
            cc = slice(j * FC, (j + 1) * FC)
            w_up = weights["up"][:, :, :, :, cc].reshape(D, FC)
            w_down = weights["down"][j].reshape(FC, D)
            pre = nn(second, w_up) + bias[:, cc]
            s = 0.5 * jnp.tanh((0.5 * GELU_SLOPE) * pre) + 0.5
            a = pre * s
            act = a.astype(bf16)
            gp = (nt(branch, w_down) * (s + GELU_SLOPE * a * (1.0 - s))).astype(bf16)
            gbias[:, cc] += col_sum(gp.astype(f32))
            GM[rows] += nn(act, w_down)
            gn2 = gn2 + nt(gp, w_up)
            grads["down"][j] += tn(act, branch).reshape(grads["down"].shape[1:])
            grads["up"][:, :, :, :, cc] += tn(second, gp).reshape(grads["up"].shape[:4] + (FC,))
        res = GM[rows].astype(bf16)
        for i in range(RB):
            cbuf[slot, i] = res[SP * i : SP * i + S]
        out_copy(b, slot).start()
        xh2 = xs[...]
        h = gn2 * g2
        up = branch.astype(f32)
        gm = up + r2 * (h - lane_mean(h) - xh2 * lane_mean(h * xh2))
        GM[rows] = gm
        gl = gm.astype(bf16)
        grads["out"][...] += tn(att, gl).reshape(grads["out"].shape)
        ATT[rows] = nt(gl, w_out).astype(bf16)
        gsmall[4:5] += col_sum(gl.astype(f32))
        gsmall[5:6] += col_sum(gn2 * xh2)
        gsmall[6:7] += col_sum(gn2)
        gsmall[7:8] += col_sum(up)
        return carry

    def attend_back_row(r):
        rows = pl.ds(pl.multiple_of(r * SP, 16), SP)
        for g in range(HEADS // GROUP):
            here = slice(GW * g, GW * g + GW)
            q = QKV[rows, here]
            v = QKV[rows, 2 * D + GW * g : 2 * D + GW * g + GW]
            low = PT[2 * r + g]
            p = low.astype(f32)
            go = stack(ATT[rows, here])
            dpr = nt(v, go)
            ds = (p * (dpr - col_sum(p * dpr))).astype(bf16)
            gv = nn(low, go)
            gk = nn(ds, stack(q))
            dsq = ds.T
            parts = []
            for t in range(GW // 128):
                at = D + GW * g + 128 * t
                o = nn(dsq[2 * SP * t : 2 * SP * t + 2 * SP], QKV[rows, at : at + 128])
                parts.append((jnp.where(low_half, o[0:SP], o[SP : 2 * SP]) * scale).astype(bf16))
            for t in range(GW // 128):
                QKV[rows, GW * g + 128 * t : GW * g + 128 * t + 128] = parts[t]
            QKV[rows, D + GW * g : D + GW * g + GW] = gk.astype(bf16)
            QKV[rows, 2 * D + GW * g : 2 * D + GW * g + GW] = gv.astype(bf16)

    def attend_back(i, carry):
        for u in range(UNROLL):
            attend_back_row(i * UNROLL + u)
        return carry

    def input_grad(b, carry):
        load_x(b)
        rows = rows_of(b)
        gq = QKV[rows]
        gn1 = nt(gq, w_qkv(0, 3 * D))
        xh1, r1 = normalize(xs[...])
        h = gn1 * g1
        res = (GM[rows] + r1 * (h - lane_mean(h) - xh1 * lane_mean(h * xh1))).astype(bf16)
        for i in range(RB):
            tokv[b * RB + i] = res[SP * i : SP * i + S]
        gsmall[0:1] += col_sum(gn1 * xh1)
        gsmall[1:2] += col_sum(gn1)
        gsmall[2:3] += col_sum(gq[:, 0:D].astype(f32))
        gsmall[3:4] += col_sum(gq[:, 2 * D : 3 * D].astype(f32))
        return carry

    def loop(a, b, f):
        lax.fori_loop(a, b, f, 0)

    def qkv_grad(j):
        return tn(FL[...], QKV[:, j * D : (j + 1) * D]).reshape(4, 4, 2, D // 32, D)

    NA = R // UNROLL
    if not comm:
        loop(0, NB, project)
        loop(0, NA, attend)
        loop(0, NB, feed)
        out_copy(NB - 1, (NB - 1) % 2).wait()
        loop(0, NA, attend_back)
        for j in range(3):
            grads["qkv"][:, :, :, :, j * D : (j + 1) * D] = qkv_grad(j)
        loop(0, NB, input_grad)
        tok_back = pltpu.make_async_copy(tokv, gtok, tsem)
        tok_back.start()
        tok_back.wait()
        grads["small"][0:8] = gsmall[...]
        grads["small"][8:12] = gbias[...].reshape(4, D)
        return

    loop(0, NB, project)
    for g in rest:
        g.start_onward()
    loop(0, NA // 2, attend)
    for g in rest:
        g.start_core()
    loop(NA // 2, NA, attend)
    for g in rest:
        g.finish()
    loop(0, NB, feed)
    out_copy(NB - 1, (NB - 1) % 2).wait()

    scat = {}
    for i, name in enumerate(ARRAYS[1:]):
        scat[name] = Scatter(grads[name], weights[name].at[:, :, 0], from_core[name], from_dp[name], from_z[name],
                             ssend.at[i], srecv.at[i], pos)
    for j in range(3):
        cols = pl.ds(j * D, D)
        scat[j] = Scatter(grads["qkv"].at[:, :, :, cols], weights["up"].at[:, :, 1, :, cols],
                          from_core["qkv"].at[:, :, :, cols], from_dp["qkv"].at[:, :, :, cols],
                          from_z["qkv"].at[:, :, cols], ssend.at[3 + j], srecv.at[3 + j], pos)
    scat["small"] = Scatter(grads["small"], small_half, from_core["small"], from_dp["small"], from_z["small"],
                            ssend.at[6], srecv.at[6], pos, f32)
    rest = [scat[n] for n in ARRAYS[1:]]

    for s in rest:
        s.start_core()
    loop(0, NA // 3, attend_back)
    for s in rest:
        s.start_dp()
    loop(NA // 3, NA, attend_back)
    for j in range(3):
        scat[j].start_core(qkv_grad(j))
        if j:
            scat[j - 1].start_dp()
    for s in rest:
        s.start_z()
    loop(0, NB // 2, input_grad)
    scat[2].start_dp()
    for j in range(2):
        scat[j].start_z()
    loop(NB // 2, NB, input_grad)
    tok_back = pltpu.make_async_copy(tokv, gtok, tsem)
    tok_back.start()
    gs = grads["small"]
    for s in range(32):
        row = s // 4
        gs[s // 8, (s % 8) // 2, s % 2, 0:1, 0:128] = gsmall[row : row + 1, 128 * (s % 4) : 128 * (s % 4) + 128]
        two = gbias[:, 128 * (s // 2) : 128 * (s // 2) + 128]
        gs[s // 8, (s % 8) // 2, s % 2, 1:2, 0:64] = two[:, 64 * (s % 2) : 64 * (s % 2) + 64]
    small = scat["small"]
    small.start_core()
    scat[2].start_z()

    def give(name, total, first=0):
        rows, cols = total.shape
        per = shards[name].shape[0] // rows
        for j in range(cols // 128):
            shares[name][pl.ds(first + j, rows, stride=per), :] = total[:, 128 * j : 128 * j + 128]

    small.start_dp()
    for name in ARRAYS[1:]:
        give(name, scat[name].finish())
    small.start_z()
    for j in range(3):
        give("qkv", scat[j].finish(), j * D // 128)
    shares["small"][...] = small.finish()
    tok_back.wait()


def block_call(comm, tokens, segments, cotangent, pieces, FF):
    R, S, D = tokens.shape
    SP = (S + 15) // 16 * 16
    T, M = R * SP, ROW_BLOCK * SP
    V, dma = pltpu.VMEM, pltpu.SemaphoreType.DMA
    vm, hbm = pl.BlockSpec(memory_space=pltpu.VMEM), pl.BlockSpec(memory_space=pl.ANY)
    rows = {"qkv": (16, 3 * D), "out": (16, D), "up": (16, FF), "down": (FF // 32, D)}
    out_shape = [jax.ShapeDtypeStruct(tokens.shape, bf16)] * 2
    if comm:
        out_shape += [jax.ShapeDtypeStruct(p.shape, f32) for p in pieces[:4]]
        out_shape += [jax.ShapeDtypeStruct((8, 128), f32)]
    else:
        out_shape += [jax.ShapeDtypeStruct((4, 4, 2) + rows[n], f32) for n in ARRAYS]
        out_shape += [jax.ShapeDtypeStruct((12, D), f32)]
    scratch = [
        V((R, S, D), bf16), V((2, ROW_BLOCK, S, D), bf16), V((M, D), f32), V((M, D), bf16), V((T, D), bf16),
        V((T, 3 * D), bf16), V((T, D), bf16), V((2 * R, SP, GROUP * SP), bf16), V((T, D), f32),
        V((R, 1, GROUP * SP), jnp.int32), V((1, FF), f32), V((8, D), f32),
        V((1, FF), f32), V((8, D), f32), dma, dma((2,)), dma((2,)),
    ]
    if comm:
        small = {"small": (8, 128)}
        wide = {n: (r, cl + (128 if n == "qkv" else 0)) for n, (r, cl) in rows.items()}
        scratch += [V((4, 4, 2) + wide[n], bf16) for n in ARRAYS]
        for lead in ((4, 4, 2), (4, 4), (3, 4), (3,)):
            kind = f32 if lead == (4, 4, 2) else bf16
            scratch += [V(((4, 4) if n == "qkv" and kind == f32 else lead) + rows[n], kind) for n in ARRAYS]
            scratch += [V(lead + small["small"], f32)]
        scratch += [V((4, 4, 8, 128), f32), dma((4, 8)), dma((4, 8)), dma((7, 7)), dma((7, 7))]
    params = dict(vmem_limit_bytes=63 * 1000 * 1000 + 256 * 1024)
    if comm:
        params.update(collective_id=1, has_side_effects=True)
    return pl.pallas_call(
        functools.partial(block_kernel, comm, R, S, SP, D, FF),
        out_shape=out_shape,
        in_specs=[hbm, vm, hbm] + [vm] * 5,
        out_specs=[hbm, hbm] + [vm] * 5,
        scratch_shapes=scratch,
        compiler_params=pltpu.CompilerParams(**params),
    )(tokens, segments, cotangent, *pieces)


def body(sizes, tokens, segment_ids, qkv_weight, out_weight, up_weight, up_bias, down_weight, small_params, cotangent):
    D = tokens.shape[2]
    n = sizes[0] * sizes[1]
    FF = up_bias.shape[0] * n
    flats = (qkv_weight, out_weight, up_weight, down_weight)
    if sizes == (4, 8):
        tile = jnp.pad(jnp.concatenate([small_params, up_bias]), (0, 16 * 128 - 192)).reshape(16, 128)
        o = block_call(True, tokens, segment_ids, cotangent, [f.reshape(-1, 128) for f in flats] + [tile], FF)
        shares = [v.reshape(-1) for v in o[2:6]]
        return (o[0], o[1], shares[0], shares[1], shares[2], o[6][1, :64], shares[3], o[6][0])
    axes = ("dp", "fsdp")

    def gather(v):
        return lax.all_gather(v, axes, axis=0, tiled=True)

    def scatter(v):
        return lax.psum_scatter(v.reshape(-1), axes, scatter_dimension=0, tiled=True)

    packed = lax.all_gather(jnp.concatenate([small_params, up_bias]), axes, axis=0, tiled=False)
    count = small_params.shape[0]
    tile = jnp.concatenate([packed[:, :count].reshape(8, D), packed[:, count:].reshape(4, D)])
    whole = [gather(f) for f in flats]
    shapes = ((4, 4, 2, 16, 3 * D), (4, 4, 2, 16, D), (4, 4, 2, 16, FF), (4, 4, 2, FF // 32, D))
    o = block_call(False, tokens, segment_ids, cotangent, [w.reshape(s) for w, s in zip(whole, shapes)] + [tile], FF)
    return (o[0], o[1], scatter(o[2]), scatter(o[3]), scatter(o[4]), scatter(o[6][8:12]), scatter(o[5]), scatter(o[6][0:8]))


def solution(mesh):
    rows, flat = P(("dp", "fsdp"), None, None), P(("dp", "fsdp"))
    in_specs = (rows, P(("dp", "fsdp"), None), flat, flat, flat, flat, flat, flat, rows)
    out_specs = (rows, rows, flat, flat, flat, flat, flat, flat)
    sizes = (mesh.shape["dp"], mesh.shape["fsdp"])
    return jax.shard_map(functools.partial(body, sizes), mesh=mesh, in_specs=in_specs, out_specs=out_specs, check_vma=False)
```

```python
import functools

import jax
import jax.numpy as jnp
from jax import lax
from jax.experimental import pallas as pl
from jax.experimental.pallas import tpu as pltpu
from jax.sharding import PartitionSpec as P

bf16 = jnp.bfloat16
f32 = jnp.float32
HEADS = 8
HEAD_DIM = 64
GROUP = 4
NORM_EPS = 1e-05
GELU_SLOPE = 1.702
MASKED_SCORE = -1e30
MESH = pl.DeviceIdType.MESH
ROW_BLOCK = 6
UNROLL = 3
ARRAYS = ("qkv", "out", "up", "down")
HELD = ("qkv", "out", "up0", "down", "up1")


def nn(a, b):
    return lax.dot_general(a, b, (((1,), (0,)), ((), ())), preferred_element_type=f32)


def nt(a, b):
    return lax.dot_general(a, b, (((1,), (1,)), ((), ())), preferred_element_type=f32)


def tn(a, b):
    return lax.dot_general(a, b, (((0,), (0,)), ((), ())), preferred_element_type=f32)


def col_sum(v):
    return jnp.sum(v, axis=0, keepdims=True)


def lane_mean(v):
    return jnp.sum(v, axis=-1, keepdims=True) * (1.0 / v.shape[-1])


def normalize(x):
    xc = x - lane_mean(x)
    inv = lax.rsqrt(lane_mean(xc * xc) + NORM_EPS)
    return xc * inv, inv


def flip(index, bits):
    low, high = index % 2, index // 2
    if bits & 1:
        low = 1 - low
    if bits & 2:
        high = 1 - high
    return high * 2 + low


class Gather:
    def __init__(self, buf, send, recv, pos):
        self.buf, self.send, self.recv = buf, send, recv
        self.dp, self.z, self.c = pos

    def copy(self, index, slot, device):
        ref = self.buf.at[index]
        return pltpu.make_async_remote_copy(
            src_ref=ref, dst_ref=ref, send_sem=self.send.at[slot], recv_sem=self.recv.at[slot],
            device_id=device, device_id_type=MESH)

    def along_z(self, k, mine=True):
        z = self.z if mine else flip(self.z, k)
        return self.copy((self.dp, z, self.c), k - 1, (self.dp, flip(self.z, k) * 2 + self.c))

    def column(self, bit, mine=True):
        dp = self.dp if mine else flip(self.dp, bit)
        return self.copy((dp, slice(None), self.c), 2 + bit, (flip(self.dp, bit), self.z * 2 + self.c))

    def onward(self, bit, mine=True):
        other = 3 - bit
        dp = flip(self.dp, other) if mine else flip(self.dp, 3)
        half = pl.ds(0, 2) if bit == 2 else pl.ds(2, 2)
        return self.copy((dp, half, self.c), 4 + bit, (flip(self.dp, bit), self.z * 2 + self.c))

    def to_core(self, mine=True):
        c = self.c if mine else 1 - self.c
        return self.copy((slice(None), slice(None), c), 7, (self.dp, self.z * 2 + 1 - self.c))

    def start_z(self):
        for k in (1, 2, 3):
            self.along_z(k).start()

    def start_column(self):
        for k in (1, 2, 3):
            self.along_z(k, False).wait_recv()
        for bit in (1, 2):
            self.column(bit).start()

    def start_onward(self):
        for bit in (1, 2):
            self.column(3 - bit, False).wait_recv()
            self.onward(bit).start()

    def start_core(self):
        for bit in (1, 2):
            self.onward(bit, False).wait_recv()
        self.to_core().start()

    def finish(self):
        self.to_core(False).wait_recv()
        for k in (1, 2, 3):
            self.along_z(k).wait_send()
        for bit in (1, 2):
            self.column(bit).wait_send()
            self.onward(bit).wait_send()
        self.to_core().wait_send()


class EagerGather(Gather):
    def shard(self, k, bit, mine=True):
        dp = self.dp if mine else flip(self.dp, bit)
        return self.copy((dp, flip(self.z, k), self.c), 2 + bit * 4 + k - 1, (flip(self.dp, bit), self.z * 2 + self.c))

    def forward(self, k, mine=True):
        bit = 2 - k % 2
        dp = flip(self.dp, 3 - bit) if mine else flip(self.dp, 3)
        return self.copy((dp, flip(self.z, k), self.c), 13 + k, (flip(self.dp, bit), self.z * 2 + self.c))

    def core_column(self, bits, mine=True):
        c = self.c if mine else 1 - self.c
        return self.copy((flip(self.dp, bits), slice(None), c), 17 + bits, (self.dp, self.z * 2 + 1 - self.c))

    def start(self):
        for k in (1, 2, 3):
            self.along_z(k).start()
        for bit in (1, 2):
            self.shard(0, bit).start()

    def start_column(self):
        for k in (1, 2, 3):
            self.along_z(k, False).wait_recv()
            for bit in (1, 2):
                self.shard(k, bit).start()
        self.core_column(0).start()

    def start_onward(self):
        for k in (0, 1, 2, 3):
            bit = 2 - k % 2
            self.shard(k, 3 - bit, False).wait_recv()
            self.forward(k).start()
        for k in (0, 1, 2, 3):
            bit = 2 - k % 2
            self.shard(k, bit, False).wait_recv()
        for bit in (1, 2):
            self.core_column(bit).start()

    def start_core(self):
        for k in (0, 1, 2, 3):
            self.forward(k, False).wait_recv()
        self.core_column(3).start()

    def finish(self):
        for bits in (0, 1, 2, 3):
            self.core_column(bits, False).wait_recv()
        for k in (1, 2, 3):
            self.along_z(k).wait_send()
        for k in (0, 1, 2, 3):
            for bit in (1, 2):
                self.shard(k, bit).wait_send()
            self.forward(k).wait_send()
            self.core_column(k).wait_send()


class Scatter:
    def __init__(self, grad, half, from_core, from_dp, from_z, send, recv, pos, dtype=bf16):
        self.grad, self.half, self.from_core, self.from_dp, self.from_z = grad, half, from_core, from_dp, from_z
        self.send, self.recv, self.dtype = send, recv, dtype
        self.dp, self.z, self.c = pos

    def copy(self, src, dst, slot, device):
        return pltpu.make_async_remote_copy(
            src_ref=src, dst_ref=dst, send_sem=self.send.at[slot], recv_sem=self.recv.at[slot],
            device_id=device, device_id_type=MESH)

    def core_copy(self):
        return self.copy(self.half, self.from_core, 0, (self.dp, self.z * 2 + 1 - self.c))

    def dp_copy(self, step, bit, onward):
        half = bit - 1 if step == 0 else 2 - bit
        dp = flip(self.dp, 3 if onward else bit)
        return self.copy(self.from_core.at[dp, pl.ds(2 * half, 2)], self.from_dp.at[2 * step + onward, bit - 1],
                         1 + 2 * (2 * step + onward) + bit - 1, (flip(self.dp, bit), self.z * 2 + self.c))

    def z_copy(self, k):
        return self.copy(self.from_core.at[self.dp, flip(self.z, k)], self.from_z.at[k - 1], 6 + k,
                         (self.dp, flip(self.z, k) * 2 + self.c))

    def start_core(self, whole=None):
        if whole is not None:
            zero, one = whole[:, :, 0], whole[:, :, 1]
            self.grad[...] = jnp.where(self.c == 0, zero, one)
            self.half[...] = jnp.where(self.c == 0, one, zero).astype(self.dtype)
        self.core_copy().start()

    def own_part(self, *index):
        return self.grad[self.own(*index)].astype(f32)

    def own(self, *index):
        return index if len(self.grad.shape) == 4 else index + (slice(None),) * (2 - len(index)) + (self.c,)

    def start_dp(self):
        self.core_copy().wait_recv()
        for bit in (1, 2):
            for onward in (1, 0):
                at = (flip(self.dp, 3 if onward else bit), pl.ds(2 * (bit - 1), 2))
                self.from_core[at] = (self.own_part(*at) + self.from_core[at].astype(f32)).astype(self.dtype)
                self.dp_copy(0, bit, onward).start()

    def start_onward(self):
        for bit in (1, 2):
            first = 3 - bit
            self.dp_copy(0, first, 1).wait_recv()
            at = (flip(self.dp, bit), pl.ds(2 * (first - 1), 2))
            total = self.own_part(*at) + self.from_core[at].astype(f32)
            self.from_core[at] = (total + self.from_dp[1, first - 1].astype(f32)).astype(self.dtype)
            self.dp_copy(1, bit, 0).start()

    def start_z(self):
        for bit in (1, 2):
            self.dp_copy(0, bit, 0).wait_recv()
            self.dp_copy(1, bit, 0).wait_recv()
        for half in (0, 1):
            at = (self.dp, pl.ds(2 * half, 2))
            total = self.own_part(*at) + self.from_core[at].astype(f32)
            total += self.from_dp[0, half].astype(f32) + self.from_dp[2, 1 - half].astype(f32)
            self.grad[self.own(*at)] = total.astype(self.grad.dtype)
            self.from_core[at] = total.astype(self.dtype)
        for k in (1, 2, 3):
            self.z_copy(k).start()

    def finish(self):
        for k in (1, 2, 3):
            self.z_copy(k).wait_recv()
        total = self.own_part(self.dp, self.z)
        for k in (1, 2, 3):
            total += self.from_z[k - 1].astype(f32)
        self.core_copy().wait_send()
        for bit in (1, 2):
            self.dp_copy(0, bit, 0).wait_send()
            self.dp_copy(0, bit, 1).wait_send()
            self.dp_copy(1, bit, 0).wait_send()
        for k in (1, 2, 3):
            self.z_copy(k).wait_send()
        return total


def block_kernel(comm, R, S, SP, D, FF, *refs):
    RB, M, NB, FC, FH = ROW_BLOCK, ROW_BLOCK * SP, R // ROW_BLOCK, FF // 8, FF // 2
    GW = GROUP * HEAD_DIM
    refs = list(refs)

    def take(n):
        out = refs[:n]
        del refs[:n]
        return out

    tok, seg, cot = take(3)
    shards = dict(zip(ARRAYS + ("small",), take(5)))
    out, gtok = take(2)
    if comm:
        shares = dict(zip(ARRAYS + ("small",), take(5)))
    else:
        grads = dict(zip(ARRAYS + ("small",), take(5)))
    tokv, cbuf, cs, QKV, ATT, PT, GM, ACC, GN, start, bias, smallv, gbias, gsmall = take(14)
    FL = ACC
    acc_up, acc_down = take(2)
    tsem, csem, osem = take(3)
    names = HELD + ("small",)
    if comm:
        weights = dict(zip(HELD, take(5)))
        small_grad = take(1)[0]
        from_core, from_dp, from_z = (dict(zip(names, take(6))) for _ in range(3))
        gsend, grecv, ssend, srecv = take(4)
        small_half = acc_up.at[:, :, 1, pl.ds(0, 8), pl.ds(D, 128)]
    else:
        weights = {k: shards[k] for k in ARRAYS if k != "up"}
        for i in (0, 1):
            weights["up%d" % i] = shards["up"].at[:, :, :, :, pl.ds(i * (FF // 2), FF // 2)]

    tok_copy = pltpu.make_async_copy(tok, tokv, tsem)
    tok_copy.start()

    def cot_copy(b, slot):
        return pltpu.make_async_copy(cot.at[pl.ds(b % NB * RB, RB)], cbuf.at[slot], csem.at[slot])

    def out_copy(b, slot):
        return pltpu.make_async_copy(cbuf.at[slot], out.at[pl.ds(b * RB, RB)], osem.at[slot])

    cot_copy(0, 0).start()
    if comm:
        dp = lax.axis_index("dp")
        fs = lax.axis_index("fsdp")
        pos = (dp, fs // 2, fs % 2)
        z, c = pos[1], pos[2]
        peers = [(flip(dp, k), fs) for k in (1, 2, 3)] + [(dp, flip(z, k) * 2 + c) for k in (1, 2, 3)]
        peers.append((dp, z * 2 + 1 - c))
        barrier = pltpu.get_barrier_semaphore()
        for peer in peers:
            pl.semaphore_signal(barrier, inc=1, device_id=peer, device_id_type=MESH)
        spread = small_grad.reshape(256, 128)
        for name in ARRAYS:
            rows = FF // 32 if name == "down" else 16
            src = shards[name]
            per = src.shape[0] // rows
            spread[0 : src.shape[0]] = src[...].astype(f32)
            for j in range(per):
                piece = spread[pl.ds(j, rows, stride=per), :].astype(bf16)
                half, at = divmod(128 * j, FH)
                held = weights["up%d" % half] if name == "up" else weights[name]
                held[dp, z, c, :, (at if name == "up" else 128 * j) : (at if name == "up" else 128 * j) + 128] = piece
        weights["qkv"][dp, z, c, :, 3 * D :] = shards["small"][...]
        gathers = {n: Gather(weights[n], gsend.at[i], grecv.at[i], pos) for i, n in enumerate(HELD)}
        gathers["qkv"] = EagerGather(weights["qkv"], gsend.at[0], grecv.at[0], pos)
        pl.semaphore_wait(barrier, len(peers))
        gathers["qkv"].start()
        gathers["qkv"].start_column()
        for name in HELD[1:]:
            gathers[name].start_z()
        rest = [gathers[n] for n in HELD[1:]]

    cs[...] = jnp.zeros(cs.shape, bf16)
    sg = seg[...]
    st = jnp.zeros(sg.shape, jnp.int32)
    for v in range(1, 4):
        count = jnp.sum((sg < v).astype(f32), axis=1, keepdims=True).astype(jnp.int32)
        st = jnp.where(sg == v, count, st)
    st = jnp.concatenate([st, jnp.zeros((R, SP - S), jnp.int32)], axis=1)
    start[...] = jnp.concatenate([st] * GROUP, axis=1).reshape(R, 1, GROUP * SP)
    for ref in (acc_up, acc_down, gbias, gsmall):
        ref[...] = jnp.zeros(ref.shape, f32)
    tok_copy.wait()

    def load_x(b):
        for i in range(RB):
            cs[SP * i : SP * i + S] = tokv[b * RB + i]
        return cs[...].astype(f32)

    def rows_of(b):
        return pl.ds(pl.multiple_of(b * M, 16), M)

    def norm_one(b, carry):
        rows = rows_of(b)
        xh1 = normalize(load_x(b))[0]
        high = xh1.astype(bf16)
        ACC[rows] = high
        GN[rows] = (xh1 - high.astype(f32)).astype(bf16)
        return carry

    if comm:
        gathers["qkv"].start_onward()
        lax.fori_loop(0, NB // 2, norm_one, 0)
        gathers["qkv"].start_core()
        for g in rest:
            g.start_column()
        lax.fori_loop(NB // 2, NB, norm_one, 0)
        gathers["qkv"].finish()
        wq = weights["qkv"]
        for s in range(32):
            piece = wq[s // 8, (s % 8) // 2, s % 2, :, 3 * D :].astype(f32)
            smallv[s // 4 : s // 4 + 1, 128 * (s % 4) : 128 * (s % 4) + 128] = piece[0:1]
        for s in range(0, 32, 2):
            two = [wq[s // 8, (s % 8) // 2, i, :, 3 * D : 3 * D + 64].astype(f32)[1:2] for i in (0, 1)]
            bias[:, 64 * s : 64 * s + 128] = jnp.concatenate(two, axis=1)
    else:
        lax.fori_loop(0, NB, norm_one, 0)
        bias[...] = shards["small"][8:12].astype(f32).reshape(1, FF)
        smallv[...] = shards["small"][0:8].astype(f32)

    def w_qkv(a, b):
        return weights["qkv"][:, :, :, :, a:b].reshape(D, b - a)

    sm = smallv[...]
    g1, c1, bq, bv, bo, g2, c2, bd = [sm[i : i + 1] for i in range(8)]
    scale = HEAD_DIM ** (-0.5)
    bkv = jnp.concatenate([jnp.zeros_like(bv), bv], axis=1)
    lane = lax.broadcasted_iota(jnp.int32, (1, GW), 1)
    head_mask = [(lane // HEAD_DIM == j).astype(f32).astype(bf16) for j in range(GROUP)]
    low_half = lax.broadcasted_iota(jnp.int32, (1, 128), 1) < HEAD_DIM

    def stack(v):
        return jnp.concatenate([v * head_mask[j] for j in range(GROUP)], axis=0)

    def project(b, carry):
        rows = rows_of(b)
        fl = ((ACC[rows].astype(f32) + GN[rows].astype(f32)) * g1 + c1).astype(bf16)
        QKV[rows, 0:D] = ((nn(fl, w_qkv(0, D)) + bq) * scale).astype(bf16)
        QKV[rows, D : 3 * D] = (nn(fl, w_qkv(D, 3 * D)) + bkv).astype(bf16)
        return carry

    kidx = lax.broadcasted_iota(jnp.int32, (SP, GROUP * SP), 0)
    qidx = lax.broadcasted_iota(jnp.int32, (1, GROUP * SP), 1)
    qidx = qidx - SP * sum((qidx >= SP * j).astype(jnp.int32) for j in range(1, GROUP))

    NG = HEADS // GROUP
    TILES = GW // 128

    def attend(i, carry):
        rs = [i * UNROLL + u for u in range(UNROLL)]
        rows = [pl.ds(pl.multiple_of(r * SP, 16), SP) for r in rs]
        todo = [(u, g) for u in range(UNROLL) for g in range(NG)]
        allowed = [(kidx >= start[r]) & (kidx <= qidx) for r in rs]
        ss = [nt(QKV[rows[u], D + GW * g : D + GW * g + GW], stack(QKV[rows[u], GW * g : GW * g + GW])) for u, g in todo]
        ss = [jnp.where(allowed[u], s, MASKED_SCORE) for (u, g), s in zip(todo, ss)]
        es = [jnp.exp(s - jnp.max(s, axis=0, keepdims=True)) for s in ss]
        ps = [(e * (1.0 / col_sum(e))).astype(bf16) for e in es]
        pqs = [p.T for p in ps]
        for (u, g), p in zip(todo, ps):
            PT[2 * rs[u] + g] = p
        for (u, g), pq in zip(todo, pqs):
            for t in range(TILES):
                at = GW * g + 128 * t
                o = nn(pq[2 * SP * t : 2 * SP * t + 2 * SP], QKV[rows[u], 2 * D + at : 2 * D + at + 128])
                ATT[rows[u], at : at + 128] = jnp.where(low_half, o[0:SP], o[SP : 2 * SP]).astype(bf16)
        return carry

    def feed(half, b, carry):
        step = half * NB + b
        slot = step % 2
        rows = rows_of(b)
        mid = load_x(b) + nn(ATT[rows], weights["out"][...].reshape(D, D)) + bo
        cot_copy(step, slot).wait()
        for i in range(RB):
            cs[SP * i : SP * i + S] = cbuf[slot, i]
        if half:

            @pl.when(b > 0)
            def _():
                out_copy(b - 1, 1 - slot).wait()

            @pl.when(b + 1 < NB)
            def _():
                cot_copy(b + 1, 1 - slot).start()

        else:
            cot_copy(b + 1, 1 - slot).start()
        xh2, r2 = normalize(mid)
        second = (xh2 * g2 + c2).astype(bf16)
        branch = cs[...]
        acts, gps = [], []
        for j in range(4):
            w_up = weights["up%d" % half][:, :, :, :, j * FC : (j + 1) * FC].reshape(D, FC)
            w_down = weights["down"][2 * half + j // 2, 2 * (j % 2) : 2 * (j % 2) + 2].reshape(FC, D)
            cols = slice((4 * half + j) * FC, (4 * half + j + 1) * FC)
            pre = nn(second, w_up) + bias[:, cols]
            s = 0.5 * jnp.tanh((0.5 * GELU_SLOPE) * pre) + 0.5
            a = pre * s
            gp = (nt(branch, w_down) * (s + GELU_SLOPE * a * (1.0 - s))).astype(bf16)
            gbias[:, cols] += col_sum(gp.astype(f32))
            acts.append(a.astype(bf16))
            gps.append(gp)
        act, gp = jnp.concatenate(acts, axis=1), jnp.concatenate(gps, axis=1)
        w_down = weights["down"][2 * half : 2 * half + 2].reshape(FH, D)
        w_up = weights["up%d" % half][...].reshape(D, FH)
        grown = nn(act, w_down)
        gn2 = nt(gp, w_up)
        acc_down[...] += tn(act, branch).reshape(acc_down.shape)
        acc_up[...] += tn(second, gp).reshape(acc_up.shape)
        if not half:
            ACC[rows] = grown.astype(bf16)
            GN[rows] = gn2.astype(bf16)
            return carry
        res = (mid + bd + ACC[rows].astype(f32) + grown).astype(bf16)
        for i in range(RB):
            cbuf[slot, i] = res[SP * i : SP * i + S]
        out_copy(b, slot).start()
        gn2 = gn2 + GN[rows].astype(f32)
        h = gn2 * g2
        up = branch.astype(f32)
        gm = up + r2 * (h - lane_mean(h) - xh2 * lane_mean(h * xh2))
        GM[rows] = gm.astype(bf16)
        gsmall[4:5] += col_sum(gm.astype(bf16).astype(f32))
        gsmall[5:6] += col_sum(gn2 * xh2)
        gsmall[6:7] += col_sum(gn2)
        gsmall[7:8] += col_sum(up)
        return carry

    def out_grad():
        return tn(ATT[...], GM[...]).reshape(4, 4, 2, D // 32, D)

    def attended_grad(b, carry):
        rows = rows_of(b)
        ATT[rows] = nt(GM[rows], weights["out"][...].reshape(D, D)).astype(bf16)
        return carry

    def attend_back(i, carry):
        rs = [i * UNROLL + u for u in range(UNROLL)]
        rows = [pl.ds(pl.multiple_of(r * SP, 16), SP) for r in rs]
        todo = [(u, g) for u in range(UNROLL) for g in range(NG)]
        gos = [stack(ATT[rows[u], GW * g : GW * g + GW]) for u, g in todo]
        dps = [nt(QKV[rows[u], 2 * D + GW * g : 2 * D + GW * g + GW], go) for (u, g), go in zip(todo, gos)]
        qs = [stack(QKV[rows[u], GW * g : GW * g + GW]) for u, g in todo]
        lows = [PT[2 * rs[u] + g] for u, g in todo]
        gvs = [nn(low, go).astype(bf16) for low, go in zip(lows, gos)]
        dss = []
        for low, dpr in zip(lows, dps):
            p = low.astype(f32)
            dss.append((p * (dpr - col_sum(p * dpr))).astype(bf16))
        gks = [nn(ds, q).astype(bf16) for ds, q in zip(dss, qs)]
        gqs = []
        for (u, g), ds in zip(todo, dss):
            dsq = ds.T
            for t in range(TILES):
                at = D + GW * g + 128 * t
                o = nn(dsq[2 * SP * t : 2 * SP * t + 2 * SP], QKV[rows[u], at : at + 128])
                gqs.append((jnp.where(low_half, o[0:SP], o[SP : 2 * SP]) * scale).astype(bf16))
        for r in rs:
            x = normalize(tokv[r].astype(f32))[0]
            FL[pl.ds(pl.multiple_of(r * SP, 16), S)] = (x * g1 + c1).astype(bf16)
        for n, (u, g) in enumerate(todo):
            for t in range(TILES):
                QKV[rows[u], GW * g + 128 * t : GW * g + 128 * t + 128] = gqs[n * TILES + t]
            QKV[rows[u], D + GW * g : D + GW * g + GW] = gks[n]
            QKV[rows[u], 2 * D + GW * g : 2 * D + GW * g + GW] = gvs[n]
        return carry

    def input_grad(b, carry):
        rows = rows_of(b)
        gq = QKV[rows]
        gn1 = nt(gq, w_qkv(0, 3 * D))
        xh1, r1 = normalize(load_x(b))
        h = gn1 * g1
        res = (GM[rows].astype(f32) + r1 * (h - lane_mean(h) - xh1 * lane_mean(h * xh1))).astype(bf16)
        for i in range(RB):
            tokv[b * RB + i] = res[SP * i : SP * i + S]
        gsmall[0:1] += col_sum(gn1 * xh1)
        gsmall[1:2] += col_sum(gn1)
        gsmall[2:3] += col_sum(gq[:, 0:D].astype(f32))
        gsmall[3:4] += col_sum(gq[:, 2 * D : 3 * D].astype(f32))
        return carry

    def loop(a, b, f):
        lax.fori_loop(a, b, f, 0)

    def qkv_grad(j):
        return tn(FL[...], QKV[:, j * D : (j + 1) * D]).reshape(4, 4, 2, D // 32, D)

    NA = R // UNROLL

    def staged(count, step, events):
        at = 0
        for when, act in events:
            if when > at:
                loop(at, when, step)
                at = when
            act()
        loop(at, count, step)

    def when(plan):
        return [(NA * at // 18, act) for at, act in plan]

    if not comm:
        loop(0, NB, project)
        loop(0, NA, attend)
        for half in (0, 1):
            loop(0, NB, functools.partial(feed, half))
            grads["up"][:, :, :, :, half * FH : (half + 1) * FH] = acc_up[...]
            grads["down"][2 * half : 2 * half + 2] = acc_down[...]
            if not half:
                acc_up[...] = jnp.zeros(acc_up.shape, f32)
                acc_down[...] = jnp.zeros(acc_down.shape, f32)
        grads["out"][...] = out_grad()
        loop(0, NB, attended_grad)
        out_copy(NB - 1, (2 * NB - 1) % 2).wait()
        loop(0, NA, attend_back)
        for j in range(3):
            grads["qkv"][:, :, :, :, j * D : (j + 1) * D] = qkv_grad(j)
        loop(0, NB, input_grad)
        tok_back = pltpu.make_async_copy(tokv, gtok, tsem)
        tok_back.start()
        tok_back.wait()
        grads["small"][0:8] = gsmall[...]
        grads["small"][8:12] = gbias[...].reshape(4, D)
        return

    loop(0, NB, project)
    scat = {}
    for i, name in enumerate(HELD[1:]):
        scat[name] = Scatter(weights[name], weights[name].at[:, :, 1 - c], from_core[name], from_dp[name], from_z[name],
                             ssend.at[i], srecv.at[i], pos)
    for j in range(3):
        cols = pl.ds(j * D, D)
        own = acc_up.at[:, :, j // 2, :, pl.ds(j % 2 * D, D)]
        away = GN.at[pl.ds(j * D // 2, D // 2)].reshape(4, 4, D // 32, D)
        scat[j] = Scatter(own, away, from_core["qkv"].at[:, :, :, cols], from_dp["qkv"].at[:, :, :, :, cols],
                          from_z["qkv"].at[:, :, cols], ssend.at[4 + j], srecv.at[4 + j], pos)
    small = Scatter(small_grad, small_half, from_core["small"], from_dp["small"], from_z["small"],
                    ssend.at[7], srecv.at[7], pos, f32)
    out_s, up0_s, down_s, up1_s = (scat[n] for n in HELD[1:])
    later = rest[3:]

    staged(NA, attend, when([
        (9, lambda: [g.start_onward() for g in rest[:3]]), (18, lambda: [g.start_core() for g in rest[:3]]),
    ]))
    for g in rest[:3]:
        g.finish()
    staged(NB, functools.partial(feed, 0), [(1, rest[3].start_onward), (3, rest[3].start_core)])
    rest[3].finish()
    weights["up0"][...] = acc_up[...].astype(bf16)
    weights["down"][0:2] = acc_down[...].astype(bf16)
    up0_s.start_core()
    acc_up[...] = jnp.zeros(acc_up.shape, f32)
    acc_down[...] = jnp.zeros(acc_down.shape, f32)
    staged(NB, functools.partial(feed, 1), [(1, up0_s.start_dp), (3, up0_s.start_onward), (5, up0_s.start_z)])
    weights["down"][2:4] = acc_down[...].astype(bf16)
    down_s.start_core()
    weights["up1"][...] = acc_up[...].astype(bf16)
    up1_s.start_core()
    grad = out_grad().astype(bf16)
    loop(0, NB, attended_grad)
    weights["out"][...] = grad
    out_s.start_core()
    out_copy(NB - 1, (2 * NB - 1) % 2).wait()
    staged(NA, attend_back, when([
        (4, down_s.start_dp), (8, up1_s.start_dp), (12, out_s.start_dp), (16, down_s.start_onward),
    ]))
    for j in range(3):
        scat[j].start_core(qkv_grad(j))
        if j:
            scat[j - 1].start_dp()
        if j == 1:
            up1_s.start_onward()
            out_s.start_onward()
    staged(NB, input_grad, [
        (1, scat[2].start_dp), (2, down_s.start_z), (3, scat[0].start_onward), (3, up1_s.start_z),
        (4, scat[1].start_onward), (4, out_s.start_z), (5, scat[2].start_onward), (5, scat[0].start_z),
    ])
    tok_back = pltpu.make_async_copy(tokv, gtok, tsem)
    tok_back.start()
    gs = small_grad
    for s in range(32):
        row = s // 4
        gs[s // 8, (s % 8) // 2, s % 2, 0:1, 0:128] = gsmall[row : row + 1, 128 * (s % 4) : 128 * (s % 4) + 128]
        two = gbias[:, 128 * (s // 2) : 128 * (s // 2) + 128]
        gs[s // 8, (s % 8) // 2, s % 2, 1:2, 0:64] = two[:, 64 * (s % 2) : 64 * (s % 2) + 64]
    small_half[...] = small_grad[:, :, 1 - c]
    small.start_core()
    scat[1].start_z()
    scat[2].start_z()

    def give(name, total, first=0):
        rows, cols = total.shape
        per = shares[name].shape[0] // rows
        for j in range(cols // 128):
            shares[name][pl.ds(first + j, rows, stride=per), :] = total[:, 128 * j : 128 * j + 128]

    small.start_dp()
    give("up", up0_s.finish())
    give("down", down_s.finish())
    give("up", up1_s.finish(), FH // 128)
    give("out", out_s.finish())
    small.start_onward()
    small.start_z()
    for j in range(3):
        give("qkv", scat[j].finish(), j * D // 128)
    shares["small"][...] = small.finish()
    tok_back.wait()


def block_call(comm, tokens, segments, cotangent, pieces, FF):
    R, S, D = tokens.shape
    SP = (S + 15) // 16 * 16
    T, M = R * SP, ROW_BLOCK * SP
    V, dma = pltpu.VMEM, pltpu.SemaphoreType.DMA
    vm, hbm = pl.BlockSpec(memory_space=pltpu.VMEM), pl.BlockSpec(memory_space=pl.ANY)
    rows = {"qkv": (16, 3 * D), "out": (16, D), "up": (16, FF), "down": (FF // 32, D)}
    out_shape = [jax.ShapeDtypeStruct(tokens.shape, bf16)] * 2
    if comm:
        out_shape += [jax.ShapeDtypeStruct(p.shape, f32) for p in pieces[:4]]
        out_shape += [jax.ShapeDtypeStruct((8, 128), f32)]
    else:
        out_shape += [jax.ShapeDtypeStruct((4, 4, 2) + rows[n], f32) for n in ARRAYS]
        out_shape += [jax.ShapeDtypeStruct((12, D), f32)]
    scratch = [
        V((R, S, D), bf16), V((2, ROW_BLOCK, S, D), bf16), V((M, D), bf16),
        V((T, 3 * D), bf16), V((T, D), bf16), V((2 * R, SP, GROUP * SP), bf16), V((T, D), bf16),
        V((T, D), bf16), V((T, D), bf16), V((R, 1, GROUP * SP), jnp.int32), V((1, FF), f32), V((8, D), f32),
        V((1, FF), f32), V((8, D), f32), V((4, 4, 2, 16, FF // 2), f32),
        V((2, 4, 2, FF // 32, D), f32), dma, dma((2,)), dma((2,)),
    ]
    if comm:
        small = (8, 128)
        held = {"qkv": (16, 3 * D), "out": (16, D), "up0": (16, FF // 2), "down": (FF // 32, D), "up1": (16, FF // 2)}
        scratch += [V((4, 4, 2) + (held[n] if n != "qkv" else (16, 3 * D + 128)), bf16) for n in HELD]
        scratch += [V((4, 4, 2) + small, f32)]
        for lead in ((4, 4), (3, 2, 2), (3,)):
            scratch += [V(lead + held[n], bf16) for n in HELD] + [V(lead + small, f32)]
        scratch += [dma((5, 21)), dma((5, 21)), dma((8, 10)), dma((8, 10))]
    params = dict(vmem_limit_bytes=63480 * 1000)
    if comm:
        params.update(collective_id=1, has_side_effects=True)
    return pl.pallas_call(
        functools.partial(block_kernel, comm, R, S, SP, D, FF),
        out_shape=out_shape,
        in_specs=[hbm, vm, hbm] + [vm] * 5,
        out_specs=[hbm, hbm] + [vm] * 5,
        scratch_shapes=scratch,
        compiler_params=pltpu.CompilerParams(**params),
    )(tokens, segments, cotangent, *pieces)


def hand_over_kernel(parts, *refs):
    n = len(parts)
    given, kept, held, into, away = refs[: n + 1], refs[n + 1 : 2 * n + 3], refs[2 * n + 3 : 3 * n + 3], refs[-2], refs[-1]
    spans, slot = [], 0
    for i, count in enumerate(parts):
        size = given[i].shape[0] // count
        for p in range(count):
            rows = pl.ds(p * size, size)
            first = pltpu.make_async_copy(given[i].at[rows], held[i].at[rows], into.at[slot])
            spans.append((first, pltpu.make_async_copy(held[i].at[rows], kept[i].at[rows], away.at[slot])))
            slot += 1
    for first, _ in spans:
        first.start()
    kept[n][...] = given[n][0:1]
    kept[n + 1][...] = given[n][1:2, 0 : kept[n + 1].shape[1]]
    for first, second in spans:
        first.wait()
        second.start()
    for _, second in spans:
        second.wait()


def hand_over(arrays, tile, count):
    n = len(arrays)
    parts = [6 if a.ndim == 3 else 1 for a in arrays]
    hbm, vm = pl.BlockSpec(memory_space=pl.ANY), pl.BlockSpec(memory_space=pltpu.VMEM)
    shapes = [jax.ShapeDtypeStruct(a.shape, a.dtype) for a in arrays]
    shapes += [jax.ShapeDtypeStruct((1, tile.shape[1]), f32), jax.ShapeDtypeStruct((1, count), f32)]
    sems = pltpu.SemaphoreType.DMA((sum(parts),))
    return pl.pallas_call(
        functools.partial(hand_over_kernel, parts), out_shape=shapes, in_specs=[hbm] * n + [vm],
        out_specs=[hbm] * n + [vm, vm], scratch_shapes=[pltpu.VMEM(a.shape, a.dtype) for a in arrays] + [sems, sems],
        compiler_params=pltpu.CompilerParams(vmem_limit_bytes=60 * 1024 * 1024),
    )(*arrays, tile)


def body(sizes, tokens, segment_ids, qkv_weight, out_weight, up_weight, up_bias, down_weight, small_params, cotangent):
    D = tokens.shape[2]
    n = sizes[0] * sizes[1]
    FF = up_bias.shape[0] * n
    flats = (qkv_weight, out_weight, up_weight, down_weight)
    if sizes == (4, 8):
        tile = jnp.pad(jnp.concatenate([small_params, up_bias]), (0, 16 * 128 - 192)).reshape(16, 128)
        o = block_call(True, tokens, segment_ids, cotangent, [f.reshape(-1, 128) for f in flats] + [tile], FF)
        o = hand_over(o[:6], o[6], up_bias.shape[0])
        shares = [v.reshape(-1) for v in o[2:]]
        return (o[0], o[1], shares[0], shares[1], shares[2], shares[5], shares[3], shares[4])
    axes = ("dp", "fsdp")

    def gather(v):
        return lax.all_gather(v, axes, axis=0, tiled=True)

    def scatter(v):
        return lax.psum_scatter(v.reshape(-1), axes, scatter_dimension=0, tiled=True)

    packed = lax.all_gather(jnp.concatenate([small_params, up_bias]), axes, axis=0, tiled=False)
    count = small_params.shape[0]
    tile = jnp.concatenate([packed[:, :count].reshape(8, D), packed[:, count:].reshape(4, D)])
    whole = [gather(f) for f in flats]
    shapes = ((4, 4, 2, 16, 3 * D), (4, 4, 2, 16, D), (4, 4, 2, 16, FF), (4, 4, 2, FF // 32, D))
    o = block_call(False, tokens, segment_ids, cotangent, [w.reshape(s) for w, s in zip(whole, shapes)] + [tile], FF)
    return (o[0], o[1], scatter(o[2]), scatter(o[3]), scatter(o[4]), scatter(o[6][8:12]), scatter(o[5]), scatter(o[6][0:8]))


def solution(mesh):
    rows, flat = P(("dp", "fsdp"), None, None), P(("dp", "fsdp"))
    in_specs = (rows, P(("dp", "fsdp"), None), flat, flat, flat, flat, flat, flat, rows)
    out_specs = (rows, rows, flat, flat, flat, flat, flat, flat)
    sizes = (mesh.shape["dp"], mesh.shape["fsdp"])
    return jax.shard_map(functools.partial(body, sizes), mesh=mesh, in_specs=in_specs, out_specs=out_specs, check_vma=False)
```

```python
import functools

import jax
import jax.numpy as jnp
from jax import lax
from jax.experimental import pallas as pl
from jax.experimental.pallas import tpu as pltpu
from jax.sharding import PartitionSpec as P

bf16 = jnp.bfloat16
f32 = jnp.float32
HEADS = 8
HEAD_DIM = 64
GROUP = 4
NORM_EPS = 1e-05
GELU_SLOPE = 1.702
MASKED_SCORE = -1e30
MESH = pl.DeviceIdType.MESH
ROW_BLOCK = 6
UNROLL = 3
GATHER = (2, 3, 1, 3, 0, 3, 9)
REDUCE = (3, 2, 3, 6, 7, 9, 11, 11)
REDUCE_QKV = (1, 2, 3, 3, 4, 4, 5, 5, 6)
ARRAYS = ("qkv", "out", "up", "down")
HELD = ("qkv", "out", "up0", "down", "up1")


def nn(a, b):
    return lax.dot_general(a, b, (((1,), (0,)), ((), ())), preferred_element_type=f32)


def nt(a, b):
    return lax.dot_general(a, b, (((1,), (1,)), ((), ())), preferred_element_type=f32)


def tn(a, b):
    return lax.dot_general(a, b, (((0,), (0,)), ((), ())), preferred_element_type=f32)


def col_sum(v):
    return jnp.sum(v, axis=0, keepdims=True)


def lane_mean(v):
    return jnp.sum(v, axis=-1, keepdims=True) * (1.0 / v.shape[-1])


def normalize(x):
    xc = x - lane_mean(x)
    inv = lax.rsqrt(lane_mean(xc * xc) + NORM_EPS)
    return xc * inv, inv


def flip(index, bits):
    low, high = index % 2, index // 2
    if bits & 1:
        low = 1 - low
    if bits & 2:
        high = 1 - high
    return high * 2 + low


class Gather:
    def __init__(self, buf, send, recv, pos):
        self.buf, self.send, self.recv = buf, send, recv
        self.dp, self.z, self.c = pos

    def copy(self, index, slot, device):
        ref = self.buf.at[index]
        return pltpu.make_async_remote_copy(
            src_ref=ref, dst_ref=ref, send_sem=self.send.at[slot], recv_sem=self.recv.at[slot],
            device_id=device, device_id_type=MESH)

    def along_z(self, k, mine=True):
        z = self.z if mine else flip(self.z, k)
        return self.copy((self.dp, z, self.c), k - 1, (self.dp, flip(self.z, k) * 2 + self.c))

    def column(self, bit, mine=True):
        dp = self.dp if mine else flip(self.dp, bit)
        return self.copy((dp, slice(None), self.c), 2 + bit, (flip(self.dp, bit), self.z * 2 + self.c))

    def onward(self, bit, mine=True):
        other = 3 - bit
        dp = flip(self.dp, other) if mine else flip(self.dp, 3)
        half = pl.ds(0, 2) if bit == 2 else pl.ds(2, 2)
        return self.copy((dp, half, self.c), 4 + bit, (flip(self.dp, bit), self.z * 2 + self.c))

    def to_core(self, mine=True):
        c = self.c if mine else 1 - self.c
        return self.copy((slice(None), slice(None), c), 7, (self.dp, self.z * 2 + 1 - self.c))

    def start_z(self):
        for k in (1, 2, 3):
            self.along_z(k).start()

    def start_column(self):
        for k in (1, 2, 3):
            self.along_z(k, False).wait_recv()
        for bit in (1, 2):
            self.column(bit).start()

    def start_onward(self):
        for bit in (1, 2):
            self.column(3 - bit, False).wait_recv()
            self.onward(bit).start()

    def start_core(self):
        for bit in (1, 2):
            self.onward(bit, False).wait_recv()
        self.to_core().start()

    def finish(self):
        self.to_core(False).wait_recv()
        for k in (1, 2, 3):
            self.along_z(k).wait_send()
        for bit in (1, 2):
            self.column(bit).wait_send()
            self.onward(bit).wait_send()
        self.to_core().wait_send()


class EagerGather(Gather):
    def shard(self, k, bit, mine=True):
        dp = self.dp if mine else flip(self.dp, bit)
        return self.copy((dp, flip(self.z, k), self.c), 2 + bit * 4 + k - 1, (flip(self.dp, bit), self.z * 2 + self.c))

    def forward(self, k, mine=True):
        bit = 2 - k % 2
        dp = flip(self.dp, 3 - bit) if mine else flip(self.dp, 3)
        return self.copy((dp, flip(self.z, k), self.c), 13 + k, (flip(self.dp, bit), self.z * 2 + self.c))

    def core_column(self, bits, mine=True):
        c = self.c if mine else 1 - self.c
        return self.copy((flip(self.dp, bits), slice(None), c), 17 + bits, (self.dp, self.z * 2 + 1 - self.c))

    def start(self):
        for k in (1, 2, 3):
            self.along_z(k).start()
        for bit in (1, 2):
            self.shard(0, bit).start()

    def start_column(self, between=lambda: None):
        for k in (1, 2, 3):
            self.along_z(k, False).wait_recv()
            for bit in (1, 2):
                self.shard(k, bit).start()
            if k == 1:
                between()
        self.core_column(0).start()

    def start_onward(self):
        for k in (0, 1, 2, 3):
            bit = 2 - k % 2
            self.shard(k, 3 - bit, False).wait_recv()
            self.forward(k).start()
        for k in (0, 1, 2, 3):
            bit = 2 - k % 2
            self.shard(k, bit, False).wait_recv()
        for bit in (1, 2):
            self.core_column(bit).start()

    def start_core(self):
        for k in (0, 1, 2, 3):
            self.forward(k, False).wait_recv()
        self.core_column(3).start()

    def finish(self):
        for bits in (0, 1, 2, 3):
            self.core_column(bits, False).wait_recv()
        for k in (1, 2, 3):
            self.along_z(k).wait_send()
        for k in (0, 1, 2, 3):
            for bit in (1, 2):
                self.shard(k, bit).wait_send()
            self.forward(k).wait_send()
            self.core_column(k).wait_send()


class Scatter:
    def __init__(self, grad, half, from_core, from_dp, from_z, send, recv, pos, dtype=bf16):
        self.grad, self.half, self.from_core, self.from_dp, self.from_z = grad, half, from_core, from_dp, from_z
        self.send, self.recv, self.dtype = send, recv, dtype
        self.dp, self.z, self.c = pos

    def copy(self, src, dst, slot, device):
        return pltpu.make_async_remote_copy(
            src_ref=src, dst_ref=dst, send_sem=self.send.at[slot], recv_sem=self.recv.at[slot],
            device_id=device, device_id_type=MESH)

    def core_copy(self):
        return self.copy(self.half, self.from_core, 0, (self.dp, self.z * 2 + 1 - self.c))

    def dp_copy(self, step, bit, onward):
        half = bit - 1 if step == 0 else 2 - bit
        dp = flip(self.dp, 3 if onward else bit)
        return self.copy(self.from_core.at[dp, pl.ds(2 * half, 2)], self.from_dp.at[2 * step + onward, bit - 1],
                         1 + 2 * (2 * step + onward) + bit - 1, (flip(self.dp, bit), self.z * 2 + self.c))

    def z_copy(self, k):
        return self.copy(self.from_core.at[self.dp, flip(self.z, k)], self.from_z.at[k - 1], 6 + k,
                         (self.dp, flip(self.z, k) * 2 + self.c))

    def start_core(self, whole=None):
        if whole is not None:
            zero, one = whole[:, :, 0], whole[:, :, 1]
            self.grad[...] = jnp.where(self.c == 0, zero, one)
            self.half[...] = jnp.where(self.c == 0, one, zero).astype(self.dtype)
        self.core_copy().start()

    def own_part(self, *index):
        return self.grad[self.own(*index)].astype(f32)

    def own(self, *index):
        return index if len(self.grad.shape) == 4 else index + (slice(None),) * (2 - len(index)) + (self.c,)

    def start_dp(self):
        self.core_copy().wait_recv()
        for bit in (1, 2):
            for onward in (1, 0):
                at = (flip(self.dp, 3 if onward else bit), pl.ds(2 * (bit - 1), 2))
                self.from_core[at] = (self.own_part(*at) + self.from_core[at].astype(f32)).astype(self.dtype)
                self.dp_copy(0, bit, onward).start()

    def start_onward(self):
        for bit in (1, 2):
            first = 3 - bit
            self.dp_copy(0, first, 1).wait_recv()
            at = (flip(self.dp, bit), pl.ds(2 * (first - 1), 2))
            total = self.own_part(*at) + self.from_core[at].astype(f32)
            self.from_core[at] = (total + self.from_dp[1, first - 1].astype(f32)).astype(self.dtype)
            self.dp_copy(1, bit, 0).start()

    def start_z(self):
        for bit in (1, 2):
            self.dp_copy(0, bit, 0).wait_recv()
            self.dp_copy(1, bit, 0).wait_recv()
        for half in (0, 1):
            at = (self.dp, pl.ds(2 * half, 2))
            total = self.own_part(*at) + self.from_core[at].astype(f32)
            total += self.from_dp[0, half].astype(f32) + self.from_dp[2, 1 - half].astype(f32)
            self.grad[self.own(*at)] = total.astype(self.grad.dtype)
            self.from_core[at] = total.astype(self.dtype)
        for k in (1, 2, 3):
            self.z_copy(k).start()

    def finish(self):
        for k in (1, 2, 3):
            self.z_copy(k).wait_recv()
        total = self.own_part(self.dp, self.z)
        for k in (1, 2, 3):
            total += self.from_z[k - 1].astype(f32)
        self.core_copy().wait_send()
        for bit in (1, 2):
            self.dp_copy(0, bit, 0).wait_send()
            self.dp_copy(0, bit, 1).wait_send()
            self.dp_copy(1, bit, 0).wait_send()
        for k in (1, 2, 3):
            self.z_copy(k).wait_send()
        return total


class SmallScatter:
    def __init__(self, grad, from_fsdp, from_dp, send, recv, pos):
        self.grad, self.from_fsdp, self.from_dp, self.send, self.recv = grad, from_fsdp, from_dp, send, recv
        self.dp, self.z, self.c = pos

    def copy(self, src, dst, slot, device):
        return pltpu.make_async_remote_copy(
            src_ref=src, dst_ref=dst, send_sem=self.send.at[slot], recv_sem=self.recv.at[slot],
            device_id=device, device_id_type=MESH)

    def first(self, k):
        z, c = flip(self.z, k // 2), self.c if k % 2 == 0 else 1 - self.c
        return self.copy(self.grad.at[:, z, c], self.from_fsdp.at[k - 1], k - 1, (self.dp, z * 2 + c))

    def second(self, k):
        dp = flip(self.dp, k)
        return self.copy(self.grad.at[dp, self.z, self.c], self.from_dp.at[k - 1], 6 + k, (dp, self.z * 2 + self.c))

    def start(self):
        for k in range(1, 8):
            self.first(k).start()

    def pass_on(self):
        for k in range(1, 8):
            self.first(k).wait_recv()
        total = self.grad[:, self.z, self.c]
        for k in range(1, 8):
            total += self.from_fsdp[k - 1]
        self.grad[:, self.z, self.c] = total
        for k in (1, 2, 3):
            self.second(k).start()

    def finish(self):
        for k in (1, 2, 3):
            self.second(k).wait_recv()
        total = self.grad[self.dp, self.z, self.c] + self.from_dp[0] + self.from_dp[1] + self.from_dp[2]
        for k in range(1, 8):
            self.first(k).wait_send()
        for k in (1, 2, 3):
            self.second(k).wait_send()
        return total


def block_kernel(comm, R, S, SP, D, FF, *refs):
    RB, M, NB, FC, FH, NA = ROW_BLOCK, ROW_BLOCK * SP, R // ROW_BLOCK, FF // 8, FF // 2, R // UNROLL
    GW = GROUP * HEAD_DIM
    refs = list(refs)

    def take(n):
        out = refs[:n]
        del refs[:n]
        return out

    tok, seg, cot = take(3)
    shards = dict(zip(ARRAYS + ("small",), take(5)))
    out, gtok = take(2)
    if comm:
        shares = dict(zip(ARRAYS + ("small",), take(5)))
    else:
        grads = dict(zip(ARRAYS + ("small",), take(5)))
    tokv, cbuf, cs, QKV, ATT, PT, GM, ACC, GN, start, bias, smallv, gbias, gsmall = take(14)
    FL = ACC
    acc_up, acc_down = take(2)
    tsem, csem, osem = take(3)
    if comm:
        weights = dict(zip(HELD, take(5)))
        small_grad = take(1)[0]
        from_core, from_dp, from_z = (dict(zip(HELD, take(5))) for _ in range(3))
        small_fsdp, small_dp, gsend, grecv, ssend, srecv = take(6)
    else:
        weights = {k: shards[k] for k in ARRAYS if k != "up"}
        for i in (0, 1):
            weights["up%d" % i] = shards["up"].at[:, :, :, :, pl.ds(i * (FF // 2), FF // 2)]

    def loop(a, b, f):
        lax.fori_loop(a, b, f, 0)

    def staged(count, step, events):
        def body(i, carry):
            for at, act in events:
                if at < count:
                    pl.when(i == at)(act)
            return step(i, carry)

        loop(0, count, body)
        for at, act in events:
            if at >= count:
                act()

    def each(things, act):
        for thing in things:
            act(thing)

    def when(plan):
        return [(NA * at // 18, act) for at, act in plan]

    tok_copy = pltpu.make_async_copy(tok, tokv, tsem)
    tok_copy.start()

    def cot_copy(b, slot):
        return pltpu.make_async_copy(cot.at[pl.ds(b % NB * RB, RB)], cbuf.at[slot], csem.at[slot])

    def out_copy(b, slot):
        return pltpu.make_async_copy(cbuf.at[slot], out.at[pl.ds(b * RB, RB)], osem.at[slot])

    cot_copy(0, 0).start()
    if comm:
        dp = lax.axis_index("dp")
        fs = lax.axis_index("fsdp")
        pos = (dp, fs // 2, fs % 2)
        z, c = pos[1], pos[2]
        peers = [(flip(dp, k), fs) for k in (1, 2, 3)] + [(dp, flip(z, k) * 2 + c) for k in (1, 2, 3)]
        peers += [(dp, flip(z, k) * 2 + 1 - c) for k in (0, 1, 2, 3)]
        barrier = pltpu.get_barrier_semaphore()
        for peer in peers:
            pl.semaphore_signal(barrier, inc=1, device_id=peer, device_id_type=MESH)
        spread = small_grad.reshape(256, 128)
        for name in ARRAYS:
            rows = FF // 32 if name == "down" else 16
            src = shards[name]
            per = src.shape[0] // rows
            spread[0 : src.shape[0]] = src[...].astype(f32)
            for j in range(per):
                piece = spread[pl.ds(j, rows, stride=per), :].astype(bf16)
                half, at = divmod(128 * j, FH)
                held = weights["up%d" % half] if name == "up" else weights[name]
                held[dp, z, c, :, (at if name == "up" else 128 * j) : (at if name == "up" else 128 * j) + 128] = piece
        weights["qkv"][dp, z, c, :, 3 * D :] = shards["small"][...]
        gathers = {n: Gather(weights[n], gsend.at[i], grecv.at[i], pos) for i, n in enumerate(HELD)}
        gathers["qkv"] = EagerGather(weights["qkv"], gsend.at[0], grecv.at[0], pos)
        pl.semaphore_wait(barrier, len(peers))
        gathers["qkv"].start()
        rest = [gathers[n] for n in HELD[1:]]
        gathers["qkv"].start_column(lambda: each(rest[:2], Gather.start_z))

    cs[...] = jnp.zeros(cs.shape, bf16)
    sg = seg[...]
    st = jnp.zeros(sg.shape, jnp.int32)
    for v in range(1, 4):
        count = jnp.sum((sg < v).astype(f32), axis=1, keepdims=True).astype(jnp.int32)
        st = jnp.where(sg == v, count, st)
    st = jnp.concatenate([st, jnp.zeros((R, SP - S), jnp.int32)], axis=1)
    start[...] = jnp.concatenate([st] * GROUP, axis=1).reshape(R, 1, GROUP * SP)
    for ref in (acc_up, acc_down, gbias, gsmall):
        ref[...] = jnp.zeros(ref.shape, f32)
    tok_copy.wait()

    def load_x(b):
        for i in range(RB):
            cs[SP * i : SP * i + S] = tokv[b * RB + i]
        return cs[...].astype(f32)

    def rows_of(b):
        return pl.ds(pl.multiple_of(b * M, 16), M)

    def norm_one(b, carry):
        rows = rows_of(b)
        xh1 = normalize(load_x(b))[0]
        high = xh1.astype(bf16)
        ACC[rows] = high
        GN[rows] = (xh1 - high.astype(f32)).astype(bf16)
        return carry

    if comm:
        staged(NB, norm_one, [
            (0, gathers["qkv"].start_onward), (0, rest[2].start_z), (GATHER[0], lambda: each(rest[:2], Gather.start_column)),
            (GATHER[1], gathers["qkv"].start_core),
        ])
        gathers["qkv"].finish()
        wq = weights["qkv"]
        for s in range(32):
            piece = wq[s // 8, (s % 8) // 2, s % 2, :, 3 * D :].astype(f32)
            smallv[s // 4 : s // 4 + 1, 128 * (s % 4) : 128 * (s % 4) + 128] = piece[0:1]
        for s in range(0, 32, 2):
            two = [wq[s // 8, (s % 8) // 2, i, :, 3 * D : 3 * D + 64].astype(f32)[1:2] for i in (0, 1)]
            bias[:, 64 * s : 64 * s + 128] = jnp.concatenate(two, axis=1)
    else:
        lax.fori_loop(0, NB, norm_one, 0)
        bias[...] = shards["small"][8:12].astype(f32).reshape(1, FF)
        smallv[...] = shards["small"][0:8].astype(f32)

    def w_qkv(a, b):
        return weights["qkv"][:, :, :, :, a:b].reshape(D, b - a)

    sm = smallv[...]
    g1, c1, bq, bv, bo, g2, c2, bd = [sm[i : i + 1] for i in range(8)]
    scale = HEAD_DIM ** (-0.5)
    bkv = jnp.concatenate([jnp.zeros_like(bv), bv], axis=1)
    lane = lax.broadcasted_iota(jnp.int32, (1, GW), 1)
    head_mask = [(lane // HEAD_DIM == j).astype(f32).astype(bf16) for j in range(GROUP)]
    low_half = lax.broadcasted_iota(jnp.int32, (1, 128), 1) < HEAD_DIM

    def stack(v):
        return jnp.concatenate([v * head_mask[j] for j in range(GROUP)], axis=0)

    def project(b, carry):
        rows = rows_of(b)
        fl = ((ACC[rows].astype(f32) + GN[rows].astype(f32)) * g1 + c1).astype(bf16)
        QKV[rows, 0:D] = ((nn(fl, w_qkv(0, D)) + bq) * scale).astype(bf16)
        QKV[rows, D : 3 * D] = (nn(fl, w_qkv(D, 3 * D)) + bkv).astype(bf16)
        return carry

    kidx = lax.broadcasted_iota(jnp.int32, (SP, GROUP * SP), 0)
    qidx = lax.broadcasted_iota(jnp.int32, (1, GROUP * SP), 1)
    qidx = qidx - SP * sum((qidx >= SP * j).astype(jnp.int32) for j in range(1, GROUP))

    NG = HEADS // GROUP
    TILES = GW // 128

    def attend(i, carry):
        rs = [i * UNROLL + u for u in range(UNROLL)]
        rows = [pl.ds(pl.multiple_of(r * SP, 16), SP) for r in rs]
        todo = [(u, g) for u in range(UNROLL) for g in range(NG)]
        allowed = [(kidx >= start[r]) & (kidx <= qidx) for r in rs]
        ss = [nt(QKV[rows[u], D + GW * g : D + GW * g + GW], stack(QKV[rows[u], GW * g : GW * g + GW])) for u, g in todo]
        ss = [jnp.where(allowed[u], s, MASKED_SCORE) for (u, g), s in zip(todo, ss)]
        es = [jnp.exp(s - jnp.max(s, axis=0, keepdims=True)) for s in ss]
        ps = [(e * (1.0 / col_sum(e))).astype(bf16) for e in es]
        pqs = [p.T for p in ps]
        for (u, g), p in zip(todo, ps):
            PT[2 * rs[u] + g] = p
        for (u, g), pq in zip(todo, pqs):
            for t in range(TILES):
                at = GW * g + 128 * t
                o = nn(pq[2 * SP * t : 2 * SP * t + 2 * SP], QKV[rows[u], 2 * D + at : 2 * D + at + 128])
                ATT[rows[u], at : at + 128] = jnp.where(low_half, o[0:SP], o[SP : 2 * SP]).astype(bf16)
        return carry

    def feed(half, b, carry):
        step = half * NB + b
        slot = step % 2
        rows = rows_of(b)
        mid = load_x(b) + nn(ATT[rows], weights["out"][...].reshape(D, D)) + bo
        cot_copy(step, slot).wait()
        for i in range(RB):
            cs[SP * i : SP * i + S] = cbuf[slot, i]
        if half:

            @pl.when(b > 0)
            def _():
                out_copy(b - 1, 1 - slot).wait()

            @pl.when(b + 1 < NB)
            def _():
                cot_copy(b + 1, 1 - slot).start()

        else:
            cot_copy(b + 1, 1 - slot).start()
        xh2, r2 = normalize(mid)
        second = (xh2 * g2 + c2).astype(bf16)
        branch = cs[...]
        acts, gps = [], []
        for j in range(4):
            w_up = weights["up%d" % half][:, :, :, :, j * FC : (j + 1) * FC].reshape(D, FC)
            w_down = weights["down"][2 * half + j // 2, 2 * (j % 2) : 2 * (j % 2) + 2].reshape(FC, D)
            cols = slice((4 * half + j) * FC, (4 * half + j + 1) * FC)
            pre = nn(second, w_up) + bias[:, cols]
            s = 0.5 * jnp.tanh((0.5 * GELU_SLOPE) * pre) + 0.5
            a = pre * s
            gp = (nt(branch, w_down) * (s + GELU_SLOPE * a * (1.0 - s))).astype(bf16)
            gbias[:, cols] += col_sum(gp.astype(f32))
            acts.append(a.astype(bf16))
            gps.append(gp)
        act, gp = jnp.concatenate(acts, axis=1), jnp.concatenate(gps, axis=1)
        w_down = weights["down"][2 * half : 2 * half + 2].reshape(FH, D)
        w_up = weights["up%d" % half][...].reshape(D, FH)
        grown = nn(act, w_down)
        gn2 = nt(gp, w_up)
        acc_down[...] += tn(act, branch).reshape(acc_down.shape)
        acc_up[...] += tn(second, gp).reshape(acc_up.shape)
        if not half:
            ACC[rows] = grown.astype(bf16)
            GN[rows] = gn2.astype(bf16)
            return carry
        res = (mid + bd + ACC[rows].astype(f32) + grown).astype(bf16)
        for i in range(RB):
            cbuf[slot, i] = res[SP * i : SP * i + S]
        out_copy(b, slot).start()
        gn2 = gn2 + GN[rows].astype(f32)
        h = gn2 * g2
        up = branch.astype(f32)
        gm = up + r2 * (h - lane_mean(h) - xh2 * lane_mean(h * xh2))
        GM[rows] = gm.astype(bf16)
        gsmall[4:5] += col_sum(gm.astype(bf16).astype(f32))
        gsmall[5:6] += col_sum(gn2 * xh2)
        gsmall[6:7] += col_sum(gn2)
        gsmall[7:8] += col_sum(up)
        return carry

    def out_grad():
        return tn(ATT[...], GM[...]).reshape(4, 4, 2, D // 32, D)

    def attended_grad(b, carry):
        rows = rows_of(b)
        ATT[rows] = nt(GM[rows], weights["out"][...].reshape(D, D)).astype(bf16)
        return carry

    def attend_back(i, carry):
        rs = [i * UNROLL + u for u in range(UNROLL)]
        rows = [pl.ds(pl.multiple_of(r * SP, 16), SP) for r in rs]
        todo = [(u, g) for u in range(UNROLL) for g in range(NG)]
        gos = [stack(ATT[rows[u], GW * g : GW * g + GW]) for u, g in todo]
        dps = [nt(QKV[rows[u], 2 * D + GW * g : 2 * D + GW * g + GW], go) for (u, g), go in zip(todo, gos)]
        qs = [stack(QKV[rows[u], GW * g : GW * g + GW]) for u, g in todo]
        lows = [PT[2 * rs[u] + g] for u, g in todo]
        gvs = [nn(low, go).astype(bf16) for low, go in zip(lows, gos)]
        dss = []
        for low, dpr in zip(lows, dps):
            p = low.astype(f32)
            dss.append((p * (dpr - col_sum(p * dpr))).astype(bf16))
        gks = [nn(ds, q).astype(bf16) for ds, q in zip(dss, qs)]
        gqs = []
        for (u, g), ds in zip(todo, dss):
            dsq = ds.T
            for t in range(TILES):
                at = D + GW * g + 128 * t
                o = nn(dsq[2 * SP * t : 2 * SP * t + 2 * SP], QKV[rows[u], at : at + 128])
                gqs.append((jnp.where(low_half, o[0:SP], o[SP : 2 * SP]) * scale).astype(bf16))
        for r in rs:
            x = normalize(tokv[r].astype(f32))[0]
            FL[pl.ds(pl.multiple_of(r * SP, 16), S)] = (x * g1 + c1).astype(bf16)
        for n, (u, g) in enumerate(todo):
            for t in range(TILES):
                QKV[rows[u], GW * g + 128 * t : GW * g + 128 * t + 128] = gqs[n * TILES + t]
            QKV[rows[u], D + GW * g : D + GW * g + GW] = gks[n]
            QKV[rows[u], 2 * D + GW * g : 2 * D + GW * g + GW] = gvs[n]
        return carry

    def input_grad(b, carry):
        rows = rows_of(b)
        gq = QKV[rows]
        gn1 = nt(gq, w_qkv(0, 3 * D))
        xh1, r1 = normalize(load_x(b))
        h = gn1 * g1
        res = (GM[rows].astype(f32) + r1 * (h - lane_mean(h) - xh1 * lane_mean(h * xh1))).astype(bf16)
        for i in range(RB):
            tokv[b * RB + i] = res[SP * i : SP * i + S]
        gsmall[0:1] += col_sum(gn1 * xh1)
        gsmall[1:2] += col_sum(gn1)
        gsmall[2:3] += col_sum(gq[:, 0:D].astype(f32))
        gsmall[3:4] += col_sum(gq[:, 2 * D : 3 * D].astype(f32))
        return carry

    def qkv_grad(j):
        return tn(FL[...], QKV[:, j * D : (j + 1) * D]).reshape(4, 4, 2, D // 32, D)

    if not comm:
        loop(0, NB, project)
        loop(0, NA, attend)
        for half in (0, 1):
            loop(0, NB, functools.partial(feed, half))
            grads["up"][:, :, :, :, half * FH : (half + 1) * FH] = acc_up[...]
            grads["down"][2 * half : 2 * half + 2] = acc_down[...]
            if not half:
                acc_up[...] = jnp.zeros(acc_up.shape, f32)
                acc_down[...] = jnp.zeros(acc_down.shape, f32)
        grads["out"][...] = out_grad()
        loop(0, NB, attended_grad)
        out_copy(NB - 1, (2 * NB - 1) % 2).wait()
        loop(0, NA, attend_back)
        for j in range(3):
            grads["qkv"][:, :, :, :, j * D : (j + 1) * D] = qkv_grad(j)
        loop(0, NB, input_grad)
        tok_back = pltpu.make_async_copy(tokv, gtok, tsem)
        tok_back.start()
        tok_back.wait()
        grads["small"][0:8] = gsmall[...]
        grads["small"][8:12] = gbias[...].reshape(4, D)
        return

    staged(NB, project, [
        (GATHER[2], lambda: each(rest[:2], Gather.start_onward)), (GATHER[3], rest[2].start_column), (GATHER[3], rest[3].start_z),
    ])
    scat = {}
    for i, name in enumerate(HELD[1:]):
        scat[name] = Scatter(weights[name], weights[name].at[:, :, 1 - c], from_core[name], from_dp[name], from_z[name],
                             ssend.at[i], srecv.at[i], pos)
    for j in range(3):
        cols = pl.ds(j * D, D)
        own = acc_up.at[:, :, j // 2, :, pl.ds(j % 2 * D, D)]
        away = GN.at[pl.ds(j * D // 2, D // 2)].reshape(4, 4, D // 32, D)
        scat[j] = Scatter(own, away, from_core["qkv"].at[:, :, :, cols], from_dp["qkv"].at[:, :, :, :, cols],
                          from_z["qkv"].at[:, :, cols], ssend.at[4 + j], srecv.at[4 + j], pos)
    small = SmallScatter(small_grad, small_fsdp, small_dp, ssend.at[7], srecv.at[7], pos)
    out_s, up0_s, down_s, up1_s = (scat[n] for n in HELD[1:])
    staged(NA, attend, [
        (GATHER[4], lambda: each(rest[:2], Gather.start_core)), (GATHER[5], rest[2].start_onward),
        (GATHER[6], rest[2].start_core),
    ])
    for g in rest[:3]:
        g.finish()
    staged(NB, functools.partial(feed, 0), [(0, rest[3].start_column), (2, rest[3].start_onward), (3, rest[3].start_core)])
    rest[3].finish()
    weights["up0"][...] = acc_up[...].astype(bf16)
    weights["down"][0:2] = acc_down[...].astype(bf16)
    up0_s.start_core()
    acc_up[...] = jnp.zeros(acc_up.shape, f32)
    acc_down[...] = jnp.zeros(acc_down.shape, f32)
    staged(NB, functools.partial(feed, 1), [(1, up0_s.start_dp), (3, up0_s.start_onward), (5, up0_s.start_z)])
    weights["down"][2:4] = acc_down[...].astype(bf16)
    down_s.start_core()
    weights["up1"][...] = acc_up[...].astype(bf16)
    grad = out_grad().astype(bf16)
    loop(0, NB, attended_grad)
    weights["out"][...] = grad
    out_copy(NB - 1, (2 * NB - 1) % 2).wait()
    names = (down_s.start_dp, up1_s.start_core, out_s.start_core, up1_s.start_dp, out_s.start_dp,
             down_s.start_onward, up1_s.start_onward, out_s.start_onward)
    staged(NA, attend_back, list(zip(REDUCE, names)))
    for j in range(3):
        scat[j].start_core(qkv_grad(j))
        if j:
            scat[j - 1].start_dp()
    names = (scat[2].start_dp, down_s.start_z, scat[0].start_onward, up1_s.start_z, scat[1].start_onward, out_s.start_z,
             scat[2].start_onward, scat[0].start_z, scat[1].start_z)
    staged(NB, input_grad, list(zip(REDUCE_QKV, names)))
    tok_back = pltpu.make_async_copy(tokv, gtok, tsem)
    tok_back.start()
    gs = small_grad
    for s in range(32):
        row = s // 4
        gs[s // 8, (s % 8) // 2, s % 2, 0:1, 0:128] = gsmall[row : row + 1, 128 * (s % 4) : 128 * (s % 4) + 128]
        two = gbias[:, 128 * (s // 2) : 128 * (s // 2) + 128]
        gs[s // 8, (s % 8) // 2, s % 2, 1:2, 0:64] = two[:, 64 * (s % 2) : 64 * (s % 2) + 64]
    small.start()
    scat[2].start_z()

    def give(name, total, first=0):
        rows, cols = total.shape
        per = shares[name].shape[0] // rows
        for j in range(cols // 128):
            shares[name][pl.ds(first + j, rows, stride=per), :] = total[:, 128 * j : 128 * j + 128]

    give("up", up0_s.finish())
    give("down", down_s.finish())
    give("up", up1_s.finish(), FH // 128)
    give("out", out_s.finish())
    small.pass_on()
    for j in range(3):
        give("qkv", scat[j].finish(), j * D // 128)
    shares["small"][...] = small.finish()
    tok_back.wait()


def block_call(comm, tokens, segments, cotangent, pieces, FF):
    R, S, D = tokens.shape
    SP = (S + 15) // 16 * 16
    T, M = R * SP, ROW_BLOCK * SP
    V, dma = pltpu.VMEM, pltpu.SemaphoreType.DMA
    vm, hbm = pl.BlockSpec(memory_space=pltpu.VMEM), pl.BlockSpec(memory_space=pl.ANY)
    rows = {"qkv": (16, 3 * D), "out": (16, D), "up": (16, FF), "down": (FF // 32, D)}
    out_shape = [jax.ShapeDtypeStruct(tokens.shape, bf16)] * 2
    if comm:
        out_shape += [jax.ShapeDtypeStruct(p.shape, f32) for p in pieces[:4]]
        out_shape += [jax.ShapeDtypeStruct((8, 128), f32)]
    else:
        out_shape += [jax.ShapeDtypeStruct((4, 4, 2) + rows[n], f32) for n in ARRAYS]
        out_shape += [jax.ShapeDtypeStruct((12, D), f32)]
    scratch = [
        V((R, S, D), bf16), V((2, ROW_BLOCK, S, D), bf16), V((M, D), bf16),
        V((T, 3 * D), bf16), V((T, D), bf16), V((2 * R, SP, GROUP * SP), bf16), V((T, D), bf16),
        V((T, D), bf16), V((T, D), bf16), V((R, 1, GROUP * SP), jnp.int32), V((1, FF), f32), V((8, D), f32),
        V((1, FF), f32), V((8, D), f32), V((4, 4, 2, 16, FF // 2), f32),
        V((2, 4, 2, FF // 32, D), f32), dma, dma((2,)), dma((2,)),
    ]
    if comm:
        small = (8, 128)
        held = {"qkv": (16, 3 * D), "out": (16, D), "up0": (16, FF // 2), "down": (FF // 32, D), "up1": (16, FF // 2)}
        scratch += [V((4, 4, 2) + (held[n] if n != "qkv" else (16, 3 * D + 128)), bf16) for n in HELD]
        scratch += [V((4, 4, 2) + small, f32)]
        for lead in ((4, 4), (3, 2, 2), (3,)):
            scratch += [V(lead + held[n], bf16) for n in HELD]
        scratch += [V((7, 4) + small, f32), V((3,) + small, f32), dma((5, 21)), dma((5, 21)), dma((8, 10)), dma((8, 10))]
    params = dict(vmem_limit_bytes=63480 * 1000)
    if comm:
        params.update(collective_id=1, has_side_effects=True)
    return pl.pallas_call(
        functools.partial(block_kernel, comm, R, S, SP, D, FF),
        out_shape=out_shape,
        in_specs=[hbm, vm, hbm] + [vm] * 5,
        out_specs=[hbm, hbm] + [vm] * 5,
        scratch_shapes=scratch,
        compiler_params=pltpu.CompilerParams(**params),
    )(tokens, segments, cotangent, *pieces)


def hand_over_kernel(parts, *refs):
    n = len(parts)
    given, kept, held, into, away = refs[: n + 1], refs[n + 1 : 2 * n + 3], refs[2 * n + 3 : 3 * n + 3], refs[-2], refs[-1]
    spans, slot = [], 0
    for i, count in enumerate(parts):
        size = given[i].shape[0] // count
        for p in range(count):
            rows = pl.ds(p * size, size)
            first = pltpu.make_async_copy(given[i].at[rows], held[i].at[rows], into.at[slot])
            spans.append((first, pltpu.make_async_copy(held[i].at[rows], kept[i].at[rows], away.at[slot])))
            slot += 1
    for first, _ in spans:
        first.start()
    kept[n][...] = given[n][0:1]
    kept[n + 1][...] = given[n][1:2, 0 : kept[n + 1].shape[1]]
    for first, second in spans:
        first.wait()
        second.start()
    for _, second in spans:
        second.wait()


def hand_over(arrays, tile, count):
    n = len(arrays)
    parts = [6 if a.ndim == 3 else 1 for a in arrays]
    hbm, vm = pl.BlockSpec(memory_space=pl.ANY), pl.BlockSpec(memory_space=pltpu.VMEM)
    shapes = [jax.ShapeDtypeStruct(a.shape, a.dtype) for a in arrays]
    shapes += [jax.ShapeDtypeStruct((1, tile.shape[1]), f32), jax.ShapeDtypeStruct((1, count), f32)]
    sems = pltpu.SemaphoreType.DMA((sum(parts),))
    return pl.pallas_call(
        functools.partial(hand_over_kernel, parts), out_shape=shapes, in_specs=[hbm] * n + [vm],
        out_specs=[hbm] * n + [vm, vm], scratch_shapes=[pltpu.VMEM(a.shape, a.dtype) for a in arrays] + [sems, sems],
        compiler_params=pltpu.CompilerParams(vmem_limit_bytes=60 * 1024 * 1024),
    )(*arrays, tile)


def body(sizes, tokens, segment_ids, qkv_weight, out_weight, up_weight, up_bias, down_weight, small_params, cotangent):
    D = tokens.shape[2]
    n = sizes[0] * sizes[1]
    FF = up_bias.shape[0] * n
    flats = (qkv_weight, out_weight, up_weight, down_weight)
    if sizes == (4, 8):
        tile = jnp.pad(jnp.concatenate([small_params, up_bias]), (0, 16 * 128 - 192)).reshape(16, 128)
        o = block_call(True, tokens, segment_ids, cotangent, [f.reshape(-1, 128) for f in flats] + [tile], FF)
        o = hand_over(o[:6], o[6], up_bias.shape[0])
        shares = [v.reshape(-1) for v in o[2:]]
        return (o[0], o[1], shares[0], shares[1], shares[2], shares[5], shares[3], shares[4])
    axes = ("dp", "fsdp")

    def gather(v):
        return lax.all_gather(v, axes, axis=0, tiled=True)

    def scatter(v):
        return lax.psum_scatter(v.reshape(-1), axes, scatter_dimension=0, tiled=True)

    packed = lax.all_gather(jnp.concatenate([small_params, up_bias]), axes, axis=0, tiled=False)
    count = small_params.shape[0]
    tile = jnp.concatenate([packed[:, :count].reshape(8, D), packed[:, count:].reshape(4, D)])
    whole = [gather(f) for f in flats]
    shapes = ((4, 4, 2, 16, 3 * D), (4, 4, 2, 16, D), (4, 4, 2, 16, FF), (4, 4, 2, FF // 32, D))
    o = block_call(False, tokens, segment_ids, cotangent, [w.reshape(s) for w, s in zip(whole, shapes)] + [tile], FF)
    return (o[0], o[1], scatter(o[2]), scatter(o[3]), scatter(o[4]), scatter(o[6][8:12]), scatter(o[5]), scatter(o[6][0:8]))


def solution(mesh):
    rows, flat = P(("dp", "fsdp"), None, None), P(("dp", "fsdp"))
    in_specs = (rows, P(("dp", "fsdp"), None), flat, flat, flat, flat, flat, flat, rows)
    out_specs = (rows, rows, flat, flat, flat, flat, flat, flat)
    sizes = (mesh.shape["dp"], mesh.shape["fsdp"])
    return jax.shard_map(functools.partial(body, sizes), mesh=mesh, in_specs=in_specs, out_specs=out_specs, check_vma=False)
```

```python
import functools

import jax
import jax.numpy as jnp
from jax import lax
from jax.experimental import pallas as pl
from jax.experimental.pallas import tpu as pltpu
from jax.sharding import PartitionSpec as P

bf16 = jnp.bfloat16
f32 = jnp.float32
HEADS = 8
HEAD_DIM = 64
GROUP = 4
NORM_EPS = 1e-05
GELU_SLOPE = 1.702
MASKED_SCORE = -1e30
MESH = pl.DeviceIdType.MESH
ROW_BLOCK = 6
UNROLL = 4
GATHER = (2, 3, 2, 4, 2, 8)
FEED = (2, 4, 2, 4, 5)
REDUCE = (0, 2, 3, 5, 7, 8)
REDUCE_QKV = (0, 1, 1, 2, 2, 3, 4, 4, 5)
ARRAYS = ("qkv", "out", "up", "down")
HELD = ("qkv", "out", "up0", "down0", "up1", "down1")
PART = {"down0": 0, "down1": 1}


def nn(a, b):
    return lax.dot_general(a, b, (((1,), (0,)), ((), ())), preferred_element_type=f32)


def nt(a, b):
    return lax.dot_general(a, b, (((1,), (1,)), ((), ())), preferred_element_type=f32)


def tn(a, b):
    return lax.dot_general(a, b, (((0,), (0,)), ((), ())), preferred_element_type=f32)


def col_sum(v):
    return jnp.sum(v, axis=0, keepdims=True)


def lane_mean(v):
    return jnp.sum(v, axis=-1, keepdims=True) * (1.0 / v.shape[-1])


def normalize(x):
    xc = x - lane_mean(x)
    inv = lax.rsqrt(lane_mean(xc * xc) + NORM_EPS)
    return xc * inv, inv


def flip(index, bits):
    low, high = index % 2, index // 2
    if bits & 1:
        low = 1 - low
    if bits & 2:
        high = 1 - high
    return high * 2 + low


class Gather:
    def __init__(self, buf, send, recv, pos, part=None):
        self.buf, self.send, self.recv, self.part = buf, send, recv, part
        self.dp, self.z, self.c = pos
        self.nz = buf.shape[1]

    def only(self, z, act):
        if self.part is None:
            act()
        else:
            pl.when(z // 2 == self.part)(act)

    def copy(self, index, slot, device):
        ref = self.buf.at[index]
        return pltpu.make_async_remote_copy(
            src_ref=ref, dst_ref=ref, send_sem=self.send.at[slot], recv_sem=self.recv.at[slot],
            device_id=device, device_id_type=MESH)

    def along_z(self, k, mine=True):
        z = self.z if mine else flip(self.z, k)
        return self.copy((self.dp, z % self.nz, self.c), k - 1, (self.dp, flip(self.z, k) * 2 + self.c))

    def column(self, bit, mine=True):
        dp = self.dp if mine else flip(self.dp, bit)
        return self.copy((dp, slice(None), self.c), 2 + bit, (flip(self.dp, bit), self.z * 2 + self.c))

    def onward(self, bit, mine=True):
        other = 3 - bit
        dp = flip(self.dp, other) if mine else flip(self.dp, 3)
        half = pl.ds(0 if bit == 2 else self.nz // 2, self.nz // 2)
        return self.copy((dp, half, self.c), 4 + bit, (flip(self.dp, bit), self.z * 2 + self.c))

    def to_core(self, mine=True):
        c = self.c if mine else 1 - self.c
        return self.copy((slice(None), slice(None), c), 7, (self.dp, self.z * 2 + 1 - self.c))

    def start_z(self):
        for k in (1, 2, 3):
            self.only(self.z, self.along_z(k).start)

    def start_column(self):
        for k in (1, 2, 3):
            self.only(flip(self.z, k), self.along_z(k, False).wait_recv)
        for bit in (1, 2):
            self.column(bit).start()

    def start_onward(self):
        for bit in (1, 2):
            self.column(3 - bit, False).wait_recv()
            self.onward(bit).start()

    def start_core(self):
        for bit in (1, 2):
            self.onward(bit, False).wait_recv()
        self.to_core().start()

    def finish(self):
        self.to_core(False).wait_recv()
        for k in (1, 2, 3):
            self.only(self.z, self.along_z(k).wait_send)
        for bit in (1, 2):
            self.column(bit).wait_send()
            self.onward(bit).wait_send()
        self.to_core().wait_send()


class EagerGather(Gather):
    def shard(self, k, bit, mine=True):
        dp = self.dp if mine else flip(self.dp, bit)
        return self.copy((dp, flip(self.z, k), self.c), 2 + bit * 4 + k - 1, (flip(self.dp, bit), self.z * 2 + self.c))

    def forward(self, k, mine=True):
        bit = 2 - k % 2
        dp = flip(self.dp, 3 - bit) if mine else flip(self.dp, 3)
        return self.copy((dp, flip(self.z, k), self.c), 13 + k, (flip(self.dp, bit), self.z * 2 + self.c))

    def core_column(self, bits, mine=True):
        c = self.c if mine else 1 - self.c
        return self.copy((flip(self.dp, bits), slice(None), c), 17 + bits, (self.dp, self.z * 2 + 1 - self.c))

    def start(self):
        for k in (1, 2, 3):
            self.along_z(k).start()
        for bit in (1, 2):
            self.shard(0, bit).start()

    def start_column(self, between=lambda: None):
        for k in (1, 2, 3):
            self.along_z(k, False).wait_recv()
            for bit in (1, 2):
                self.shard(k, bit).start()
            if k == 1:
                between()
        self.core_column(0).start()

    def start_onward(self):
        for k in (0, 1, 2, 3):
            bit = 2 - k % 2
            self.shard(k, 3 - bit, False).wait_recv()
            self.forward(k).start()
        for k in (0, 1, 2, 3):
            bit = 2 - k % 2
            self.shard(k, bit, False).wait_recv()
        for bit in (1, 2):
            self.core_column(bit).start()

    def start_core(self):
        for k in (0, 1, 2, 3):
            self.forward(k, False).wait_recv()
        self.core_column(3).start()

    def finish(self):
        for bits in (0, 1, 2, 3):
            self.core_column(bits, False).wait_recv()
        for k in (1, 2, 3):
            self.along_z(k).wait_send()
        for k in (0, 1, 2, 3):
            for bit in (1, 2):
                self.shard(k, bit).wait_send()
            self.forward(k).wait_send()
            self.core_column(k).wait_send()


class Scatter:
    def __init__(self, grad, half, from_core, from_dp, from_z, send, recv, pos, part=None):
        self.part, self.nz, self.dtype = part, from_core.shape[1], bf16
        self.grad, self.half, self.from_core, self.from_dp, self.from_z = grad, half, from_core, from_dp, from_z
        self.send, self.recv = send, recv
        self.dp, self.z, self.c = pos

    def copy(self, src, dst, slot, device):
        return pltpu.make_async_remote_copy(
            src_ref=src, dst_ref=dst, send_sem=self.send.at[slot], recv_sem=self.recv.at[slot],
            device_id=device, device_id_type=MESH)

    def only(self, z, act):
        if self.part is None:
            act()
        else:
            pl.when(z // 2 == self.part)(act)

    def half_of(self, half):
        return pl.ds(half * self.nz // 2, self.nz // 2)

    def core_copy(self):
        return self.copy(self.half, self.from_core, 0, (self.dp, self.z * 2 + 1 - self.c))

    def dp_copy(self, step, bit, onward):
        half = bit - 1 if step == 0 else 2 - bit
        dp = flip(self.dp, 3 if onward else bit)
        return self.copy(self.from_core.at[dp, self.half_of(half)], self.from_dp.at[2 * step + onward, bit - 1],
                         1 + 2 * (2 * step + onward) + bit - 1, (flip(self.dp, bit), self.z * 2 + self.c))

    def z_copy(self, k):
        return self.copy(self.from_core.at[self.dp, flip(self.z, k) % self.nz], self.from_z.at[k - 1], 6 + k,
                         (self.dp, flip(self.z, k) * 2 + self.c))

    def start_core(self, whole=None):
        if whole is not None:
            zero, one = whole[:, :, 0], whole[:, :, 1]
            self.grad[...] = jnp.where(self.c == 0, zero, one)
            self.half[...] = jnp.where(self.c == 0, one, zero).astype(self.dtype)
        self.core_copy().start()

    def own_part(self, *index):
        return self.grad[self.own(*index)].astype(f32)

    def own(self, *index):
        return index if len(self.grad.shape) == 4 else index + (slice(None),) * (2 - len(index)) + (self.c,)

    def start_dp(self):
        self.core_copy().wait_recv()
        for bit in (1, 2):
            for onward in (1, 0):
                at = (flip(self.dp, 3 if onward else bit), self.half_of(bit - 1))
                self.from_core[at] = (self.own_part(*at) + self.from_core[at].astype(f32)).astype(self.dtype)
                self.dp_copy(0, bit, onward).start()

    def start_onward(self):
        for bit in (1, 2):
            first = 3 - bit
            self.dp_copy(0, first, 1).wait_recv()
            at = (flip(self.dp, bit), self.half_of(first - 1))
            total = self.own_part(*at) + self.from_core[at].astype(f32)
            self.from_core[at] = (total + self.from_dp[1, first - 1].astype(f32)).astype(self.dtype)
            self.dp_copy(1, bit, 0).start()

    def start_z(self):
        for bit in (1, 2):
            self.dp_copy(0, bit, 0).wait_recv()
            self.dp_copy(1, bit, 0).wait_recv()
        for half in (0, 1):
            at = (self.dp, self.half_of(half))
            total = self.own_part(*at) + self.from_core[at].astype(f32)
            total += self.from_dp[0, half].astype(f32) + self.from_dp[2, 1 - half].astype(f32)
            self.grad[self.own(*at)] = total.astype(self.grad.dtype)
            self.from_core[at] = total.astype(self.dtype)
        for k in (1, 2, 3):
            self.only(flip(self.z, k), self.z_copy(k).start)

    def finish(self, use):
        def whole():
            for k in (1, 2, 3):
                self.z_copy(k).wait_recv()
            total = self.own_part(self.dp, self.z % self.nz)
            for k in (1, 2, 3):
                total += self.from_z[k - 1].astype(f32)
            use(total)

        self.only(self.z, whole)
        self.core_copy().wait_send()
        for bit in (1, 2):
            self.dp_copy(0, bit, 0).wait_send()
            self.dp_copy(0, bit, 1).wait_send()
            self.dp_copy(1, bit, 0).wait_send()
        for k in (1, 2, 3):
            self.only(flip(self.z, k), self.z_copy(k).wait_send)


class SmallScatter:
    def __init__(self, grad, from_fsdp, from_dp, send, recv, pos):
        self.grad, self.from_fsdp, self.from_dp, self.send, self.recv = grad, from_fsdp, from_dp, send, recv
        self.dp, self.z, self.c = pos

    def copy(self, src, dst, slot, device):
        return pltpu.make_async_remote_copy(
            src_ref=src, dst_ref=dst, send_sem=self.send.at[slot], recv_sem=self.recv.at[slot],
            device_id=device, device_id_type=MESH)

    def first(self, k):
        z, c = flip(self.z, k // 2), self.c if k % 2 == 0 else 1 - self.c
        return self.copy(self.grad.at[:, z, c], self.from_fsdp.at[k - 1], k - 1, (self.dp, z * 2 + c))

    def second(self, k):
        dp = flip(self.dp, k)
        return self.copy(self.grad.at[dp, self.z, self.c], self.from_dp.at[k - 1], 6 + k, (dp, self.z * 2 + self.c))

    def start(self):
        for k in range(1, 8):
            self.first(k).start()

    def pass_on(self):
        for k in range(1, 8):
            self.first(k).wait_recv()
        total = self.grad[:, self.z, self.c]
        for k in range(1, 8):
            total += self.from_fsdp[k - 1]
        self.grad[:, self.z, self.c] = total
        for k in (1, 2, 3):
            self.second(k).start()

    def finish(self):
        for k in (1, 2, 3):
            self.second(k).wait_recv()
        total = self.grad[self.dp, self.z, self.c] + self.from_dp[0] + self.from_dp[1] + self.from_dp[2]
        for k in range(1, 8):
            self.first(k).wait_send()
        for k in (1, 2, 3):
            self.second(k).wait_send()
        return total


def block_kernel(comm, R, S, SP, D, FF, *refs):
    RB, M, NB, FC, FH, NA = ROW_BLOCK, ROW_BLOCK * SP, R // ROW_BLOCK, FF // 8, FF // 2, R // UNROLL
    GW = GROUP * HEAD_DIM
    refs = list(refs)

    def take(n):
        out = refs[:n]
        del refs[:n]
        return out

    tok, seg, cot = take(3)
    shards = dict(zip(ARRAYS + ("small",), take(5)))
    out, gtok = take(2)
    if comm:
        shares = dict(zip(ARRAYS + ("small",), take(5)))
    else:
        grads = dict(zip(ARRAYS + ("small",), take(5)))
    tokv, cbuf, cs, QKV, ATT, PT, GM, ACC, GN, start, bias, smallv, gbias, gsmall = take(14)
    FL = ACC
    acc_up, acc_down = take(2)
    tsem, csem, osem = take(3)
    if comm:
        weights = dict(zip(HELD, take(6)))
        small_grad = take(1)[0]
        from_core, from_dp, from_z = (dict(zip(HELD, take(6))) for _ in range(3))
        small_fsdp, small_dp, gsend, grecv, ssend, srecv = take(6)
    else:
        weights = shards

    def loop(a, b, f):
        lax.fori_loop(a, b, f, 0)

    def staged(count, step, events):
        def body(i, carry):
            for at, act in events:
                if at < count:
                    pl.when(i == at)(act)
            return step(i, carry)

        loop(0, count, body)
        for at, act in events:
            if at >= count:
                act()

    def each(things, act):
        for thing in things:
            act(thing)

    def when(plan):
        return [(NA * at // 18, act) for at, act in plan]

    tok_copy = pltpu.make_async_copy(tok, tokv, tsem)
    tok_copy.start()

    def cot_copy(b, slot):
        return pltpu.make_async_copy(cot.at[pl.ds(b % NB * RB, RB)], cbuf.at[slot], csem.at[slot])

    def out_copy(b, slot):
        return pltpu.make_async_copy(cbuf.at[slot], out.at[pl.ds(b * RB, RB)], osem.at[slot])

    cot_copy(0, 0).start()
    if comm:
        dp = lax.axis_index("dp")
        fs = lax.axis_index("fsdp")
        pos = (dp, fs // 2, fs % 2)
        z, c = pos[1], pos[2]
        peers = [(flip(dp, k), fs) for k in (1, 2, 3)] + [(dp, flip(z, k) * 2 + c) for k in (1, 2, 3)]
        peers += [(dp, flip(z, k) * 2 + 1 - c) for k in (0, 1, 2, 3)]
        barrier = pltpu.get_barrier_semaphore()
        for peer in peers:
            pl.semaphore_signal(barrier, inc=1, device_id=peer, device_id_type=MESH)
        spread = small_grad.reshape(256, 128)
        for name in ARRAYS:
            rows = FF // 32 if name == "down" else 16
            src = shards[name]
            per = src.shape[0] // rows
            spread[0 : src.shape[0]] = src[...].astype(f32)
            for j in range(per):
                piece = spread[pl.ds(j, rows, stride=per), :].astype(bf16)
                at = slice(128 * j, 128 * j + 128)
                if name == "up":
                    run, left = divmod(128 * j, 2 * FC)
                    half, left = divmod(left, FC)
                    weights["up%d" % half][dp, z, c, :, run * FC + left : run * FC + left + 128] = piece
                elif name == "down":
                    for part in (0, 1):

                        @pl.when(z // 2 == part)
                        def _(part=part, at=at, piece=piece):
                            weights["down%d" % part][dp, z % 2, c, :, at] = piece

                else:
                    weights[name][dp, z, c, :, at] = piece
        weights["qkv"][dp, z, c, :, 3 * D :] = shards["small"][...]
        gathers = {n: Gather(weights[n], gsend.at[i], grecv.at[i], pos, PART.get(n)) for i, n in enumerate(HELD)}
        gathers["qkv"] = EagerGather(weights["qkv"], gsend.at[0], grecv.at[0], pos)
        pl.semaphore_wait(barrier, len(peers))
        gathers["qkv"].start()
        rest = [gathers[n] for n in HELD[1:]]
        gathers["qkv"].start_column(lambda: each(rest[:2], Gather.start_z))

    cs[...] = jnp.zeros(cs.shape, bf16)
    sg = seg[...]
    st = jnp.zeros(sg.shape, jnp.int32)
    for v in range(1, 4):
        count = jnp.sum((sg < v).astype(f32), axis=1, keepdims=True).astype(jnp.int32)
        st = jnp.where(sg == v, count, st)
    st = jnp.concatenate([st, jnp.zeros((R, SP - S), jnp.int32)], axis=1)
    start[...] = jnp.concatenate([st] * GROUP, axis=1).reshape(R, 1, GROUP * SP)
    for ref in (acc_up, acc_down, gbias, gsmall):
        ref[...] = jnp.zeros(ref.shape, f32)
    tok_copy.wait()

    def load_x(b):
        for i in range(RB):
            cs[SP * i : SP * i + S] = tokv[b * RB + i]
        return cs[...].astype(f32)

    def rows_of(b):
        return pl.ds(pl.multiple_of(b * M, 16), M)

    def norm_one(b, carry):
        rows = rows_of(b)
        xh1 = normalize(load_x(b))[0]
        high = xh1.astype(bf16)
        ACC[rows] = high
        GN[rows] = (xh1 - high.astype(f32)).astype(bf16)
        return carry

    if comm:
        staged(NB, norm_one, [
            (0, gathers["qkv"].start_onward), (0, rest[2].start_z), (GATHER[0], lambda: each(rest[:3], Gather.start_column)),
            (GATHER[1], gathers["qkv"].start_core),
        ])
        gathers["qkv"].finish()
        wq = weights["qkv"]
        for s in range(32):
            piece = wq[s // 8, (s % 8) // 2, s % 2, :, 3 * D :].astype(f32)
            smallv[s // 4 : s // 4 + 1, 128 * (s % 4) : 128 * (s % 4) + 128] = piece[0:1]
        for s in range(0, 32, 2):
            two = [wq[s // 8, (s % 8) // 2, i, :, 3 * D : 3 * D + 64].astype(f32)[1:2] for i in (0, 1)]
            bias[:, 64 * s : 64 * s + 128] = jnp.concatenate(two, axis=1)
    else:
        lax.fori_loop(0, NB, norm_one, 0)
        bias[...] = shards["small"][8:12].astype(f32).reshape(1, FF)
        smallv[...] = shards["small"][0:8].astype(f32)

    def w_qkv(a, b):
        return weights["qkv"][:, :, :, :, a:b].reshape(D, b - a)

    sm = smallv[...]
    g1, c1, bq, bv, bo, g2, c2, bd = [sm[i : i + 1] for i in range(8)]
    scale = HEAD_DIM ** (-0.5)
    bkv = jnp.concatenate([jnp.zeros_like(bv), bv], axis=1)
    lane = lax.broadcasted_iota(jnp.int32, (1, GW), 1)
    head_mask = [(lane // HEAD_DIM == j).astype(f32).astype(bf16) for j in range(GROUP)]
    low_half = lax.broadcasted_iota(jnp.int32, (1, 128), 1) < HEAD_DIM

    def stack(v):
        return jnp.concatenate([v * head_mask[j] for j in range(GROUP)], axis=0)

    def project(b, carry):
        rows = rows_of(b)
        fl = ((ACC[rows].astype(f32) + GN[rows].astype(f32)) * g1 + c1).astype(bf16)
        QKV[rows, 0:D] = ((nn(fl, w_qkv(0, D)) + bq) * scale).astype(bf16)
        QKV[rows, D : 3 * D] = (nn(fl, w_qkv(D, 3 * D)) + bkv).astype(bf16)
        return carry

    kidx = lax.broadcasted_iota(jnp.int32, (SP, GROUP * SP), 0)
    qidx = lax.broadcasted_iota(jnp.int32, (1, GROUP * SP), 1)
    qidx = qidx - SP * sum((qidx >= SP * j).astype(jnp.int32) for j in range(1, GROUP))

    NG = HEADS // GROUP
    TILES = GW // 128

    def attend(i, carry):
        rs = [i * UNROLL + u for u in range(UNROLL)]
        rows = [pl.ds(pl.multiple_of(r * SP, 16), SP) for r in rs]
        todo = [(u, g) for u in range(UNROLL) for g in range(NG)]
        allowed = [(kidx >= start[r]) & (kidx <= qidx) for r in rs]
        ss = [nt(QKV[rows[u], D + GW * g : D + GW * g + GW], stack(QKV[rows[u], GW * g : GW * g + GW])) for u, g in todo]
        ss = [jnp.where(allowed[u], s, MASKED_SCORE) for (u, g), s in zip(todo, ss)]
        es = [jnp.exp(s - jnp.max(s, axis=0, keepdims=True)) for s in ss]
        ps = [(e * (1.0 / col_sum(e))).astype(bf16) for e in es]
        pqs = [p.T for p in ps]
        for (u, g), p in zip(todo, ps):
            PT[2 * rs[u] + g] = p
        for (u, g), pq in zip(todo, pqs):
            for t in range(TILES):
                at = GW * g + 128 * t
                o = nn(pq[2 * SP * t : 2 * SP * t + 2 * SP], QKV[rows[u], 2 * D + at : 2 * D + at + 128])
                ATT[rows[u], at : at + 128] = jnp.where(low_half, o[0:SP], o[SP : 2 * SP]).astype(bf16)
        return carry

    def up_part(half, j):
        if comm:
            return weights["up%d" % half][:, :, :, :, j * FC : (j + 1) * FC].reshape(D, FC)
        return weights["up"][:, :, :, :, (2 * j + half) * FC : (2 * j + half + 1) * FC].reshape(D, FC)

    def down_part(half, j):
        if comm:
            return weights["down%d" % half][j].reshape(FC, D)
        return weights["down"][j, 2 * half : 2 * half + 2].reshape(FC, D)

    def feed(half, b, carry):
        step = half * NB + b
        slot = step % 2
        rows = rows_of(b)
        mid = load_x(b) + nn(ATT[rows], weights["out"][...].reshape(D, D)) + bo
        cot_copy(step, slot).wait()
        for i in range(RB):
            cs[SP * i : SP * i + S] = cbuf[slot, i]
        if half:

            @pl.when(b > 0)
            def _():
                out_copy(b - 1, 1 - slot).wait()

            @pl.when(b + 1 < NB)
            def _():
                cot_copy(b + 1, 1 - slot).start()

        else:
            cot_copy(b + 1, 1 - slot).start()
        xh2, r2 = normalize(mid)
        second = (xh2 * g2 + c2).astype(bf16)
        branch = cs[...]
        acts, gps = [], []
        for j in range(4):
            w_up, w_down = up_part(half, j), down_part(half, j)
            cols = slice((2 * j + half) * FC, (2 * j + half + 1) * FC)
            pre = nn(second, w_up) + bias[:, cols]
            s = 0.5 * jnp.tanh((0.5 * GELU_SLOPE) * pre) + 0.5
            a = pre * s
            gp = (nt(branch, w_down) * (s + GELU_SLOPE * a * (1.0 - s))).astype(bf16)
            gbias[:, cols] += col_sum(gp.astype(f32))
            acts.append(a.astype(bf16))
            gps.append(gp)
        act, gp = jnp.concatenate(acts, axis=1), jnp.concatenate(gps, axis=1)
        w_down = jnp.concatenate([down_part(half, j) for j in range(4)], axis=0)
        w_up = jnp.concatenate([up_part(half, j) for j in range(4)], axis=1)
        grown = nn(act, w_down)
        gn2 = nt(gp, w_up)
        acc_down[...] += tn(act, branch).reshape(acc_down.shape)
        acc_up[...] += tn(second, gp).reshape(acc_up.shape)
        if not half:
            ACC[rows] = grown.astype(bf16)
            GN[rows] = gn2.astype(bf16)
            return carry
        res = (mid + bd + ACC[rows].astype(f32) + grown).astype(bf16)
        for i in range(RB):
            cbuf[slot, i] = res[SP * i : SP * i + S]
        out_copy(b, slot).start()
        gn2 = gn2 + GN[rows].astype(f32)
        h = gn2 * g2
        up = branch.astype(f32)
        gm = up + r2 * (h - lane_mean(h) - xh2 * lane_mean(h * xh2))
        GM[rows] = gm.astype(bf16)
        gsmall[4:5] += col_sum(gm.astype(bf16).astype(f32))
        gsmall[5:6] += col_sum(gn2 * xh2)
        gsmall[6:7] += col_sum(gn2)
        gsmall[7:8] += col_sum(up)
        return carry

    def out_grad():
        return tn(ATT[...], GM[...]).reshape(4, 4, 2, D // 32, D)

    def attended_grad(b, carry):
        rows = rows_of(b)
        ATT[rows] = nt(GM[rows], weights["out"][...].reshape(D, D)).astype(bf16)
        return carry

    def attend_back(i, carry):
        rs = [i * UNROLL + u for u in range(UNROLL)]
        rows = [pl.ds(pl.multiple_of(r * SP, 16), SP) for r in rs]
        todo = [(u, g) for u in range(UNROLL) for g in range(NG)]
        gos = [stack(ATT[rows[u], GW * g : GW * g + GW]) for u, g in todo]
        dps = [nt(QKV[rows[u], 2 * D + GW * g : 2 * D + GW * g + GW], go) for (u, g), go in zip(todo, gos)]
        qs = [stack(QKV[rows[u], GW * g : GW * g + GW]) for u, g in todo]
        lows = [PT[2 * rs[u] + g] for u, g in todo]
        gvs = [nn(low, go).astype(bf16) for low, go in zip(lows, gos)]
        dss = []
        for low, dpr in zip(lows, dps):
            p = low.astype(f32)
            dss.append((p * (dpr - col_sum(p * dpr))).astype(bf16))
        gks = [nn(ds, q).astype(bf16) for ds, q in zip(dss, qs)]
        gqs = []
        for (u, g), ds in zip(todo, dss):
            dsq = ds.T
            for t in range(TILES):
                at = D + GW * g + 128 * t
                o = nn(dsq[2 * SP * t : 2 * SP * t + 2 * SP], QKV[rows[u], at : at + 128])
                gqs.append((jnp.where(low_half, o[0:SP], o[SP : 2 * SP]) * scale).astype(bf16))
        for r in rs:
            x = normalize(tokv[r].astype(f32))[0]
            FL[pl.ds(pl.multiple_of(r * SP, 16), S)] = (x * g1 + c1).astype(bf16)
        for n, (u, g) in enumerate(todo):
            for t in range(TILES):
                QKV[rows[u], GW * g + 128 * t : GW * g + 128 * t + 128] = gqs[n * TILES + t]
            QKV[rows[u], D + GW * g : D + GW * g + GW] = gks[n]
            QKV[rows[u], 2 * D + GW * g : 2 * D + GW * g + GW] = gvs[n]
        return carry

    def input_grad(b, carry):
        rows = rows_of(b)
        gq = QKV[rows]
        gn1 = nt(gq, w_qkv(0, 3 * D))
        xh1, r1 = normalize(load_x(b))
        h = gn1 * g1
        res = (GM[rows].astype(f32) + r1 * (h - lane_mean(h) - xh1 * lane_mean(h * xh1))).astype(bf16)
        for i in range(RB):
            tokv[b * RB + i] = res[SP * i : SP * i + S]
        gsmall[0:1] += col_sum(gn1 * xh1)
        gsmall[1:2] += col_sum(gn1)
        gsmall[2:3] += col_sum(gq[:, 0:D].astype(f32))
        gsmall[3:4] += col_sum(gq[:, 2 * D : 3 * D].astype(f32))
        return carry

    def qkv_grad(j):
        return tn(FL[...], QKV[:, j * D : (j + 1) * D]).reshape(4, 4, 2, D // 32, D)

    if not comm:
        loop(0, NB, project)
        loop(0, NA, attend)
        for half in (0, 1):
            loop(0, NB, functools.partial(feed, half))
            for j in range(4):
                at = (2 * j + half) * FC
                grads["up"][:, :, :, :, at : at + FC] = acc_up[:, :, :, :, j * FC : (j + 1) * FC]
            grads["down"][:, 2 * half : 2 * half + 2] = acc_down[...]
            if not half:
                acc_up[...] = jnp.zeros(acc_up.shape, f32)
                acc_down[...] = jnp.zeros(acc_down.shape, f32)
        grads["out"][...] = out_grad()
        loop(0, NB, attended_grad)
        out_copy(NB - 1, (2 * NB - 1) % 2).wait()
        loop(0, NA, attend_back)
        for j in range(3):
            grads["qkv"][:, :, :, :, j * D : (j + 1) * D] = qkv_grad(j)
        loop(0, NB, input_grad)
        tok_back = pltpu.make_async_copy(tokv, gtok, tsem)
        tok_back.start()
        tok_back.wait()
        grads["small"][0:8] = gsmall[...]
        grads["small"][8:12] = gbias[...].reshape(4, D)
        return

    staged(NB, project, [
        (GATHER[2], lambda: each(rest[:3], Gather.start_onward)), (GATHER[3], lambda: each(rest[3:], Gather.start_z)),
    ])
    scat = {}
    for i, name in enumerate(HELD[1:]):
        scat[name] = Scatter(weights[name], weights[name].at[:, :, 1 - c], from_core[name], from_dp[name], from_z[name],
                             ssend.at[i], srecv.at[i], pos, PART.get(name))
    for j in range(3):
        cols = pl.ds(j * D, D)
        own = acc_up.at[:, :, j // 2, :, pl.ds(j % 2 * D, D)]
        away = GN.at[pl.ds(j * D // 2, D // 2)].reshape(4, 4, D // 32, D)
        scat[j] = Scatter(own, away, from_core["qkv"].at[:, :, :, cols], from_dp["qkv"].at[:, :, :, :, cols],
                          from_z["qkv"].at[:, :, cols], ssend.at[5 + j], srecv.at[5 + j], pos)
    small = SmallScatter(small_grad, small_fsdp, small_dp, ssend.at[8], srecv.at[8], pos)
    out_s, up0_s, down0_s, up1_s, down_s = (scat[n] for n in HELD[1:])
    first = (up0_s, down0_s)
    staged(NA, attend, [
        (GATHER[4], lambda: each(rest[:3], Gather.start_core)), (GATHER[5], lambda: each(rest[3:], Gather.start_column)),
    ])
    for g in rest[:3]:
        g.finish()
    staged(NB, functools.partial(feed, 0), [
        (FEED[0], lambda: each(rest[3:], Gather.start_onward)), (FEED[1], lambda: each(rest[3:], Gather.start_core)),
    ])
    for g in rest[3:]:
        g.finish()
    weights["up0"][...] = acc_up[...].astype(bf16)
    weights["down0"][...] = acc_down[...].astype(bf16)
    each(first, Scatter.start_core)
    acc_up[...] = jnp.zeros(acc_up.shape, f32)
    acc_down[...] = jnp.zeros(acc_down.shape, f32)
    staged(NB, functools.partial(feed, 1), [
        (FEED[2], lambda: each(first, Scatter.start_dp)), (FEED[3], lambda: each(first, Scatter.start_onward)),
        (FEED[4], lambda: each(first, Scatter.start_z)),
    ])
    weights["down1"][...] = acc_down[...].astype(bf16)
    down_s.start_core()
    weights["up1"][...] = acc_up[...].astype(bf16)
    up1_s.start_core()
    grad = out_grad().astype(bf16)
    loop(0, NB, attended_grad)
    weights["out"][...] = grad
    out_s.start_core()
    out_copy(NB - 1, (2 * NB - 1) % 2).wait()
    names = (down_s.start_dp, up1_s.start_dp, out_s.start_dp,
             down_s.start_onward, up1_s.start_onward, out_s.start_onward)
    staged(NA, attend_back, list(zip(REDUCE, names)))
    for j in range(3):
        scat[j].start_core(qkv_grad(j))
        if j:
            scat[j - 1].start_dp()
    names = (down_s.start_z, scat[2].start_dp, up1_s.start_z, out_s.start_z, scat[0].start_onward, scat[1].start_onward,
             scat[2].start_onward, scat[0].start_z, scat[1].start_z)
    staged(NB, input_grad, list(zip(REDUCE_QKV, names)))
    tok_back = pltpu.make_async_copy(tokv, gtok, tsem)
    tok_back.start()
    gs = small_grad
    for s in range(32):
        row = s // 4
        gs[s // 8, (s % 8) // 2, s % 2, 0:1, 0:128] = gsmall[row : row + 1, 128 * (s % 4) : 128 * (s % 4) + 128]
        two = gbias[:, 128 * (s // 2) : 128 * (s // 2) + 128]
        gs[s // 8, (s % 8) // 2, s % 2, 1:2, 0:64] = two[:, 64 * (s % 2) : 64 * (s % 2) + 64]
    small.start()
    scat[2].start_z()

    def give(name, total, place=lambda j: j):
        rows, cols = total.shape
        per = shares[name].shape[0] // rows
        for j in range(cols // 128):
            shares[name][pl.ds(place(j), rows, stride=per), :] = total[:, 128 * j : 128 * j + 128]

    def give_up(half, total):
        runs = FC // 128
        give("up", total, lambda j: (2 * (j // runs) + half) * runs + j % runs)

    up0_s.finish(functools.partial(give_up, 0))
    down0_s.finish(functools.partial(give, "down"))
    down_s.finish(functools.partial(give, "down"))
    up1_s.finish(functools.partial(give_up, 1))
    out_s.finish(functools.partial(give, "out"))
    small.pass_on()
    for j in range(3):
        scat[j].finish(functools.partial(give, "qkv", place=lambda i, j=j: j * D // 128 + i))
    shares["small"][...] = small.finish()
    tok_back.wait()


def block_call(comm, tokens, segments, cotangent, pieces, FF):
    R, S, D = tokens.shape
    SP = (S + 15) // 16 * 16
    T, M = R * SP, ROW_BLOCK * SP
    V, dma = pltpu.VMEM, pltpu.SemaphoreType.DMA
    vm, hbm = pl.BlockSpec(memory_space=pltpu.VMEM), pl.BlockSpec(memory_space=pl.ANY)
    rows = {"qkv": (16, 3 * D), "out": (16, D), "up": (16, FF), "down": (FF // 32, D)}
    out_shape = [jax.ShapeDtypeStruct(tokens.shape, bf16)] * 2
    if comm:
        out_shape += [jax.ShapeDtypeStruct(p.shape, f32) for p in pieces[:4]]
        out_shape += [jax.ShapeDtypeStruct((8, 128), f32)]
    else:
        out_shape += [jax.ShapeDtypeStruct((4, 4, 2) + rows[n], f32) for n in ARRAYS]
        out_shape += [jax.ShapeDtypeStruct((12, D), f32)]
    scratch = [
        V((R, S, D), bf16), V((2, ROW_BLOCK, S, D), bf16), V((M, D), bf16),
        V((T, 3 * D), bf16), V((T, D), bf16), V((2 * R, SP, GROUP * SP), bf16), V((T, D), bf16),
        V((T, D), bf16), V((T, D), bf16), V((R, 1, GROUP * SP), jnp.int32), V((1, FF), f32), V((8, D), f32),
        V((1, FF), f32), V((8, D), f32), V((4, 4, 2, 16, FF // 2), f32),
        V((4, 2, 2, FF // 32, D), f32), dma, dma((2,)), dma((2,)),
    ]
    if comm:
        small = (8, 128)
        held = {"qkv": (16, 3 * D), "out": (16, D)}
        for half in "01":
            held.update({"up" + half: (16, FF // 2), "down" + half: (FF // 32, D)})
        depth = {n: 2 if n in PART else 4 for n in HELD}
        scratch += [V((4, depth[n], 2) + (held[n] if n != "qkv" else (16, 3 * D + 128)), bf16) for n in HELD]
        scratch += [V((4, 4, 2) + small, f32)]
        scratch += [V((4, depth[n]) + held[n], bf16) for n in HELD]
        scratch += [V((3, 2, depth[n] // 2) + held[n], bf16) for n in HELD]
        scratch += [V((3,) + held[n], bf16) for n in HELD]
        scratch += [V((7, 4) + small, f32), V((3,) + small, f32), dma((6, 21)), dma((6, 21)), dma((9, 10)), dma((9, 10))]
    params = dict(vmem_limit_bytes=63480 * 1000)
    if comm:
        params.update(collective_id=1, has_side_effects=True)
    return pl.pallas_call(
        functools.partial(block_kernel, comm, R, S, SP, D, FF),
        out_shape=out_shape,
        in_specs=[hbm, vm, hbm] + [vm] * 5,
        out_specs=[hbm, hbm] + [vm] * 5,
        scratch_shapes=scratch,
        compiler_params=pltpu.CompilerParams(**params),
    )(tokens, segments, cotangent, *pieces)


def hand_over_kernel(parts, *refs):
    n = len(parts)
    given, kept, held, into, away = refs[: n + 1], refs[n + 1 : 2 * n + 3], refs[2 * n + 3 : 3 * n + 3], refs[-2], refs[-1]
    spans, slot = [], 0
    for i, count in enumerate(parts):
        size = given[i].shape[0] // count
        for p in range(count):
            rows = pl.ds(p * size, size)
            first = pltpu.make_async_copy(given[i].at[rows], held[i].at[rows], into.at[slot])
            spans.append((first, pltpu.make_async_copy(held[i].at[rows], kept[i].at[rows], away.at[slot])))
            slot += 1
    for first, _ in spans:
        first.start()
    kept[n][...] = given[n][0:1]
    kept[n + 1][...] = given[n][1:2, 0 : kept[n + 1].shape[1]]
    for first, second in spans:
        first.wait()
        second.start()
    for _, second in spans:
        second.wait()


def hand_over(arrays, tile, count):
    n = len(arrays)
    parts = [6 if a.ndim == 3 else 1 for a in arrays]
    hbm, vm = pl.BlockSpec(memory_space=pl.ANY), pl.BlockSpec(memory_space=pltpu.VMEM)
    shapes = [jax.ShapeDtypeStruct(a.shape, a.dtype) for a in arrays]
    shapes += [jax.ShapeDtypeStruct((1, tile.shape[1]), f32), jax.ShapeDtypeStruct((1, count), f32)]
    sems = pltpu.SemaphoreType.DMA((sum(parts),))
    return pl.pallas_call(
        functools.partial(hand_over_kernel, parts), out_shape=shapes, in_specs=[hbm] * n + [vm],
        out_specs=[hbm] * n + [vm, vm], scratch_shapes=[pltpu.VMEM(a.shape, a.dtype) for a in arrays] + [sems, sems],
        compiler_params=pltpu.CompilerParams(vmem_limit_bytes=60 * 1024 * 1024),
    )(*arrays, tile)


def body(sizes, tokens, segment_ids, qkv_weight, out_weight, up_weight, up_bias, down_weight, small_params, cotangent):
    D = tokens.shape[2]
    n = sizes[0] * sizes[1]
    FF = up_bias.shape[0] * n
    flats = (qkv_weight, out_weight, up_weight, down_weight)
    if sizes == (4, 8):
        tile = jnp.pad(jnp.concatenate([small_params, up_bias]), (0, 16 * 128 - 192)).reshape(16, 128)
        o = block_call(True, tokens, segment_ids, cotangent, [f.reshape(-1, 128) for f in flats] + [tile], FF)
        o = hand_over(o[:6], o[6], up_bias.shape[0])
        shares = [v.reshape(-1) for v in o[2:]]
        return (o[0], o[1], shares[0], shares[1], shares[2], shares[5], shares[3], shares[4])
    axes = ("dp", "fsdp")

    def gather(v):
        return lax.all_gather(v, axes, axis=0, tiled=True)

    def scatter(v):
        return lax.psum_scatter(v.reshape(-1), axes, scatter_dimension=0, tiled=True)

    packed = lax.all_gather(jnp.concatenate([small_params, up_bias]), axes, axis=0, tiled=False)
    count = small_params.shape[0]
    tile = jnp.concatenate([packed[:, :count].reshape(8, D), packed[:, count:].reshape(4, D)])
    whole = [gather(f) for f in flats]
    shapes = ((4, 4, 2, 16, 3 * D), (4, 4, 2, 16, D), (4, 4, 2, 16, FF), (4, 4, 2, FF // 32, D))
    o = block_call(False, tokens, segment_ids, cotangent, [w.reshape(s) for w, s in zip(whole, shapes)] + [tile], FF)
    return (o[0], o[1], scatter(o[2]), scatter(o[3]), scatter(o[4]), scatter(o[6][8:12]), scatter(o[5]), scatter(o[6][0:8]))


def solution(mesh):
    rows, flat = P(("dp", "fsdp"), None, None), P(("dp", "fsdp"))
    in_specs = (rows, P(("dp", "fsdp"), None), flat, flat, flat, flat, flat, flat, rows)
    out_specs = (rows, rows, flat, flat, flat, flat, flat, flat)
    sizes = (mesh.shape["dp"], mesh.shape["fsdp"])
    return jax.shard_map(functools.partial(body, sizes), mesh=mesh, in_specs=in_specs, out_specs=out_specs, check_vma=False)
```

```python
import functools

import jax
import jax.numpy as jnp
from jax import lax
from jax.experimental import pallas as pl
from jax.experimental.pallas import tpu as pltpu
from jax.sharding import PartitionSpec as P

bf16 = jnp.bfloat16
f32 = jnp.float32
HEADS = 8
HEAD_DIM = 64
GROUP = 4
NORM_EPS = 1e-05
GELU_SLOPE = 1.702
MASKED_SCORE = -1e30
MESH = pl.DeviceIdType.MESH
ROW_BLOCK = 6
UNROLL = 4
GATHER = (2, 3, 2, 4, 2, 8)
FEED = (2, 4, 2, 4, 5)
REDUCE = (0, 2, 3, 5, 7, 8)
REDUCE_QKV = (0, 1, 1, 2, 2, 3, 4, 4, 5)
ARRAYS = ("qkv", "out", "up", "down")
HELD = ("qkv", "out", "up0", "down0", "up1", "down1")
PART = {"down0": 0, "down1": 1}


def nn(a, b):
    return lax.dot_general(a, b, (((1,), (0,)), ((), ())), preferred_element_type=f32)


def nt(a, b):
    return lax.dot_general(a, b, (((1,), (1,)), ((), ())), preferred_element_type=f32)


def tn(a, b):
    return lax.dot_general(a, b, (((0,), (0,)), ((), ())), preferred_element_type=f32)


def col_sum(v):
    return jnp.sum(v, axis=0, keepdims=True)


def lane_mean(v):
    return jnp.sum(v, axis=-1, keepdims=True) * (1.0 / v.shape[-1])


def normalize(x):
    xc = x - lane_mean(x)
    inv = lax.rsqrt(lane_mean(xc * xc) + NORM_EPS)
    return xc * inv, inv


def flip(index, bits):
    low, high = index % 2, index // 2
    if bits & 1:
        low = 1 - low
    if bits & 2:
        high = 1 - high
    return high * 2 + low


class Gather:
    def __init__(self, buf, send, recv, pos, part=None):
        self.buf, self.send, self.recv, self.part = buf, send, recv, part
        self.dp, self.z, self.c = pos
        self.nz = buf.shape[1]

    def only(self, z, act):
        if self.part is None:
            act()
        else:
            pl.when(z // 2 == self.part)(act)

    def copy(self, index, slot, device):
        ref = self.buf.at[index]
        return pltpu.make_async_remote_copy(
            src_ref=ref, dst_ref=ref, send_sem=self.send.at[slot], recv_sem=self.recv.at[slot],
            device_id=device, device_id_type=MESH)

    def along_z(self, k, mine=True):
        z = self.z if mine else flip(self.z, k)
        return self.copy((self.dp, z % self.nz, self.c), k - 1, (self.dp, flip(self.z, k) * 2 + self.c))

    def column(self, bit, mine=True):
        dp = self.dp if mine else flip(self.dp, bit)
        return self.copy((dp, slice(None), self.c), 2 + bit, (flip(self.dp, bit), self.z * 2 + self.c))

    def onward(self, bit, mine=True):
        other = 3 - bit
        dp = flip(self.dp, other) if mine else flip(self.dp, 3)
        half = pl.ds(0 if bit == 2 else self.nz // 2, self.nz // 2)
        return self.copy((dp, half, self.c), 4 + bit, (flip(self.dp, bit), self.z * 2 + self.c))

    def to_core(self, mine=True):
        c = self.c if mine else 1 - self.c
        return self.copy((slice(None), slice(None), c), 7, (self.dp, self.z * 2 + 1 - self.c))

    def start_z(self):
        for k in (1, 2, 3):
            self.only(self.z, self.along_z(k).start)

    def start_column(self):
        for k in (1, 2, 3):
            self.only(flip(self.z, k), self.along_z(k, False).wait_recv)
        for bit in (1, 2):
            self.column(bit).start()

    def start_onward(self):
        for bit in (1, 2):
            self.column(3 - bit, False).wait_recv()
            self.onward(bit).start()

    def start_core(self):
        for bit in (1, 2):
            self.onward(bit, False).wait_recv()
        self.to_core().start()

    def finish(self):
        self.to_core(False).wait_recv()
        for k in (1, 2, 3):
            self.only(self.z, self.along_z(k).wait_send)
        for bit in (1, 2):
            self.column(bit).wait_send()
            self.onward(bit).wait_send()
        self.to_core().wait_send()


class EagerGather(Gather):
    def shard(self, k, bit, mine=True):
        dp = self.dp if mine else flip(self.dp, bit)
        return self.copy((dp, flip(self.z, k), self.c), 2 + bit * 4 + k - 1, (flip(self.dp, bit), self.z * 2 + self.c))

    def forward(self, k, mine=True):
        bit = 2 - k % 2
        dp = flip(self.dp, 3 - bit) if mine else flip(self.dp, 3)
        return self.copy((dp, flip(self.z, k), self.c), 13 + k, (flip(self.dp, bit), self.z * 2 + self.c))

    def core_column(self, bits, mine=True):
        c = self.c if mine else 1 - self.c
        return self.copy((flip(self.dp, bits), slice(None), c), 17 + bits, (self.dp, self.z * 2 + 1 - self.c))

    def start(self):
        for k in (1, 2, 3):
            self.along_z(k).start()
        for bit in (1, 2):
            self.shard(0, bit).start()

    def start_column(self, between=lambda: None):
        for k in (1, 2, 3):
            self.along_z(k, False).wait_recv()
            for bit in (1, 2):
                self.shard(k, bit).start()
            if k == 1:
                between()
        self.core_column(0).start()

    def start_onward(self):
        for k in (0, 1, 2, 3):
            bit = 2 - k % 2
            self.shard(k, 3 - bit, False).wait_recv()
            self.forward(k).start()
        for k in (0, 1, 2, 3):
            bit = 2 - k % 2
            self.shard(k, bit, False).wait_recv()
        for bit in (1, 2):
            self.core_column(bit).start()

    def start_core(self):
        for k in (0, 1, 2, 3):
            self.forward(k, False).wait_recv()
        self.core_column(3).start()

    def finish(self):
        for bits in (0, 1, 2, 3):
            self.core_column(bits, False).wait_recv()
        for k in (1, 2, 3):
            self.along_z(k).wait_send()
        for k in (0, 1, 2, 3):
            for bit in (1, 2):
                self.shard(k, bit).wait_send()
            self.forward(k).wait_send()
            self.core_column(k).wait_send()


class Scatter:
    def __init__(self, grad, half, from_core, from_dp, from_z, send, recv, pos, part=None):
        self.part, self.nz, self.dtype = part, from_core.shape[1], bf16
        self.grad, self.half, self.from_core, self.from_dp, self.from_z = grad, half, from_core, from_dp, from_z
        self.send, self.recv = send, recv
        self.dp, self.z, self.c = pos

    def copy(self, src, dst, slot, device):
        return pltpu.make_async_remote_copy(
            src_ref=src, dst_ref=dst, send_sem=self.send.at[slot], recv_sem=self.recv.at[slot],
            device_id=device, device_id_type=MESH)

    def only(self, z, act):
        if self.part is None:
            act()
        else:
            pl.when(z // 2 == self.part)(act)

    def half_of(self, half):
        return pl.ds(half * self.nz // 2, self.nz // 2)

    def core_copy(self):
        return self.copy(self.half, self.from_core, 0, (self.dp, self.z * 2 + 1 - self.c))

    def dp_copy(self, step, bit, onward):
        half = bit - 1 if step == 0 else 2 - bit
        dp = flip(self.dp, 3 if onward else bit)
        return self.copy(self.from_core.at[dp, self.half_of(half)], self.from_dp.at[2 * step + onward, bit - 1],
                         1 + 2 * (2 * step + onward) + bit - 1, (flip(self.dp, bit), self.z * 2 + self.c))

    def z_copy(self, k):
        return self.copy(self.from_core.at[self.dp, flip(self.z, k) % self.nz], self.from_z.at[k - 1], 6 + k,
                         (self.dp, flip(self.z, k) * 2 + self.c))

    def start_core(self, whole=None):
        if whole is not None:
            zero, one = whole[:, :, 0], whole[:, :, 1]
            self.grad[...] = jnp.where(self.c == 0, zero, one)
            self.half[...] = jnp.where(self.c == 0, one, zero).astype(self.dtype)
        self.core_copy().start()

    def own_part(self, *index):
        return self.grad[self.own(*index)].astype(f32)

    def own(self, *index):
        return index if len(self.grad.shape) == 4 else index + (slice(None),) * (2 - len(index)) + (self.c,)

    def start_dp(self):
        self.core_copy().wait_recv()
        for bit in (1, 2):
            for onward in (1, 0):
                at = (flip(self.dp, 3 if onward else bit), self.half_of(bit - 1))
                self.from_core[at] = (self.own_part(*at) + self.from_core[at].astype(f32)).astype(self.dtype)
                self.dp_copy(0, bit, onward).start()

    def start_onward(self):
        for bit in (1, 2):
            first = 3 - bit
            self.dp_copy(0, first, 1).wait_recv()
            at = (flip(self.dp, bit), self.half_of(first - 1))
            total = self.own_part(*at) + self.from_core[at].astype(f32)
            self.from_core[at] = (total + self.from_dp[1, first - 1].astype(f32)).astype(self.dtype)
            self.dp_copy(1, bit, 0).start()

    def start_z(self):
        for bit in (1, 2):
            self.dp_copy(0, bit, 0).wait_recv()
            self.dp_copy(1, bit, 0).wait_recv()
        for half in (0, 1):
            at = (self.dp, self.half_of(half))
            total = self.own_part(*at) + self.from_core[at].astype(f32)
            total += self.from_dp[0, half].astype(f32) + self.from_dp[2, 1 - half].astype(f32)
            self.grad[self.own(*at)] = total.astype(self.grad.dtype)
            self.from_core[at] = total.astype(self.dtype)
        for k in (1, 2, 3):
            self.only(flip(self.z, k), self.z_copy(k).start)

    def finish(self, use):
        def whole():
            for k in (1, 2, 3):
                self.z_copy(k).wait_recv()
            total = self.own_part(self.dp, self.z % self.nz)
            for k in (1, 2, 3):
                total += self.from_z[k - 1].astype(f32)
            use(total)

        self.only(self.z, whole)
        self.core_copy().wait_send()
        for bit in (1, 2):
            self.dp_copy(0, bit, 0).wait_send()
            self.dp_copy(0, bit, 1).wait_send()
            self.dp_copy(1, bit, 0).wait_send()
        for k in (1, 2, 3):
            self.only(flip(self.z, k), self.z_copy(k).wait_send)


class SmallScatter:
    def __init__(self, grad, from_fsdp, from_dp, send, recv, pos):
        self.grad, self.from_fsdp, self.from_dp, self.send, self.recv = grad, from_fsdp, from_dp, send, recv
        self.dp, self.z, self.c = pos

    def copy(self, src, dst, slot, device):
        return pltpu.make_async_remote_copy(
            src_ref=src, dst_ref=dst, send_sem=self.send.at[slot], recv_sem=self.recv.at[slot],
            device_id=device, device_id_type=MESH)

    def first(self, k):
        z, c = flip(self.z, k // 2), self.c if k % 2 == 0 else 1 - self.c
        return self.copy(self.grad.at[:, z, c], self.from_fsdp.at[k - 1], k - 1, (self.dp, z * 2 + c))

    def second(self, k):
        dp = flip(self.dp, k)
        return self.copy(self.grad.at[dp, self.z, self.c], self.from_dp.at[k - 1], 6 + k, (dp, self.z * 2 + self.c))

    def start(self):
        for k in range(1, 8):
            self.first(k).start()

    def pass_on(self):
        for k in range(1, 8):
            self.first(k).wait_recv()
        total = self.grad[:, self.z, self.c]
        for k in range(1, 8):
            total += self.from_fsdp[k - 1]
        self.grad[:, self.z, self.c] = total
        for k in (1, 2, 3):
            self.second(k).start()

    def finish(self):
        for k in (1, 2, 3):
            self.second(k).wait_recv()
        total = self.grad[self.dp, self.z, self.c] + self.from_dp[0] + self.from_dp[1] + self.from_dp[2]
        for k in range(1, 8):
            self.first(k).wait_send()
        for k in (1, 2, 3):
            self.second(k).wait_send()
        return total


def block_kernel(comm, R, S, SP, D, FF, *refs):
    RB, M, NB, FC, FH, NA = ROW_BLOCK, ROW_BLOCK * SP, R // ROW_BLOCK, FF // 8, FF // 2, R // UNROLL
    GW = GROUP * HEAD_DIM
    refs = list(refs)

    def take(n):
        out = refs[:n]
        del refs[:n]
        return out

    tok, seg, cot = take(3)
    shards = dict(zip(ARRAYS + ("small",), take(5)))
    if comm:
        shards["bias"] = take(1)[0]
    out, gtok = take(2)
    if comm:
        shares = dict(zip(ARRAYS + ("small",), take(5)))
    else:
        grads = dict(zip(ARRAYS + ("small",), take(5)))
    tokv, cbuf, cs, QKV, ATT, PT, GM, ACC, GN, start, bias, smallv, gbias, gsmall = take(14)
    FL = ACC
    acc_up, acc_down = take(2)
    tsem, csem, osem = take(3)
    if comm:
        weights = dict(zip(HELD, take(6)))
        small_grad = take(1)[0]
        from_core, from_dp, from_z = (dict(zip(HELD, take(6))) for _ in range(3))
        small_fsdp, small_dp, gsend, grecv, ssend, srecv = take(6)
    else:
        weights = shards

    def loop(a, b, f):
        lax.fori_loop(a, b, f, 0)

    def staged(count, step, events):
        def body(i, carry):
            for at, act in events:
                if at < count:
                    pl.when(i == at)(act)
            return step(i, carry)

        loop(0, count, body)
        for at, act in events:
            if at >= count:
                act()

    def each(things, act):
        for thing in things:
            act(thing)

    def when(plan):
        return [(NA * at // 18, act) for at, act in plan]

    tok_copy = pltpu.make_async_copy(tok, tokv, tsem)
    tok_copy.start()

    def cot_copy(b, slot):
        return pltpu.make_async_copy(cot.at[pl.ds(b % NB * RB, RB)], cbuf.at[slot], csem.at[slot])

    def out_copy(b, slot):
        return pltpu.make_async_copy(cbuf.at[slot], out.at[pl.ds(b * RB, RB)], osem.at[slot])

    cot_copy(0, 0).start()
    if comm:
        dp = lax.axis_index("dp")
        fs = lax.axis_index("fsdp")
        pos = (dp, fs // 2, fs % 2)
        z, c = pos[1], pos[2]
        peers = [(flip(dp, k), fs) for k in (1, 2, 3)] + [(dp, flip(z, k) * 2 + c) for k in (1, 2, 3)]
        peers += [(dp, flip(z, k) * 2 + 1 - c) for k in (0, 1, 2, 3)]
        barrier = pltpu.get_barrier_semaphore()
        for peer in peers:
            pl.semaphore_signal(barrier, inc=1, device_id=peer, device_id_type=MESH)
        spread = small_grad.reshape(256, 128)
        for name in ARRAYS:
            rows = FF // 32 if name == "down" else 16
            src = shards[name]
            per = src.shape[0] // rows
            spread[0 : src.shape[0]] = src[...].astype(f32)
            for j in range(per):
                piece = spread[pl.ds(j, rows, stride=per), :].astype(bf16)
                at = slice(128 * j, 128 * j + 128)
                if name == "up":
                    run, left = divmod(128 * j, 2 * FC)
                    half, left = divmod(left, FC)
                    weights["up%d" % half][dp, z, c, :, run * FC + left : run * FC + left + 128] = piece
                elif name == "down":
                    for part in (0, 1):

                        @pl.when(z // 2 == part)
                        def _(part=part, at=at, piece=piece):
                            weights["down%d" % part][dp, z % 2, c, :, at] = piece

                else:
                    weights[name][dp, z, c, :, at] = piece
        row = lax.broadcasted_iota(jnp.int32, (16, 128), 0)
        given, extra = shards["small"][...].astype(f32), shards["bias"][...].astype(f32)
        extra = jnp.concatenate([extra, jnp.zeros((1, 128 - extra.shape[1]), f32)], axis=1)
        tile = jnp.where(row == 0, given, jnp.where(row == 1, extra, 0.0))
        weights["qkv"][dp, z, c, :, 3 * D :] = tile.astype(bf16)
        gathers = {n: Gather(weights[n], gsend.at[i], grecv.at[i], pos, PART.get(n)) for i, n in enumerate(HELD)}
        gathers["qkv"] = EagerGather(weights["qkv"], gsend.at[0], grecv.at[0], pos)
        pl.semaphore_wait(barrier, len(peers))
        gathers["qkv"].start()
        rest = [gathers[n] for n in HELD[1:]]
        gathers["qkv"].start_column(lambda: each(rest[:2], Gather.start_z))

    cs[...] = jnp.zeros(cs.shape, bf16)
    sg = seg[...]
    st = jnp.zeros(sg.shape, jnp.int32)
    for v in range(1, 4):
        count = jnp.sum((sg < v).astype(f32), axis=1, keepdims=True).astype(jnp.int32)
        st = jnp.where(sg == v, count, st)
    st = jnp.concatenate([st, jnp.zeros((R, SP - S), jnp.int32)], axis=1)
    start[...] = jnp.concatenate([st] * GROUP, axis=1).reshape(R, 1, GROUP * SP)
    for ref in (acc_up, acc_down, gbias, gsmall):
        ref[...] = jnp.zeros(ref.shape, f32)
    tok_copy.wait()

    def load_x(b):
        for i in range(RB):
            cs[SP * i : SP * i + S] = tokv[b * RB + i]
        return cs[...].astype(f32)

    def rows_of(b):
        return pl.ds(pl.multiple_of(b * M, 16), M)

    def norm_one(b, carry):
        rows = rows_of(b)
        xh1 = normalize(load_x(b))[0]
        high = xh1.astype(bf16)
        ACC[rows] = high
        GN[rows] = (xh1 - high.astype(f32)).astype(bf16)
        return carry

    if comm:
        staged(NB, norm_one, [
            (0, gathers["qkv"].start_onward), (0, rest[2].start_z), (GATHER[0], lambda: each(rest[:3], Gather.start_column)),
            (GATHER[1], gathers["qkv"].start_core),
        ])
        gathers["qkv"].finish()
        wq = weights["qkv"]
        for s in range(32):
            piece = wq[s // 8, (s % 8) // 2, s % 2, :, 3 * D :].astype(f32)
            smallv[s // 4 : s // 4 + 1, 128 * (s % 4) : 128 * (s % 4) + 128] = piece[0:1]
        for s in range(0, 32, 2):
            two = [wq[s // 8, (s % 8) // 2, i, :, 3 * D : 3 * D + 64].astype(f32)[1:2] for i in (0, 1)]
            bias[:, 64 * s : 64 * s + 128] = jnp.concatenate(two, axis=1)
    else:
        lax.fori_loop(0, NB, norm_one, 0)
        bias[...] = shards["small"][8:12].astype(f32).reshape(1, FF)
        smallv[...] = shards["small"][0:8].astype(f32)

    def w_qkv(a, b):
        return weights["qkv"][:, :, :, :, a:b].reshape(D, b - a)

    sm = smallv[...]
    g1, c1, bq, bv, bo, g2, c2, bd = [sm[i : i + 1] for i in range(8)]
    scale = HEAD_DIM ** (-0.5)
    bkv = jnp.concatenate([jnp.zeros_like(bv), bv], axis=1)
    lane = lax.broadcasted_iota(jnp.int32, (1, GW), 1)
    head_mask = [(lane // HEAD_DIM == j).astype(f32).astype(bf16) for j in range(GROUP)]
    low_half = lax.broadcasted_iota(jnp.int32, (1, 128), 1) < HEAD_DIM

    def stack(v):
        return jnp.concatenate([v * head_mask[j] for j in range(GROUP)], axis=0)

    def project(b, carry):
        rows = rows_of(b)
        fl = ((ACC[rows].astype(f32) + GN[rows].astype(f32)) * g1 + c1).astype(bf16)
        QKV[rows, 0:D] = ((nn(fl, w_qkv(0, D)) + bq) * scale).astype(bf16)
        QKV[rows, D : 3 * D] = (nn(fl, w_qkv(D, 3 * D)) + bkv).astype(bf16)
        return carry

    kidx = lax.broadcasted_iota(jnp.int32, (SP, GROUP * SP), 0)
    qidx = lax.broadcasted_iota(jnp.int32, (1, GROUP * SP), 1)
    qidx = qidx - SP * sum((qidx >= SP * j).astype(jnp.int32) for j in range(1, GROUP))

    NG = HEADS // GROUP
    TILES = GW // 128

    def attend(i, carry):
        rs = [i * UNROLL + u for u in range(UNROLL)]
        rows = [pl.ds(pl.multiple_of(r * SP, 16), SP) for r in rs]
        todo = [(u, g) for u in range(UNROLL) for g in range(NG)]
        allowed = [(kidx >= start[r]) & (kidx <= qidx) for r in rs]
        ss = [nt(QKV[rows[u], D + GW * g : D + GW * g + GW], stack(QKV[rows[u], GW * g : GW * g + GW])) for u, g in todo]
        ss = [jnp.where(allowed[u], s, MASKED_SCORE) for (u, g), s in zip(todo, ss)]
        es = [jnp.exp(s - jnp.max(s, axis=0, keepdims=True)) for s in ss]
        ps = [(e * (1.0 / col_sum(e))).astype(bf16) for e in es]
        pqs = [p.T for p in ps]
        for (u, g), p in zip(todo, ps):
            PT[2 * rs[u] + g] = p
        for (u, g), pq in zip(todo, pqs):
            for t in range(TILES):
                at = GW * g + 128 * t
                o = nn(pq[2 * SP * t : 2 * SP * t + 2 * SP], QKV[rows[u], 2 * D + at : 2 * D + at + 128])
                ATT[rows[u], at : at + 128] = jnp.where(low_half, o[0:SP], o[SP : 2 * SP]).astype(bf16)
        return carry

    def up_part(half, j):
        if comm:
            return weights["up%d" % half][:, :, :, :, j * FC : (j + 1) * FC].reshape(D, FC)
        return weights["up"][:, :, :, :, (2 * j + half) * FC : (2 * j + half + 1) * FC].reshape(D, FC)

    def down_part(half, j):
        if comm:
            return weights["down%d" % half][j].reshape(FC, D)
        return weights["down"][j, 2 * half : 2 * half + 2].reshape(FC, D)

    def feed(half, b, carry):
        step = half * NB + b
        slot = step % 2
        rows = rows_of(b)
        mid = load_x(b) + nn(ATT[rows], weights["out"][...].reshape(D, D)) + bo
        cot_copy(step, slot).wait()
        for i in range(RB):
            cs[SP * i : SP * i + S] = cbuf[slot, i]
        if half:

            @pl.when(b > 0)
            def _():
                out_copy(b - 1, 1 - slot).wait()

            @pl.when(b + 1 < NB)
            def _():
                cot_copy(b + 1, 1 - slot).start()

        else:
            cot_copy(b + 1, 1 - slot).start()
        xh2, r2 = normalize(mid)
        second = (xh2 * g2 + c2).astype(bf16)
        branch = cs[...]
        acts, gps = [], []
        for j in range(4):
            w_up, w_down = up_part(half, j), down_part(half, j)
            cols = slice((2 * j + half) * FC, (2 * j + half + 1) * FC)
            pre = nn(second, w_up) + bias[:, cols]
            s = 0.5 * jnp.tanh((0.5 * GELU_SLOPE) * pre) + 0.5
            a = pre * s
            gp = (nt(branch, w_down) * (s + GELU_SLOPE * a * (1.0 - s))).astype(bf16)
            gbias[:, cols] += col_sum(gp.astype(f32))
            acts.append(a.astype(bf16))
            gps.append(gp)
        act, gp = jnp.concatenate(acts, axis=1), jnp.concatenate(gps, axis=1)
        w_down = jnp.concatenate([down_part(half, j) for j in range(4)], axis=0)
        w_up = jnp.concatenate([up_part(half, j) for j in range(4)], axis=1)
        grown = nn(act, w_down)
        gn2 = nt(gp, w_up)
        acc_down[...] += tn(act, branch).reshape(acc_down.shape)
        acc_up[...] += tn(second, gp).reshape(acc_up.shape)
        if not half:
            ACC[rows] = grown.astype(bf16)
            GN[rows] = gn2.astype(bf16)
            return carry
        res = (mid + bd + ACC[rows].astype(f32) + grown).astype(bf16)
        for i in range(RB):
            cbuf[slot, i] = res[SP * i : SP * i + S]
        out_copy(b, slot).start()
        gn2 = gn2 + GN[rows].astype(f32)
        h = gn2 * g2
        up = branch.astype(f32)
        gm = up + r2 * (h - lane_mean(h) - xh2 * lane_mean(h * xh2))
        GM[rows] = gm.astype(bf16)
        gsmall[4:5] += col_sum(gm.astype(bf16).astype(f32))
        gsmall[5:6] += col_sum(gn2 * xh2)
        gsmall[6:7] += col_sum(gn2)
        gsmall[7:8] += col_sum(up)
        return carry

    def out_grad():
        return tn(ATT[...], GM[...]).reshape(4, 4, 2, D // 32, D)

    def attended_grad(b, carry):
        rows = rows_of(b)
        ATT[rows] = nt(GM[rows], weights["out"][...].reshape(D, D)).astype(bf16)
        return carry

    def attend_back(i, carry):
        rs = [i * UNROLL + u for u in range(UNROLL)]
        rows = [pl.ds(pl.multiple_of(r * SP, 16), SP) for r in rs]
        todo = [(u, g) for u in range(UNROLL) for g in range(NG)]
        gos = [stack(ATT[rows[u], GW * g : GW * g + GW]) for u, g in todo]
        dps = [nt(QKV[rows[u], 2 * D + GW * g : 2 * D + GW * g + GW], go) for (u, g), go in zip(todo, gos)]
        qs = [stack(QKV[rows[u], GW * g : GW * g + GW]) for u, g in todo]
        lows = [PT[2 * rs[u] + g] for u, g in todo]
        gvs = [nn(low, go).astype(bf16) for low, go in zip(lows, gos)]
        dss = []
        for low, dpr in zip(lows, dps):
            p = low.astype(f32)
            dss.append((p * (dpr - col_sum(p * dpr))).astype(bf16))
        gks = [nn(ds, q).astype(bf16) for ds, q in zip(dss, qs)]
        gqs = []
        for (u, g), ds in zip(todo, dss):
            dsq = ds.T
            for t in range(TILES):
                at = D + GW * g + 128 * t
                o = nn(dsq[2 * SP * t : 2 * SP * t + 2 * SP], QKV[rows[u], at : at + 128])
                gqs.append((jnp.where(low_half, o[0:SP], o[SP : 2 * SP]) * scale).astype(bf16))
        for r in rs:
            x = normalize(tokv[r].astype(f32))[0]
            FL[pl.ds(pl.multiple_of(r * SP, 16), S)] = (x * g1 + c1).astype(bf16)
        for n, (u, g) in enumerate(todo):
            for t in range(TILES):
                QKV[rows[u], GW * g + 128 * t : GW * g + 128 * t + 128] = gqs[n * TILES + t]
            QKV[rows[u], D + GW * g : D + GW * g + GW] = gks[n]
            QKV[rows[u], 2 * D + GW * g : 2 * D + GW * g + GW] = gvs[n]
        return carry

    def input_grad(b, carry):
        rows = rows_of(b)
        gq = QKV[rows]
        gn1 = nt(gq, w_qkv(0, 3 * D))
        xh1, r1 = normalize(load_x(b))
        h = gn1 * g1
        res = (GM[rows].astype(f32) + r1 * (h - lane_mean(h) - xh1 * lane_mean(h * xh1))).astype(bf16)
        for i in range(RB):
            tokv[b * RB + i] = res[SP * i : SP * i + S]
        gsmall[0:1] += col_sum(gn1 * xh1)
        gsmall[1:2] += col_sum(gn1)
        gsmall[2:3] += col_sum(gq[:, 0:D].astype(f32))
        gsmall[3:4] += col_sum(gq[:, 2 * D : 3 * D].astype(f32))
        return carry

    def qkv_grad(j):
        return tn(FL[...], QKV[:, j * D : (j + 1) * D]).reshape(4, 4, 2, D // 32, D)

    if not comm:
        loop(0, NB, project)
        loop(0, NA, attend)
        for half in (0, 1):
            loop(0, NB, functools.partial(feed, half))
            for j in range(4):
                at = (2 * j + half) * FC
                grads["up"][:, :, :, :, at : at + FC] = acc_up[:, :, :, :, j * FC : (j + 1) * FC]
            grads["down"][:, 2 * half : 2 * half + 2] = acc_down[...]
            if not half:
                acc_up[...] = jnp.zeros(acc_up.shape, f32)
                acc_down[...] = jnp.zeros(acc_down.shape, f32)
        grads["out"][...] = out_grad()
        loop(0, NB, attended_grad)
        out_copy(NB - 1, (2 * NB - 1) % 2).wait()
        loop(0, NA, attend_back)
        for j in range(3):
            grads["qkv"][:, :, :, :, j * D : (j + 1) * D] = qkv_grad(j)
        loop(0, NB, input_grad)
        tok_back = pltpu.make_async_copy(tokv, gtok, tsem)
        tok_back.start()
        tok_back.wait()
        grads["small"][0:8] = gsmall[...]
        grads["small"][8:12] = gbias[...].reshape(4, D)
        return

    staged(NB, project, [
        (GATHER[2], lambda: each(rest[:3], Gather.start_onward)), (GATHER[3], lambda: each(rest[3:], Gather.start_z)),
    ])
    scat = {}
    for i, name in enumerate(HELD[1:]):
        scat[name] = Scatter(weights[name], weights[name].at[:, :, 1 - c], from_core[name], from_dp[name], from_z[name],
                             ssend.at[i], srecv.at[i], pos, PART.get(name))
    for j in range(3):
        cols = pl.ds(j * D, D)
        own = acc_up.at[:, :, j // 2, :, pl.ds(j % 2 * D, D)]
        away = GN.at[pl.ds(j * D // 2, D // 2)].reshape(4, 4, D // 32, D)
        scat[j] = Scatter(own, away, from_core["qkv"].at[:, :, :, cols], from_dp["qkv"].at[:, :, :, :, cols],
                          from_z["qkv"].at[:, :, cols], ssend.at[5 + j], srecv.at[5 + j], pos)
    small = SmallScatter(small_grad, small_fsdp, small_dp, ssend.at[8], srecv.at[8], pos)
    out_s, up0_s, down0_s, up1_s, down_s = (scat[n] for n in HELD[1:])
    first = (up0_s, down0_s)
    staged(NA, attend, [
        (GATHER[4], lambda: each(rest[:3], Gather.start_core)), (GATHER[5], lambda: each(rest[3:], Gather.start_column)),
    ])
    for g in rest[:3]:
        g.finish()
    staged(NB, functools.partial(feed, 0), [
        (FEED[0], lambda: each(rest[3:], Gather.start_onward)), (FEED[1], lambda: each(rest[3:], Gather.start_core)),
    ])
    for g in rest[3:]:
        g.finish()
    weights["up0"][...] = acc_up[...].astype(bf16)
    weights["down0"][...] = acc_down[...].astype(bf16)
    each(first, Scatter.start_core)
    acc_up[...] = jnp.zeros(acc_up.shape, f32)
    acc_down[...] = jnp.zeros(acc_down.shape, f32)
    staged(NB, functools.partial(feed, 1), [
        (FEED[2], lambda: each(first, Scatter.start_dp)), (FEED[3], lambda: each(first, Scatter.start_onward)),
        (FEED[4], lambda: each(first, Scatter.start_z)),
    ])
    weights["down1"][...] = acc_down[...].astype(bf16)
    down_s.start_core()
    weights["up1"][...] = acc_up[...].astype(bf16)
    up1_s.start_core()
    grad = out_grad().astype(bf16)
    loop(0, NB, attended_grad)
    weights["out"][...] = grad
    out_s.start_core()
    out_copy(NB - 1, (2 * NB - 1) % 2).wait()
    names = (down_s.start_dp, up1_s.start_dp, out_s.start_dp,
             down_s.start_onward, up1_s.start_onward, out_s.start_onward)
    staged(NA, attend_back, list(zip(REDUCE, names)))
    for j in range(3):
        scat[j].start_core(qkv_grad(j))
        if j:
            scat[j - 1].start_dp()
    names = (down_s.start_z, scat[2].start_dp, up1_s.start_z, out_s.start_z, scat[0].start_onward, scat[1].start_onward,
             scat[2].start_onward, scat[0].start_z, scat[1].start_z)
    staged(NB, input_grad, list(zip(REDUCE_QKV, names)))
    tok_back = pltpu.make_async_copy(tokv, gtok, tsem)
    tok_back.start()
    gs = small_grad
    for s in range(32):
        row = s // 4
        gs[s // 8, (s % 8) // 2, s % 2, 0:1, 0:128] = gsmall[row : row + 1, 128 * (s % 4) : 128 * (s % 4) + 128]
        two = gbias[:, 128 * (s // 2) : 128 * (s // 2) + 128]
        gs[s // 8, (s % 8) // 2, s % 2, 1:2, 0:64] = two[:, 64 * (s % 2) : 64 * (s % 2) + 64]
    small.start()
    scat[2].start_z()

    def give(name, total, place=lambda j: j):
        rows, cols = total.shape
        per = shares[name].shape[0] // rows
        for j in range(cols // 128):
            shares[name][pl.ds(place(j), rows, stride=per), :] = total[:, 128 * j : 128 * j + 128]

    def give_up(half, total):
        runs = FC // 128
        give("up", total, lambda j: (2 * (j // runs) + half) * runs + j % runs)

    up0_s.finish(functools.partial(give_up, 0))
    down0_s.finish(functools.partial(give, "down"))
    down_s.finish(functools.partial(give, "down"))
    up1_s.finish(functools.partial(give_up, 1))
    out_s.finish(functools.partial(give, "out"))
    small.pass_on()
    for j in range(3):
        scat[j].finish(functools.partial(give, "qkv", place=lambda i, j=j: j * D // 128 + i))
    shares["small"][...] = small.finish()
    tok_back.wait()


def block_call(comm, tokens, segments, cotangent, pieces, FF):
    R, S, D = tokens.shape
    SP = (S + 15) // 16 * 16
    T, M = R * SP, ROW_BLOCK * SP
    V, dma = pltpu.VMEM, pltpu.SemaphoreType.DMA
    vm, hbm = pl.BlockSpec(memory_space=pltpu.VMEM), pl.BlockSpec(memory_space=pl.ANY)
    rows = {"qkv": (16, 3 * D), "out": (16, D), "up": (16, FF), "down": (FF // 32, D)}
    out_shape = [jax.ShapeDtypeStruct(tokens.shape, bf16)] * 2
    if comm:
        out_shape += [jax.ShapeDtypeStruct(p.shape, f32) for p in pieces[:4]]
        out_shape += [jax.ShapeDtypeStruct((8, 128), f32)]
    else:
        out_shape += [jax.ShapeDtypeStruct((4, 4, 2) + rows[n], f32) for n in ARRAYS]
        out_shape += [jax.ShapeDtypeStruct((12, D), f32)]
    scratch = [
        V((R, S, D), bf16), V((2, ROW_BLOCK, S, D), bf16), V((M, D), bf16),
        V((T, 3 * D), bf16), V((T, D), bf16), V((2 * R, SP, GROUP * SP), bf16), V((T, D), bf16),
        V((T, D), bf16), V((T, D), bf16), V((R, 1, GROUP * SP), jnp.int32), V((1, FF), f32), V((8, D), f32),
        V((1, FF), f32), V((8, D), f32), V((4, 4, 2, 16, FF // 2), f32),
        V((4, 2, 2, FF // 32, D), f32), dma, dma((2,)), dma((2,)),
    ]
    if comm:
        small = (8, 128)
        held = {"qkv": (16, 3 * D), "out": (16, D)}
        for half in "01":
            held.update({"up" + half: (16, FF // 2), "down" + half: (FF // 32, D)})
        depth = {n: 2 if n in PART else 4 for n in HELD}
        scratch += [V((4, depth[n], 2) + (held[n] if n != "qkv" else (16, 3 * D + 128)), bf16) for n in HELD]
        scratch += [V((4, 4, 2) + small, f32)]
        scratch += [V((4, depth[n]) + held[n], bf16) for n in HELD]
        scratch += [V((3, 2, depth[n] // 2) + held[n], bf16) for n in HELD]
        scratch += [V((3,) + held[n], bf16) for n in HELD]
        scratch += [V((7, 4) + small, f32), V((3,) + small, f32), dma((6, 21)), dma((6, 21)), dma((9, 10)), dma((9, 10))]
    params = dict(vmem_limit_bytes=63480 * 1000)
    if comm:
        params.update(collective_id=1, has_side_effects=True)
    return pl.pallas_call(
        functools.partial(block_kernel, comm, R, S, SP, D, FF),
        out_shape=out_shape,
        in_specs=[hbm, vm, hbm] + [vm] * len(pieces),
        out_specs=[hbm, hbm] + [vm] * 5,
        scratch_shapes=scratch,
        compiler_params=pltpu.CompilerParams(**params),
    )(tokens, segments, cotangent, *pieces)


def hand_over_kernel(n, *refs):
    given, kept, held, into, away = refs[: n + 1], refs[n + 1 : 2 * n + 3], refs[2 * n + 3 : 3 * n + 3], refs[-2], refs[-1]
    reads = [pltpu.make_async_copy(given[i], held[i], into.at[i]) for i in range(n)]
    writes = [pltpu.make_async_copy(held[i], kept[i], away.at[i]) for i in range(n)]
    for read in reads:
        read.start()
    kept[n][...] = given[n][0:1]
    kept[n + 1][...] = given[n][1:2, 0 : kept[n + 1].shape[1]]
    for read, write in zip(reads, writes):
        read.wait()
        write.start()
    for write in writes:
        write.wait()


def hand_over(arrays, tile, count):
    n = len(arrays)
    hbm, vm = pl.BlockSpec(memory_space=pl.ANY), pl.BlockSpec(memory_space=pltpu.VMEM)
    shapes = [jax.ShapeDtypeStruct(a.shape, a.dtype) for a in arrays]
    shapes += [jax.ShapeDtypeStruct((1, tile.shape[1]), f32), jax.ShapeDtypeStruct((1, count), f32)]
    sems = pltpu.SemaphoreType.DMA((n,))
    return pl.pallas_call(
        functools.partial(hand_over_kernel, n), out_shape=shapes, in_specs=[hbm] * n + [vm],
        out_specs=[hbm] * n + [vm, vm], scratch_shapes=[pltpu.VMEM(a.shape, a.dtype) for a in arrays] + [sems, sems],
        compiler_params=pltpu.CompilerParams(vmem_limit_bytes=60 * 1024 * 1024),
    )(*arrays, tile)


def body(sizes, tokens, segment_ids, qkv_weight, out_weight, up_weight, up_bias, down_weight, small_params, cotangent):
    D = tokens.shape[2]
    n = sizes[0] * sizes[1]
    FF = up_bias.shape[0] * n
    flats = (qkv_weight, out_weight, up_weight, down_weight)
    if sizes == (4, 8):
        given = [f.reshape(-1, 128) for f in flats] + [small_params.reshape(1, -1), up_bias.reshape(1, -1)]
        o = block_call(True, tokens, segment_ids, cotangent, given, FF)
        o = hand_over(o[:6], o[6], up_bias.shape[0])
        shares = [v.reshape(-1) for v in o[2:]]
        return (o[0], o[1], shares[0], shares[1], shares[2], shares[5], shares[3], shares[4])
    axes = ("dp", "fsdp")

    def gather(v):
        return lax.all_gather(v, axes, axis=0, tiled=True)

    def scatter(v):
        return lax.psum_scatter(v.reshape(-1), axes, scatter_dimension=0, tiled=True)

    packed = lax.all_gather(jnp.concatenate([small_params, up_bias]), axes, axis=0, tiled=False)
    count = small_params.shape[0]
    tile = jnp.concatenate([packed[:, :count].reshape(8, D), packed[:, count:].reshape(4, D)])
    whole = [gather(f) for f in flats]
    shapes = ((4, 4, 2, 16, 3 * D), (4, 4, 2, 16, D), (4, 4, 2, 16, FF), (4, 4, 2, FF // 32, D))
    o = block_call(False, tokens, segment_ids, cotangent, [w.reshape(s) for w, s in zip(whole, shapes)] + [tile], FF)
    return (o[0], o[1], scatter(o[2]), scatter(o[3]), scatter(o[4]), scatter(o[6][8:12]), scatter(o[5]), scatter(o[6][0:8]))


def solution(mesh):
    rows, flat = P(("dp", "fsdp"), None, None), P(("dp", "fsdp"))
    in_specs = (rows, P(("dp", "fsdp"), None), flat, flat, flat, flat, flat, flat, rows)
    out_specs = (rows, rows, flat, flat, flat, flat, flat, flat)
    sizes = (mesh.shape["dp"], mesh.shape["fsdp"])
    return jax.shard_map(functools.partial(body, sizes), mesh=mesh, in_specs=in_specs, out_specs=out_specs, check_vma=False)
```

```python
import functools

import jax
import jax.numpy as jnp
from jax import lax
from jax.experimental import pallas as pl
from jax.experimental.pallas import tpu as pltpu
from jax.sharding import PartitionSpec as P

bf16 = jnp.bfloat16
f32 = jnp.float32
HEADS = 8
HEAD_DIM = 64
GROUP = 4
NORM_EPS = 1e-05
GELU_SLOPE = 1.702
MASKED_SCORE = -1e30
MESH = pl.DeviceIdType.MESH
ROW_BLOCK = 6
UNROLL = 4
GATHER = (2, 3, 2, 4, 2, 8)
FEED = (2, 4, 2, 4, 5)
REDUCE = (0, 2, 3, 5, 7, 8)
REDUCE_QKV = (0, 1, 1, 2, 2, 3, 4, 4, 5)
ARRAYS = ("qkv", "out", "up", "down")
HELD = ("qkv", "out", "up0", "down0", "up1", "down1")
PART = {"down0": 0, "down1": 1}


def nn(a, b):
    return lax.dot_general(a, b, (((1,), (0,)), ((), ())), preferred_element_type=f32)


def nt(a, b):
    return lax.dot_general(a, b, (((1,), (1,)), ((), ())), preferred_element_type=f32)


def tn(a, b):
    return lax.dot_general(a, b, (((0,), (0,)), ((), ())), preferred_element_type=f32)


def col_sum(v):
    return jnp.sum(v, axis=0, keepdims=True)


def lane_mean(v):
    return jnp.sum(v, axis=-1, keepdims=True) * (1.0 / v.shape[-1])


def normalize(x):
    xc = x - lane_mean(x)
    inv = lax.rsqrt(lane_mean(xc * xc) + NORM_EPS)
    return xc * inv, inv


def flip(index, bits):
    low, high = index % 2, index // 2
    if bits & 1:
        low = 1 - low
    if bits & 2:
        high = 1 - high
    return high * 2 + low


class Gather:
    def __init__(self, buf, send, recv, pos, part=None):
        self.buf, self.send, self.recv, self.part = buf, send, recv, part
        self.dp, self.z, self.c = pos
        self.nz = buf.shape[1]

    def only(self, z, act):
        if self.part is None:
            act()
        else:
            pl.when(z // 2 == self.part)(act)

    def copy(self, index, slot, device):
        ref = self.buf.at[index]
        return pltpu.make_async_remote_copy(
            src_ref=ref, dst_ref=ref, send_sem=self.send.at[slot], recv_sem=self.recv.at[slot],
            device_id=device, device_id_type=MESH)

    def along_z(self, k, mine=True):
        z = self.z if mine else flip(self.z, k)
        return self.copy((self.dp, z % self.nz, self.c), k - 1, (self.dp, flip(self.z, k) * 2 + self.c))

    def column(self, bit, mine=True):
        dp = self.dp if mine else flip(self.dp, bit)
        return self.copy((dp, slice(None), self.c), 2 + bit, (flip(self.dp, bit), self.z * 2 + self.c))

    def onward(self, bit, mine=True):
        other = 3 - bit
        dp = flip(self.dp, other) if mine else flip(self.dp, 3)
        half = pl.ds(0 if bit == 2 else self.nz // 2, self.nz // 2)
        return self.copy((dp, half, self.c), 4 + bit, (flip(self.dp, bit), self.z * 2 + self.c))

    def to_core(self, mine=True):
        c = self.c if mine else 1 - self.c
        return self.copy((slice(None), slice(None), c), 7, (self.dp, self.z * 2 + 1 - self.c))

    def start_z(self):
        for k in (1, 2, 3):
            self.only(self.z, self.along_z(k).start)

    def start_column(self):
        for k in (1, 2, 3):
            self.only(flip(self.z, k), self.along_z(k, False).wait_recv)
        for bit in (1, 2):
            self.column(bit).start()

    def start_onward(self):
        for bit in (1, 2):
            self.column(3 - bit, False).wait_recv()
            self.onward(bit).start()

    def start_core(self):
        for bit in (1, 2):
            self.onward(bit, False).wait_recv()
        self.to_core().start()

    def finish(self):
        self.to_core(False).wait_recv()
        for k in (1, 2, 3):
            self.only(self.z, self.along_z(k).wait_send)
        for bit in (1, 2):
            self.column(bit).wait_send()
            self.onward(bit).wait_send()
        self.to_core().wait_send()


class EagerGather(Gather):
    def shard(self, k, bit, mine=True):
        dp = self.dp if mine else flip(self.dp, bit)
        return self.copy((dp, flip(self.z, k), self.c), 2 + bit * 4 + k - 1, (flip(self.dp, bit), self.z * 2 + self.c))

    def forward(self, k, mine=True):
        bit = 2 - k % 2
        dp = flip(self.dp, 3 - bit) if mine else flip(self.dp, 3)
        return self.copy((dp, flip(self.z, k), self.c), 13 + k, (flip(self.dp, bit), self.z * 2 + self.c))

    def core_column(self, bits, mine=True):
        c = self.c if mine else 1 - self.c
        return self.copy((flip(self.dp, bits), slice(None), c), 17 + bits, (self.dp, self.z * 2 + 1 - self.c))

    def start(self):
        for k in (1, 2, 3):
            self.along_z(k).start()
        for bit in (1, 2):
            self.shard(0, bit).start()

    def start_column(self, between=lambda: None):
        for k in (1, 2, 3):
            self.along_z(k, False).wait_recv()
            for bit in (1, 2):
                self.shard(k, bit).start()
            if k == 1:
                between()
        self.core_column(0).start()

    def start_onward(self):
        for k in (0, 1, 2, 3):
            bit = 2 - k % 2
            self.shard(k, 3 - bit, False).wait_recv()
            self.forward(k).start()
        for k in (0, 1, 2, 3):
            bit = 2 - k % 2
            self.shard(k, bit, False).wait_recv()
        for bit in (1, 2):
            self.core_column(bit).start()

    def start_core(self):
        for k in (0, 1, 2, 3):
            self.forward(k, False).wait_recv()
        self.core_column(3).start()

    def finish(self):
        for bits in (0, 1, 2, 3):
            self.core_column(bits, False).wait_recv()
        for k in (1, 2, 3):
            self.along_z(k).wait_send()
        for k in (0, 1, 2, 3):
            for bit in (1, 2):
                self.shard(k, bit).wait_send()
            self.forward(k).wait_send()
            self.core_column(k).wait_send()


class Scatter:
    def __init__(self, grad, half, from_core, from_dp, from_z, send, recv, pos, part=None):
        self.part, self.nz, self.dtype = part, from_core.shape[1], bf16
        self.grad, self.half, self.from_core, self.from_dp, self.from_z = grad, half, from_core, from_dp, from_z
        self.send, self.recv = send, recv
        self.dp, self.z, self.c = pos

    def copy(self, src, dst, slot, device):
        return pltpu.make_async_remote_copy(
            src_ref=src, dst_ref=dst, send_sem=self.send.at[slot], recv_sem=self.recv.at[slot],
            device_id=device, device_id_type=MESH)

    def only(self, z, act):
        if self.part is None:
            act()
        else:
            pl.when(z // 2 == self.part)(act)

    def half_of(self, half):
        return pl.ds(half * self.nz // 2, self.nz // 2)

    def core_copy(self):
        return self.copy(self.half, self.from_core, 0, (self.dp, self.z * 2 + 1 - self.c))

    def dp_copy(self, step, bit, onward):
        half = bit - 1 if step == 0 else 2 - bit
        dp = flip(self.dp, 3 if onward else bit)
        return self.copy(self.from_core.at[dp, self.half_of(half)], self.from_dp.at[2 * step + onward, bit - 1],
                         1 + 2 * (2 * step + onward) + bit - 1, (flip(self.dp, bit), self.z * 2 + self.c))

    def z_copy(self, k):
        return self.copy(self.from_core.at[self.dp, flip(self.z, k) % self.nz], self.from_z.at[k - 1], 6 + k,
                         (self.dp, flip(self.z, k) * 2 + self.c))

    def start_core(self, whole=None):
        if whole is not None:
            zero, one = whole[:, :, 0], whole[:, :, 1]
            self.grad[...] = jnp.where(self.c == 0, zero, one)
            self.half[...] = jnp.where(self.c == 0, one, zero).astype(self.dtype)
        self.core_copy().start()

    def own_part(self, *index):
        return self.grad[self.own(*index)].astype(f32)

    def own(self, *index):
        return index if len(self.grad.shape) == 4 else index + (slice(None),) * (2 - len(index)) + (self.c,)

    def start_dp(self):
        self.core_copy().wait_recv()
        for bit in (1, 2):
            for onward in (1, 0):
                at = (flip(self.dp, 3 if onward else bit), self.half_of(bit - 1))
                self.from_core[at] = (self.own_part(*at) + self.from_core[at].astype(f32)).astype(self.dtype)
                self.dp_copy(0, bit, onward).start()

    def start_onward(self):
        for bit in (1, 2):
            first = 3 - bit
            self.dp_copy(0, first, 1).wait_recv()
            at = (flip(self.dp, bit), self.half_of(first - 1))
            total = self.own_part(*at) + self.from_core[at].astype(f32)
            self.from_core[at] = (total + self.from_dp[1, first - 1].astype(f32)).astype(self.dtype)
            self.dp_copy(1, bit, 0).start()

    def start_z(self):
        for bit in (1, 2):
            self.dp_copy(0, bit, 0).wait_recv()
            self.dp_copy(1, bit, 0).wait_recv()
        for half in (0, 1):
            at = (self.dp, self.half_of(half))
            total = self.own_part(*at) + self.from_core[at].astype(f32)
            total += self.from_dp[0, half].astype(f32) + self.from_dp[2, 1 - half].astype(f32)
            self.grad[self.own(*at)] = total.astype(self.grad.dtype)
            self.from_core[at] = total.astype(self.dtype)
        for k in (1, 2, 3):
            self.only(flip(self.z, k), self.z_copy(k).start)

    def finish(self, use):
        def whole():
            for k in (1, 2, 3):
                self.z_copy(k).wait_recv()
            total = self.own_part(self.dp, self.z % self.nz)
            for k in (1, 2, 3):
                total += self.from_z[k - 1].astype(f32)
            use(total)

        self.only(self.z, whole)
        self.core_copy().wait_send()
        for bit in (1, 2):
            self.dp_copy(0, bit, 0).wait_send()
            self.dp_copy(0, bit, 1).wait_send()
            self.dp_copy(1, bit, 0).wait_send()
        for k in (1, 2, 3):
            self.only(flip(self.z, k), self.z_copy(k).wait_send)


class SmallScatter:
    def __init__(self, grad, from_fsdp, from_dp, send, recv, pos):
        self.grad, self.from_fsdp, self.from_dp, self.send, self.recv = grad, from_fsdp, from_dp, send, recv
        self.dp, self.z, self.c = pos

    def copy(self, src, dst, slot, device):
        return pltpu.make_async_remote_copy(
            src_ref=src, dst_ref=dst, send_sem=self.send.at[slot], recv_sem=self.recv.at[slot],
            device_id=device, device_id_type=MESH)

    def first(self, k):
        z, c = flip(self.z, k // 2), self.c if k % 2 == 0 else 1 - self.c
        return self.copy(self.grad.at[:, z, c], self.from_fsdp.at[k - 1], k - 1, (self.dp, z * 2 + c))

    def second(self, k):
        dp = flip(self.dp, k)
        return self.copy(self.grad.at[dp, self.z, self.c], self.from_dp.at[k - 1], 6 + k, (dp, self.z * 2 + self.c))

    def start(self):
        for k in range(1, 8):
            self.first(k).start()

    def pass_on(self):
        for k in range(1, 8):
            self.first(k).wait_recv()
        total = self.grad[:, self.z, self.c]
        for k in range(1, 8):
            total += self.from_fsdp[k - 1]
        self.grad[:, self.z, self.c] = total
        for k in (1, 2, 3):
            self.second(k).start()

    def finish(self):
        for k in (1, 2, 3):
            self.second(k).wait_recv()
        total = self.grad[self.dp, self.z, self.c] + self.from_dp[0] + self.from_dp[1] + self.from_dp[2]
        for k in range(1, 8):
            self.first(k).wait_send()
        for k in (1, 2, 3):
            self.second(k).wait_send()
        return total


def block_kernel(comm, R, S, SP, D, FF, *refs):
    RB, M, NB, FC, FH, NA = ROW_BLOCK, ROW_BLOCK * SP, R // ROW_BLOCK, FF // 8, FF // 2, R // UNROLL
    GW = GROUP * HEAD_DIM
    refs = list(refs)

    def take(n):
        out = refs[:n]
        del refs[:n]
        return out

    tok, seg, cot = take(3)
    shards = dict(zip(ARRAYS + ("small",), take(5)))
    if comm:
        shards["bias"] = take(1)[0]
    out, gtok = take(2)
    if comm:
        shares = dict(zip(ARRAYS + ("small",), take(5)))
    else:
        grads = dict(zip(ARRAYS + ("small",), take(5)))
    tokv, cbuf, cs, QKV, ATT, PT, GM, ACC, GN, start, bias, smallv, gbias, gsmall = take(14)
    FL = ACC
    acc_up, acc_down = take(2)
    tsem, csem, osem = take(3)
    if comm:
        weights = dict(zip(HELD, take(6)))
        small_grad = take(1)[0]
        from_core, from_dp, from_z = (dict(zip(HELD, take(6))) for _ in range(3))
        small_fsdp, small_dp, gsend, grecv, ssend, srecv = take(6)
    else:
        weights = shards

    def loop(a, b, f):
        lax.fori_loop(a, b, f, 0)

    def staged(count, step, events):
        def body(i, carry):
            for at, act in events:
                if at < count:
                    pl.when(i == at)(act)
            return step(i, carry)

        loop(0, count, body)
        for at, act in events:
            if at >= count:
                act()

    def each(things, act):
        for thing in things:
            act(thing)

    def when(plan):
        return [(NA * at // 18, act) for at, act in plan]

    tok_copy = pltpu.make_async_copy(tok, tokv, tsem)
    tok_copy.start()

    def cot_copy(b, slot):
        return pltpu.make_async_copy(cot.at[pl.ds(b % NB * RB, RB)], cbuf.at[slot], csem.at[slot])

    def out_copy(b, slot):
        return pltpu.make_async_copy(cbuf.at[slot], out.at[pl.ds(b * RB, RB)], osem.at[slot])

    cot_copy(0, 0).start()
    if comm:
        dp = lax.axis_index("dp")
        fs = lax.axis_index("fsdp")
        pos = (dp, fs // 2, fs % 2)
        z, c = pos[1], pos[2]
        peers = [(flip(dp, k), fs) for k in (1, 2, 3)] + [(dp, flip(z, k) * 2 + c) for k in (1, 2, 3)]
        peers += [(dp, flip(z, k) * 2 + 1 - c) for k in (0, 1, 2, 3)]
        barrier = pltpu.get_barrier_semaphore()
        for peer in peers:
            pl.semaphore_signal(barrier, inc=1, device_id=peer, device_id_type=MESH)
        spread = small_grad.reshape(256, 128)
        for name in ARRAYS:
            rows = FF // 32 if name == "down" else 16
            src = shards[name]
            per = src.shape[0] // rows
            spread[0 : src.shape[0]] = src[...].astype(f32)
            for j in range(per):
                piece = spread[pl.ds(j, rows, stride=per), :].astype(bf16)
                at = slice(128 * j, 128 * j + 128)
                if name == "up":
                    run, left = divmod(128 * j, 2 * FC)
                    half, left = divmod(left, FC)
                    weights["up%d" % half][dp, z, c, :, run * FC + left : run * FC + left + 128] = piece
                elif name == "down":
                    for part in (0, 1):

                        @pl.when(z // 2 == part)
                        def _(part=part, at=at, piece=piece):
                            weights["down%d" % part][dp, z % 2, c, :, at] = piece

                else:
                    weights[name][dp, z, c, :, at] = piece
        row = lax.broadcasted_iota(jnp.int32, (16, 128), 0)
        given, extra = shards["small"][...].astype(f32), shards["bias"][...].astype(f32)
        extra = jnp.concatenate([extra, jnp.zeros((1, 128 - extra.shape[1]), f32)], axis=1)
        tile = jnp.where(row == 0, given, jnp.where(row == 1, extra, 0.0))
        weights["qkv"][dp, z, c, :, 3 * D :] = tile.astype(bf16)
        gathers = {n: Gather(weights[n], gsend.at[i], grecv.at[i], pos, PART.get(n)) for i, n in enumerate(HELD)}
        gathers["qkv"] = EagerGather(weights["qkv"], gsend.at[0], grecv.at[0], pos)
        pl.semaphore_wait(barrier, len(peers))
        gathers["qkv"].start()
        rest = [gathers[n] for n in HELD[1:]]
        gathers["qkv"].start_column(lambda: each(rest[:2], Gather.start_z))

    cs[...] = jnp.zeros(cs.shape, bf16)
    sg = seg[...]
    st = jnp.zeros(sg.shape, jnp.int32)
    for v in range(1, 4):
        count = jnp.sum((sg < v).astype(f32), axis=1, keepdims=True).astype(jnp.int32)
        st = jnp.where(sg == v, count, st)
    st = jnp.concatenate([st, jnp.zeros((R, SP - S), jnp.int32)], axis=1)
    start[...] = jnp.concatenate([st] * GROUP, axis=1).reshape(R, 1, GROUP * SP)
    for ref in (acc_up, acc_down, gbias, gsmall):
        ref[...] = jnp.zeros(ref.shape, f32)
    tok_copy.wait()

    def load_x(b):
        for i in range(RB):
            cs[SP * i : SP * i + S] = tokv[b * RB + i]
        return cs[...].astype(f32)

    def rows_of(b):
        return pl.ds(pl.multiple_of(b * M, 16), M)

    def norm_one(b, carry):
        rows = rows_of(b)
        xh1 = normalize(load_x(b))[0]
        high = xh1.astype(bf16)
        ACC[rows] = high
        GN[rows] = (xh1 - high.astype(f32)).astype(bf16)
        return carry

    if comm:
        staged(NB, norm_one, [
            (0, gathers["qkv"].start_onward), (0, rest[2].start_z), (GATHER[0], lambda: each(rest[:3], Gather.start_column)),
            (GATHER[1], gathers["qkv"].start_core),
        ])
        gathers["qkv"].finish()
        wq = weights["qkv"]
        for s in range(32):
            piece = wq[s // 8, (s % 8) // 2, s % 2, :, 3 * D :].astype(f32)
            smallv[s // 4 : s // 4 + 1, 128 * (s % 4) : 128 * (s % 4) + 128] = piece[0:1]
        for s in range(0, 32, 2):
            two = [wq[s // 8, (s % 8) // 2, i, :, 3 * D : 3 * D + 64].astype(f32)[1:2] for i in (0, 1)]
            bias[:, 64 * s : 64 * s + 128] = jnp.concatenate(two, axis=1)
    else:
        lax.fori_loop(0, NB, norm_one, 0)
        bias[...] = shards["small"][8:12].astype(f32).reshape(1, FF)
        smallv[...] = shards["small"][0:8].astype(f32)

    def w_qkv(a, b):
        return weights["qkv"][:, :, :, :, a:b].reshape(D, b - a)

    sm = smallv[...]
    g1, c1, bq, bv, bo, g2, c2, bd = [sm[i : i + 1] for i in range(8)]
    scale = HEAD_DIM ** (-0.5)
    bkv = jnp.concatenate([jnp.zeros_like(bv), bv], axis=1)
    lane = lax.broadcasted_iota(jnp.int32, (1, GW), 1)
    head_mask = [(lane // HEAD_DIM == j).astype(f32).astype(bf16) for j in range(GROUP)]
    low_half = lax.broadcasted_iota(jnp.int32, (1, 128), 1) < HEAD_DIM

    def stack(v):
        return jnp.concatenate([v * head_mask[j] for j in range(GROUP)], axis=0)

    def project(b, carry):
        rows = rows_of(b)
        fl = ((ACC[rows].astype(f32) + GN[rows].astype(f32)) * g1 + c1).astype(bf16)
        QKV[rows, 0:D] = ((nn(fl, w_qkv(0, D)) + bq) * scale).astype(bf16)
        QKV[rows, D : 3 * D] = (nn(fl, w_qkv(D, 3 * D)) + bkv).astype(bf16)
        return carry

    kidx = lax.broadcasted_iota(jnp.int32, (SP, GROUP * SP), 0)
    qidx = lax.broadcasted_iota(jnp.int32, (1, GROUP * SP), 1)
    qidx = qidx - SP * sum((qidx >= SP * j).astype(jnp.int32) for j in range(1, GROUP))

    NG = HEADS // GROUP
    TILES = GW // 128

    def attend(i, carry):
        rs = [i * UNROLL + u for u in range(UNROLL)]
        rows = [pl.ds(pl.multiple_of(r * SP, 16), SP) for r in rs]
        todo = [(u, g) for u in range(UNROLL) for g in range(NG)]
        allowed = [(kidx >= start[r]) & (kidx <= qidx) for r in rs]
        ss = [nt(QKV[rows[u], D + GW * g : D + GW * g + GW], stack(QKV[rows[u], GW * g : GW * g + GW])) for u, g in todo]
        ss = [jnp.where(allowed[u], s, MASKED_SCORE) for (u, g), s in zip(todo, ss)]
        es = [jnp.exp(s - jnp.max(s, axis=0, keepdims=True)) for s in ss]
        ps = [(e * (1.0 / col_sum(e))).astype(bf16) for e in es]
        pqs = [p.T for p in ps]
        for (u, g), p in zip(todo, ps):
            PT[2 * rs[u] + g] = p
        for (u, g), pq in zip(todo, pqs):
            for t in range(TILES):
                at = GW * g + 128 * t
                o = nn(pq[2 * SP * t : 2 * SP * t + 2 * SP], QKV[rows[u], 2 * D + at : 2 * D + at + 128])
                ATT[rows[u], at : at + 128] = jnp.where(low_half, o[0:SP], o[SP : 2 * SP]).astype(bf16)
        return carry

    def up_part(half, j):
        if comm:
            return weights["up%d" % half][:, :, :, :, j * FC : (j + 1) * FC].reshape(D, FC)
        return weights["up"][:, :, :, :, (2 * j + half) * FC : (2 * j + half + 1) * FC].reshape(D, FC)

    def down_part(half, j):
        if comm:
            return weights["down%d" % half][j].reshape(FC, D)
        return weights["down"][j, 2 * half : 2 * half + 2].reshape(FC, D)

    def feed(half, b, carry):
        step = half * NB + b
        slot = step % 2
        rows = rows_of(b)
        mid = load_x(b) + nn(ATT[rows], weights["out"][...].reshape(D, D)) + bo
        cot_copy(step, slot).wait()
        for i in range(RB):
            cs[SP * i : SP * i + S] = cbuf[slot, i]
        if half:

            @pl.when(b > 0)
            def _():
                out_copy(b - 1, 1 - slot).wait()

            @pl.when(b + 1 < NB)
            def _():
                cot_copy(b + 1, 1 - slot).start()

        else:
            cot_copy(b + 1, 1 - slot).start()
        xh2, r2 = normalize(mid)
        second = (xh2 * g2 + c2).astype(bf16)
        branch = cs[...]
        acts, gps = [], []
        for j in range(4):
            w_up, w_down = up_part(half, j), down_part(half, j)
            cols = slice((2 * j + half) * FC, (2 * j + half + 1) * FC)
            pre = nn(second, w_up) + bias[:, cols]
            s = 0.5 * jnp.tanh((0.5 * GELU_SLOPE) * pre) + 0.5
            a = pre * s
            gp = (nt(branch, w_down) * (s + GELU_SLOPE * a * (1.0 - s))).astype(bf16)
            gbias[:, cols] += col_sum(gp.astype(f32))
            acts.append(a.astype(bf16))
            gps.append(gp)
        act, gp = jnp.concatenate(acts, axis=1), jnp.concatenate(gps, axis=1)
        w_down = jnp.concatenate([down_part(half, j) for j in range(4)], axis=0)
        w_up = jnp.concatenate([up_part(half, j) for j in range(4)], axis=1)
        grown = nn(act, w_down)
        gn2 = nt(gp, w_up)
        for acc, term in ((acc_down, tn(act, branch)), (acc_up, tn(second, gp))):
            before = jnp.where(b == 0, 0.0, acc[...]) if half else acc[...]
            acc[...] = before + term.reshape(acc.shape)
        if not half:
            ACC[rows] = grown.astype(bf16)
            GN[rows] = gn2.astype(bf16)
            return carry
        res = (mid + bd + ACC[rows].astype(f32) + grown).astype(bf16)
        for i in range(RB):
            cbuf[slot, i] = res[SP * i : SP * i + S]
        out_copy(b, slot).start()
        gn2 = gn2 + GN[rows].astype(f32)
        h = gn2 * g2
        up = branch.astype(f32)
        gm = up + r2 * (h - lane_mean(h) - xh2 * lane_mean(h * xh2))
        GM[rows] = gm.astype(bf16)
        gsmall[4:5] += col_sum(gm.astype(bf16).astype(f32))
        gsmall[5:6] += col_sum(gn2 * xh2)
        gsmall[6:7] += col_sum(gn2)
        gsmall[7:8] += col_sum(up)
        return carry

    def out_grad():
        return tn(ATT[...], GM[...]).reshape(4, 4, 2, D // 32, D)

    def attended_grad(b, carry):
        rows = rows_of(b)
        ATT[rows] = nt(GM[rows], weights["out"][...].reshape(D, D)).astype(bf16)
        return carry

    def attend_back(i, carry):
        rs = [i * UNROLL + u for u in range(UNROLL)]
        rows = [pl.ds(pl.multiple_of(r * SP, 16), SP) for r in rs]
        todo = [(u, g) for u in range(UNROLL) for g in range(NG)]
        gos = [stack(ATT[rows[u], GW * g : GW * g + GW]) for u, g in todo]
        dps = [nt(QKV[rows[u], 2 * D + GW * g : 2 * D + GW * g + GW], go) for (u, g), go in zip(todo, gos)]
        qs = [stack(QKV[rows[u], GW * g : GW * g + GW]) for u, g in todo]
        lows = [PT[2 * rs[u] + g] for u, g in todo]
        gvs = [nn(low, go).astype(bf16) for low, go in zip(lows, gos)]
        dss = []
        for low, dpr in zip(lows, dps):
            p = low.astype(f32)
            dss.append((p * (dpr - col_sum(p * dpr))).astype(bf16))
        gks = [nn(ds, q).astype(bf16) for ds, q in zip(dss, qs)]
        gqs = []
        for (u, g), ds in zip(todo, dss):
            dsq = ds.T
            for t in range(TILES):
                at = D + GW * g + 128 * t
                o = nn(dsq[2 * SP * t : 2 * SP * t + 2 * SP], QKV[rows[u], at : at + 128])
                gqs.append((jnp.where(low_half, o[0:SP], o[SP : 2 * SP]) * scale).astype(bf16))
        for r in rs:
            x = normalize(tokv[r].astype(f32))[0]
            FL[pl.ds(pl.multiple_of(r * SP, 16), S)] = (x * g1 + c1).astype(bf16)
        for n, (u, g) in enumerate(todo):
            for t in range(TILES):
                QKV[rows[u], GW * g + 128 * t : GW * g + 128 * t + 128] = gqs[n * TILES + t]
            QKV[rows[u], D + GW * g : D + GW * g + GW] = gks[n]
            QKV[rows[u], 2 * D + GW * g : 2 * D + GW * g + GW] = gvs[n]
        return carry

    def input_grad(b, carry):
        rows = rows_of(b)
        gq = QKV[rows]
        gn1 = nt(gq, w_qkv(0, 3 * D))
        xh1, r1 = normalize(load_x(b))
        h = gn1 * g1
        res = (GM[rows].astype(f32) + r1 * (h - lane_mean(h) - xh1 * lane_mean(h * xh1))).astype(bf16)
        for i in range(RB):
            tokv[b * RB + i] = res[SP * i : SP * i + S]
        gsmall[0:1] += col_sum(gn1 * xh1)
        gsmall[1:2] += col_sum(gn1)
        gsmall[2:3] += col_sum(gq[:, 0:D].astype(f32))
        gsmall[3:4] += col_sum(gq[:, 2 * D : 3 * D].astype(f32))
        return carry

    def qkv_grad(j):
        return tn(FL[...], QKV[:, j * D : (j + 1) * D]).reshape(4, 4, 2, D // 32, D)

    if not comm:
        loop(0, NB, project)
        loop(0, NA, attend)
        for half in (0, 1):
            loop(0, NB, functools.partial(feed, half))
            for j in range(4):
                at = (2 * j + half) * FC
                grads["up"][:, :, :, :, at : at + FC] = acc_up[:, :, :, :, j * FC : (j + 1) * FC]
            grads["down"][:, 2 * half : 2 * half + 2] = acc_down[...]
        grads["out"][...] = out_grad()
        loop(0, NB, attended_grad)
        out_copy(NB - 1, (2 * NB - 1) % 2).wait()
        loop(0, NA, attend_back)
        for j in range(3):
            grads["qkv"][:, :, :, :, j * D : (j + 1) * D] = qkv_grad(j)
        loop(0, NB, input_grad)
        tok_back = pltpu.make_async_copy(tokv, gtok, tsem)
        tok_back.start()
        tok_back.wait()
        grads["small"][0:8] = gsmall[...]
        grads["small"][8:12] = gbias[...].reshape(4, D)
        return

    staged(NB, project, [
        (GATHER[2], lambda: each(rest[:3], Gather.start_onward)), (GATHER[3], lambda: each(rest[3:], Gather.start_z)),
    ])
    scat = {}
    for i, name in enumerate(HELD[1:]):
        scat[name] = Scatter(weights[name], weights[name].at[:, :, 1 - c], from_core[name], from_dp[name], from_z[name],
                             ssend.at[i], srecv.at[i], pos, PART.get(name))
    for j in range(3):
        cols = pl.ds(j * D, D)
        own = acc_up.at[:, :, j // 2, :, pl.ds(j % 2 * D, D)]
        away = GN.at[pl.ds(j * D // 2, D // 2)].reshape(4, 4, D // 32, D)
        scat[j] = Scatter(own, away, from_core["qkv"].at[:, :, :, cols], from_dp["qkv"].at[:, :, :, :, cols],
                          from_z["qkv"].at[:, :, cols], ssend.at[5 + j], srecv.at[5 + j], pos)
    small = SmallScatter(small_grad, small_fsdp, small_dp, ssend.at[8], srecv.at[8], pos)
    out_s, up0_s, down0_s, up1_s, down_s = (scat[n] for n in HELD[1:])
    first = (up0_s, down0_s)
    staged(NA, attend, [
        (GATHER[4], lambda: each(rest[:3], Gather.start_core)), (GATHER[5], lambda: each(rest[3:], Gather.start_column)),
    ])
    for g in rest[:3]:
        g.finish()
    staged(NB, functools.partial(feed, 0), [
        (FEED[0], lambda: each(rest[3:], Gather.start_onward)), (FEED[1], lambda: each(rest[3:], Gather.start_core)),
    ])
    for g in rest[3:]:
        g.finish()
    weights["up0"][...] = acc_up[...].astype(bf16)
    weights["down0"][...] = acc_down[...].astype(bf16)
    each(first, Scatter.start_core)
    staged(NB, functools.partial(feed, 1), [
        (FEED[2], lambda: each(first, Scatter.start_dp)), (FEED[3], lambda: each(first, Scatter.start_onward)),
        (FEED[4], lambda: each(first, Scatter.start_z)),
    ])
    weights["down1"][...] = acc_down[...].astype(bf16)
    down_s.start_core()
    weights["up1"][...] = acc_up[...].astype(bf16)
    up1_s.start_core()
    grad = out_grad().astype(bf16)
    loop(0, NB, attended_grad)
    weights["out"][...] = grad
    out_s.start_core()
    out_copy(NB - 1, (2 * NB - 1) % 2).wait()
    names = (down_s.start_dp, up1_s.start_dp, out_s.start_dp,
             down_s.start_onward, up1_s.start_onward, out_s.start_onward)
    staged(NA, attend_back, list(zip(REDUCE, names)))
    for j in range(3):
        scat[j].start_core(qkv_grad(j))
        if j:
            scat[j - 1].start_dp()
    names = (down_s.start_z, scat[2].start_dp, up1_s.start_z, out_s.start_z, scat[0].start_onward, scat[1].start_onward,
             scat[2].start_onward, scat[0].start_z, scat[1].start_z)
    staged(NB, input_grad, list(zip(REDUCE_QKV, names)))
    tok_back = pltpu.make_async_copy(tokv, gtok, tsem)
    tok_back.start()
    gs = small_grad
    for s in range(32):
        row = s // 4
        gs[s // 8, (s % 8) // 2, s % 2, 0:1, 0:128] = gsmall[row : row + 1, 128 * (s % 4) : 128 * (s % 4) + 128]
        two = gbias[:, 128 * (s // 2) : 128 * (s // 2) + 128]
        gs[s // 8, (s % 8) // 2, s % 2, 1:2, 0:64] = two[:, 64 * (s % 2) : 64 * (s % 2) + 64]
    small.start()
    scat[2].start_z()

    def give(name, total, place=lambda j: j):
        rows, cols = total.shape
        per = shares[name].shape[0] // rows
        for j in range(cols // 128):
            shares[name][pl.ds(place(j), rows, stride=per), :] = total[:, 128 * j : 128 * j + 128]

    def give_up(half, total):
        runs = FC // 128
        give("up", total, lambda j: (2 * (j // runs) + half) * runs + j % runs)

    up0_s.finish(functools.partial(give_up, 0))
    down0_s.finish(functools.partial(give, "down"))
    down_s.finish(functools.partial(give, "down"))
    up1_s.finish(functools.partial(give_up, 1))
    out_s.finish(functools.partial(give, "out"))
    small.pass_on()
    for j in range(3):
        scat[j].finish(functools.partial(give, "qkv", place=lambda i, j=j: j * D // 128 + i))
    shares["small"][...] = small.finish()
    tok_back.wait()


def block_call(comm, tokens, segments, cotangent, pieces, FF):
    R, S, D = tokens.shape
    SP = (S + 15) // 16 * 16
    T, M = R * SP, ROW_BLOCK * SP
    V, dma = pltpu.VMEM, pltpu.SemaphoreType.DMA
    vm, hbm = pl.BlockSpec(memory_space=pltpu.VMEM), pl.BlockSpec(memory_space=pl.ANY)
    rows = {"qkv": (16, 3 * D), "out": (16, D), "up": (16, FF), "down": (FF // 32, D)}
    out_shape = [jax.ShapeDtypeStruct(tokens.shape, bf16)] * 2
    if comm:
        out_shape += [jax.ShapeDtypeStruct(p.shape, f32) for p in pieces[:4]]
        out_shape += [jax.ShapeDtypeStruct((8, 128), f32)]
    else:
        out_shape += [jax.ShapeDtypeStruct((4, 4, 2) + rows[n], f32) for n in ARRAYS]
        out_shape += [jax.ShapeDtypeStruct((12, D), f32)]
    scratch = [
        V((R, S, D), bf16), V((2, ROW_BLOCK, S, D), bf16), V((M, D), bf16),
        V((T, 3 * D), bf16), V((T, D), bf16), V((2 * R, SP, GROUP * SP), bf16), V((T, D), bf16),
        V((T, D), bf16), V((T, D), bf16), V((R, 1, GROUP * SP), jnp.int32), V((1, FF), f32), V((8, D), f32),
        V((1, FF), f32), V((8, D), f32), V((4, 4, 2, 16, FF // 2), f32),
        V((4, 2, 2, FF // 32, D), f32), dma, dma((2,)), dma((2,)),
    ]
    if comm:
        small = (8, 128)
        held = {"qkv": (16, 3 * D), "out": (16, D)}
        for half in "01":
            held.update({"up" + half: (16, FF // 2), "down" + half: (FF // 32, D)})
        depth = {n: 2 if n in PART else 4 for n in HELD}
        scratch += [V((4, depth[n], 2) + (held[n] if n != "qkv" else (16, 3 * D + 128)), bf16) for n in HELD]
        scratch += [V((4, 4, 2) + small, f32)]
        scratch += [V((4, depth[n]) + held[n], bf16) for n in HELD]
        scratch += [V((3, 2, depth[n] // 2) + held[n], bf16) for n in HELD]
        scratch += [V((3,) + held[n], bf16) for n in HELD]
        scratch += [V((7, 4) + small, f32), V((3,) + small, f32), dma((6, 21)), dma((6, 21)), dma((9, 10)), dma((9, 10))]
    params = dict(vmem_limit_bytes=63480 * 1000)
    if comm:
        params.update(collective_id=1, has_side_effects=True)
    return pl.pallas_call(
        functools.partial(block_kernel, comm, R, S, SP, D, FF),
        out_shape=out_shape,
        in_specs=[hbm, vm, hbm] + [vm] * len(pieces),
        out_specs=[hbm, hbm] + [vm] * 5,
        scratch_shapes=scratch,
        compiler_params=pltpu.CompilerParams(**params),
    )(tokens, segments, cotangent, *pieces)


def hand_over_kernel(n, *refs):
    given, kept, held, into, away = refs[: n + 1], refs[n + 1 : 2 * n + 3], refs[2 * n + 3 : 3 * n + 3], refs[-2], refs[-1]
    reads = [pltpu.make_async_copy(given[i], held[i], into.at[i]) for i in range(n)]
    writes = [pltpu.make_async_copy(held[i], kept[i], away.at[i]) for i in range(n)]
    for read in reads:
        read.start()
    kept[n][...] = given[n][0:1]
    kept[n + 1][...] = given[n][1:2, 0 : kept[n + 1].shape[1]]
    for read, write in zip(reads, writes):
        read.wait()
        write.start()
    for write in writes:
        write.wait()


def hand_over(arrays, tile, count):
    n = len(arrays)
    hbm, vm = pl.BlockSpec(memory_space=pl.ANY), pl.BlockSpec(memory_space=pltpu.VMEM)
    shapes = [jax.ShapeDtypeStruct(a.shape, a.dtype) for a in arrays]
    shapes += [jax.ShapeDtypeStruct((1, tile.shape[1]), f32), jax.ShapeDtypeStruct((1, count), f32)]
    sems = pltpu.SemaphoreType.DMA((n,))
    return pl.pallas_call(
        functools.partial(hand_over_kernel, n), out_shape=shapes, in_specs=[hbm] * n + [vm],
        out_specs=[hbm] * n + [vm, vm], scratch_shapes=[pltpu.VMEM(a.shape, a.dtype) for a in arrays] + [sems, sems],
        compiler_params=pltpu.CompilerParams(vmem_limit_bytes=60 * 1024 * 1024),
    )(*arrays, tile)


def body(sizes, tokens, segment_ids, qkv_weight, out_weight, up_weight, up_bias, down_weight, small_params, cotangent):
    D = tokens.shape[2]
    n = sizes[0] * sizes[1]
    FF = up_bias.shape[0] * n
    flats = (qkv_weight, out_weight, up_weight, down_weight)
    if sizes == (4, 8):
        given = [f.reshape(-1, 128) for f in flats] + [small_params.reshape(1, -1), up_bias.reshape(1, -1)]
        o = block_call(True, tokens, segment_ids, cotangent, given, FF)
        o = hand_over(o[:6], o[6], up_bias.shape[0])
        shares = [v.reshape(-1) for v in o[2:]]
        return (o[0], o[1], shares[0], shares[1], shares[2], shares[5], shares[3], shares[4])
    axes = ("dp", "fsdp")

    def gather(v):
        return lax.all_gather(v, axes, axis=0, tiled=True)

    def scatter(v):
        return lax.psum_scatter(v.reshape(-1), axes, scatter_dimension=0, tiled=True)

    packed = lax.all_gather(jnp.concatenate([small_params, up_bias]), axes, axis=0, tiled=False)
    count = small_params.shape[0]
    tile = jnp.concatenate([packed[:, :count].reshape(8, D), packed[:, count:].reshape(4, D)])
    whole = [gather(f) for f in flats]
    shapes = ((4, 4, 2, 16, 3 * D), (4, 4, 2, 16, D), (4, 4, 2, 16, FF), (4, 4, 2, FF // 32, D))
    o = block_call(False, tokens, segment_ids, cotangent, [w.reshape(s) for w, s in zip(whole, shapes)] + [tile], FF)
    return (o[0], o[1], scatter(o[2]), scatter(o[3]), scatter(o[4]), scatter(o[6][8:12]), scatter(o[5]), scatter(o[6][0:8]))


def solution(mesh):
    rows, flat = P(("dp", "fsdp"), None, None), P(("dp", "fsdp"))
    in_specs = (rows, P(("dp", "fsdp"), None), flat, flat, flat, flat, flat, flat, rows)
    out_specs = (rows, rows, flat, flat, flat, flat, flat, flat)
    sizes = (mesh.shape["dp"], mesh.shape["fsdp"])
    return jax.shard_map(functools.partial(body, sizes), mesh=mesh, in_specs=in_specs, out_specs=out_specs, check_vma=False)
```
